32 devices in a mesh: rep: 2 (over core), ep: 4 (over z), dp: 4 (over y, x).
Axes of the slice: x: 2, y: 2, z: 4, core: 2. Of those that a mesh axis runs over, the one named last changes fastest.
Arguments:
- tokens: bfloat16 [1024, 2048], P(('rep', 'ep', 'dp')), may hold values from -6 to 6
- upstream: bfloat16 [1024, 2048], P(('rep', 'ep', 'dp')), may hold values from -6 to 6
- expert_ids: int32 [1024, 2], P(('rep', 'ep', 'dp')), may hold values from 0 to 3, all different within a row; in each aligned block of 32 rows (0 to 31, 32 to 63, ...) at most 20 rows name the same one
- route_weight: bfloat16 [1024, 2], P(('rep', 'ep', 'dp')), may hold values from 0.099609375 to 1
- gate_weight: bfloat16 [4, 384, 2048], P('ep', 'dp'), may hold values from -0.125 to 0.125
- up_weight: bfloat16 [4, 384, 2048], P('ep', 'dp'), may hold values from -0.125 to 0.125
- down_weight: bfloat16 [4, 384, 2048], P('ep', 'dp'), may hold values from -0.3125 to 0.3125
Outputs:
- d_tokens: bfloat16 [1024, 2048], P(('rep', 'ep', 'dp'))
- d_probs: bfloat16 [1024, 2], P(('rep', 'ep', 'dp'))
- grad_down: float32 [4, 384, 2048], P('ep', 'dp')
The draws below stay inside these ranges and needn't reach their ends.
Inputs may be any that keep to these rules, and one draw needn't show every extreme that they name: `expert_ids`: each row names 2 different experts; among the rows of one device no expert is named by more than 20 rows, and in every draw some expert is named by exactly 20 rows of some device.
All inputs are finite; a program needn't handle non-finite values.
Results may differ from the reference program's by a relative error of at most 0.012.
Values may be sent and summed in bfloat16 or wider, within the bound.
No kernel may reach another device: no remote copies, remote signals or barrier semaphores. Data moves between devices by JAX's collectives and lax.ppermute only.
A program may use at most 64 MiB of HBM per device.

```python
import math
import jax
import jax.numpy as jnp
import numpy as np
from jax import lax

D = 2048
FF = 384
TOK_DEV = 32
EXPERTS = 4
TOP = 2
CAP = 20
TOKENS = 1024


def shard_levels(key, dims, cuts, smallest, high):
    level, own = 1.0, jax.random.fold_in(key, 6)
    for position, shards_of in cuts:
        heights = jnp.exp(jax.random.uniform(jax.random.fold_in(own, position), (shards_of,), jnp.float32, smallest / len(cuts), high / len(cuts)))
        level = level * jnp.repeat(heights, dims[position] // shards_of).reshape([-1 if axis == position else 1 for axis in range(len(dims))])
    return level


def deal_out(rng, own, number, rows, count, top, most, lean):
    sequence = jax.random.permutation(rng, count)
    crowded, usual = portions_of(count, rows * top, most, lean, True), portions_of(count, rows * top, most, lean, False)
    places = jnp.arange(count)

    def named(tallies, offset_by):
        used = int((tallies > 0).sum())
        fixed = max(1, used // 4)
        shifted = fixed + (places - fixed + offset_by * (used - fixed)) % max(1, count - fixed)
        return jnp.zeros((count,), jnp.int32).at[sequence[jnp.where(places < fixed, places, shifted)]].set(jnp.asarray(tallies, jnp.int32))

    tallies = jnp.where(number % 4 == 0, named(crowded, number // 4), named(usual, number - number // 4 - 1))
    mixed = jax.random.permutation(jax.random.fold_in(own, 3), count)
    donor, sink = mixed[0:count // 2 * 2:2], mixed[1:count // 2 * 2:2]
    room = jnp.minimum(tallies[donor] - 1, most - tallies[sink]) // 2
    room = jnp.where((donor == sequence[0]) | (sink == sequence[0]) | (tallies[sink] == 0), 0, jnp.maximum(room, 0))
    shifted = jax.random.randint(jax.random.fold_in(own, 4), (count // 2,), 0, 1 << 20) % (room + 1)
    tallies = tallies.at[donor].add(-shifted).at[sink].add(shifted)
    items = jnp.searchsorted(jnp.cumsum(tallies), jnp.arange(rows * top), side="right").astype(jnp.int32)
    table = items.reshape(top, rows).T
    table = table[jax.random.permutation(jax.random.fold_in(own, 1), rows)]
    offset_by = jax.random.randint(jax.random.fold_in(own, 2), (rows, 1), 0, top)
    return jnp.take_along_axis(table, (jnp.arange(top)[None, :] + offset_by) % top, axis=1)


def portions_of(count, total, limit, lean, full):
    loads = [(1 << 20) // math.isqrt(grade ** lean) + 1 for grade in range(1, count + 1)]
    largest = limit if full else min(limit, max(-(-total // count), total * loads[0] // sum(loads)))
    least = 1 if total - largest >= count - 1 else 0
    given, surplus = [largest] + [least] * (count - 1), total - largest - least * (count - 1)
    while surplus > 0:
        candidates = [i for i in range(1, count) if given[i] < largest] or [i for i in range(1, count) if given[i] < limit]
        whole, left = sum([loads[i] for i in candidates]), surplus
        for i in candidates:
            extra = min(limit - given[i], max(1, left * loads[i] // whole), surplus)
            given[i] = given[i] + extra
            surplus = surplus - extra
    return np.array(given)


def bell_draw(key, dims, scale, most, split=(), kind=jnp.bfloat16):
    loudness = shard_levels(key, dims, split, -0.22, 0.18) if split else 1.0
    drawn = jax.random.normal(key, dims, jnp.float32) * scale * loudness
    return jnp.minimum(jnp.maximum(drawn, -most), most).astype(kind)


def setup_inputs(seed: int = 0) -> dict:
    seeds = jax.random.split(jax.random.key(seed), 8)
    tokens = bell_draw(seeds[0], (TOKENS, D), 1.0, 6.0, ((0, 32),))
    upstream = bell_draw(seeds[1], (TOKENS, D), 1.0, 6.0, ((0, 32),))
    expert_ids_keys = jax.random.split(jax.random.fold_in(seeds[2], 1), TOKENS // TOK_DEV)
    expert_ids_turns = jax.random.permutation(jax.random.fold_in(seeds[2], 3), TOKENS // TOK_DEV)
    expert_ids = jax.vmap(lambda own, number: deal_out(jax.random.fold_in(seeds[2], 2), own, number, TOK_DEV, EXPERTS, TOP, CAP, 1))(expert_ids_keys, expert_ids_turns).reshape((TOKENS, TOP))
    route_weight = jnp.clip(0.099609375 + 0.9003906 * jax.random.uniform(seeds[3], (TOKENS, TOP), jnp.float32) ** shard_levels(seeds[3], (TOKENS, TOP), ((0, 32),), -0.2, 0.2), 0.099609375, 1.0).astype(jnp.bfloat16)
    gate_weight = bell_draw(seeds[4], (EXPERTS, FF, D), D ** -0.5, 0.125, ((0, 4), (1, 4)))
    up_weight = bell_draw(seeds[5], (EXPERTS, FF, D), D ** -0.5, 0.125, ((0, 4), (1, 4)))
    down_weight = bell_draw(seeds[6], (EXPERTS, FF, D), FF ** -0.5, 0.3125, ((0, 4), (1, 4)))
    return dict(tokens=tokens, upstream=upstream, expert_ids=expert_ids, route_weight=route_weight, gate_weight=gate_weight, up_weight=up_weight, down_weight=down_weight)


def reference(tokens, upstream, expert_ids, route_weight, gate_weight, up_weight, down_weight):
    route_count = TOKENS * TOP
    most_rows = (TOKENS // TOK_DEV) * CAP
    flat_ids = expert_ids.reshape(route_count).astype(jnp.int32)
    tok_padded = jnp.concatenate([tokens, jnp.zeros((1, D), tokens.dtype)], axis=0)
    up_padded = jnp.concatenate([upstream, jnp.zeros((1, D), upstream.dtype)], axis=0)
    prob_padded = jnp.concatenate([route_weight.reshape(route_count), jnp.zeros((1,), route_weight.dtype)], axis=0)

    def one_expert(running, expert):
        dx_total, dprob_total = running
        row_index = jnp.nonzero(flat_ids == expert, size=most_rows, fill_value=route_count)[0].astype(jnp.int32)
        token_index = (row_index // TOP).astype(jnp.int32)
        x_rows = tok_padded[token_index]
        dy_rows = up_padded[token_index]
        weights = prob_padded[row_index]
        gate_mat = gate_weight[expert]
        up_mat = up_weight[expert]
        down_mat = down_weight[expert]
        gate_pre = jnp.dot(x_rows, gate_mat.T, preferred_element_type=jnp.float32)
        up_pre = jnp.dot(x_rows, up_mat.T, preferred_element_type=jnp.float32)
        sig_gate = jax.nn.sigmoid(gate_pre)
        silu_gate = gate_pre * sig_gate
        act_rows = (silu_gate * up_pre).astype(jnp.bfloat16)
        expert_out = jnp.dot(act_rows, down_mat, preferred_element_type=jnp.float32)
        dprob_rows = jnp.sum(dy_rows.astype(jnp.float32) * expert_out, axis=-1).astype(jnp.bfloat16)
        d_out = (weights.astype(jnp.float32)[:, None] * dy_rows.astype(jnp.float32)).astype(jnp.bfloat16)
        d_act = jnp.dot(d_out, down_mat.T, preferred_element_type=jnp.float32)
        d_gate = (d_act * up_pre * sig_gate * (1.0 + gate_pre * (1.0 - sig_gate))).astype(jnp.bfloat16)
        d_up = (d_act * silu_gate).astype(jnp.bfloat16)
        route_dx = (jnp.dot(d_gate, gate_mat, preferred_element_type=jnp.float32)
                    + jnp.dot(d_up, up_mat, preferred_element_type=jnp.float32)).astype(jnp.bfloat16)
        grad_rows = jnp.dot(act_rows.T, d_out, preferred_element_type=jnp.float32)
        dx_total = dx_total.at[token_index].add(route_dx.astype(jnp.float32))
        dprob_total = dprob_total.at[row_index].set(dprob_rows.astype(jnp.float32))
        return (dx_total, dprob_total), grad_rows

    start_state = (jnp.zeros((TOKENS + 1, D), jnp.float32), jnp.zeros((route_count + 1,), jnp.float32))
    final_state, grad_down = lax.scan(one_expert, start_state, jnp.arange(EXPERTS, dtype=jnp.int32))
    dx_total, dprob_total = final_state
    d_tokens = dx_total[:TOKENS].astype(jnp.bfloat16)
    d_probs = dprob_total[:route_count].reshape(TOKENS, TOP).astype(jnp.bfloat16)
    return d_tokens, d_probs, grad_down
```

```python
import jax
import jax.numpy as jnp
from jax import lax
from jax.sharding import PartitionSpec as P


def contract_last(left, right):
    return lax.dot_general(
        left, right, (((1,), (1,)), ((), ())), preferred_element_type=jnp.float32
    )


def contract_first(left, right):
    return lax.dot_general(
        left, right, (((0,), (0,)), ((), ())), preferred_element_type=jnp.float32
    )


def swap(value, axis, mask):
    return lax.ppermute(value, axis, [(i, i ^ mask) for i in range(lax.axis_size(axis))])


def local(tokens, upstream, expert_ids, route_weight, gate_weight, up_weight, down_weight):
    tok_dev, width = tokens.shape
    top = expert_ids.shape[1]
    experts, shards, reps = lax.axis_size("ep"), lax.axis_size("dp"), lax.axis_size("rep")
    cap = 2 * ((5 * tok_dev * top + 8 * experts - 1) // (8 * experts))
    rep, me = lax.axis_index("rep"), lax.axis_index("ep")
    hidden = gate_weight.shape[1] // reps

    mine = jnp.concatenate(
        [lax.dynamic_slice_in_dim(w[0], rep * hidden, hidden, 0) for w in (gate_weight, up_weight, down_weight)]
    )
    blocks = [mine] + [swap(mine, "dp", m) for m in range(1, shards)]

    onehot = (expert_ids[:, :, None] == jnp.arange(experts)[None, None, :]).astype(jnp.float32)
    named = jnp.sum(onehot, axis=1)
    before = jnp.dot(
        (jnp.arange(tok_dev)[:, None] > jnp.arange(tok_dev)[None, :]).astype(jnp.float32), named
    )
    rank = jnp.sum(before[:, None, :] * onehot, axis=2).astype(jnp.int32)
    d_out = (route_weight.astype(jnp.float32)[:, :, None] * upstream.astype(jnp.float32)[:, None, :]).astype(
        jnp.bfloat16
    )
    place = (expert_ids ^ me) * cap + rank
    select = (place[None, :, :] == jnp.arange(experts * cap)[:, None, None]).astype(jnp.bfloat16)
    x_send = jnp.dot(jnp.sum(select, axis=2), tokens, preferred_element_type=jnp.float32)
    dy_send = jnp.dot(
        select.transpose(0, 2, 1).reshape(experts * cap, top * tok_dev),
        d_out.transpose(1, 0, 2).reshape(top * tok_dev, width),
        preferred_element_type=jnp.float32,
    )
    send = jnp.concatenate(
        [x_send.reshape(experts, cap, width), dy_send.reshape(experts, cap, width)], axis=1
    ).astype(jnp.bfloat16)
    if experts <= 8:
        chunks = [send[0]] + [swap(send[m], "ep", m) for m in range(1, experts)]
    else:
        moved = lax.all_to_all(send[jnp.arange(experts) ^ me], "ep", split_axis=0, concat_axis=0, tiled=True)
        moved = moved[jnp.arange(experts) ^ me]
        chunks = [moved]
    other = [swap(c, "rep", 1) for c in chunks]
    rows = jnp.concatenate([c.reshape(-1, 2 * cap, width) for c in chunks + other])
    x_rows = rows[:, :cap].reshape(-1, width)
    d_out_rows = rows[:, cap:].reshape(-1, width)

    gate = jnp.concatenate([b[:hidden] for b in blocks])
    up = jnp.concatenate([b[hidden : 2 * hidden] for b in blocks])
    down = jnp.concatenate([b[2 * hidden :] for b in blocks])
    gate_pre = contract_last(x_rows, gate)
    up_pre = contract_last(x_rows, up)
    d_act = contract_last(d_out_rows, down)
    sig = jax.nn.sigmoid(gate_pre)
    silu = gate_pre * sig
    act = silu * up_pre
    d_gate = (d_act * up_pre * sig * (1.0 + gate_pre * (1.0 - sig))).astype(jnp.bfloat16)
    d_up = (d_act * silu).astype(jnp.bfloat16)
    act16 = act.astype(jnp.bfloat16)
    prob = jnp.sum(act * d_act, axis=1)
    dx = jnp.dot(d_gate, gate, preferred_element_type=jnp.float32)
    dx = dx + jnp.dot(d_up, up, preferred_element_type=jnp.float32)
    grad = contract_first(act16, d_out_rows).astype(jnp.bfloat16).reshape(shards, hidden, width)

    slots = experts * cap
    packed = jnp.concatenate(
        [
            dx.reshape(2 * experts, cap, width),
            jnp.pad(prob.reshape(2 * experts, 1, cap), ((0, 0), (0, 3), (0, width - cap))),
        ],
        axis=1,
    ).reshape(2, experts, cap + 4, width)
    home = packed[0] + swap(packed[1].astype(jnp.bfloat16), "rep", 1).astype(jnp.float32)
    home = home.astype(jnp.bfloat16)
    if experts <= 8:
        back = jnp.stack([home[0]] + [swap(home[m], "ep", m) for m in range(1, experts)])
    else:
        back = lax.all_to_all(home[jnp.arange(experts) ^ me], "ep", split_axis=0, concat_axis=0, tiled=True)
        back = back[jnp.arange(experts) ^ me]
    d_tokens = contract_first(jnp.sum(select, axis=2), back[:, :cap].reshape(slots, width)).astype(jnp.bfloat16)
    prob_back = back[:, cap, :cap].reshape(slots).astype(jnp.float32)
    d_probs = jnp.sum(select.astype(jnp.float32) * prob_back[:, None, None], axis=0)
    d_probs = (d_probs / route_weight.astype(jnp.float32)).astype(jnp.bfloat16)

    total = grad[0].astype(jnp.float32)
    for m in range(1, shards):
        total = total + swap(grad[m], "dp", m).astype(jnp.float32)
    total = total.astype(jnp.bfloat16)
    theirs = swap(total, "rep", 1)
    first = rep == 0
    grad_total = jnp.concatenate([jnp.where(first, total, theirs), jnp.where(first, theirs, total)])
    return (d_tokens, d_probs, grad_total.astype(jnp.float32)[None])


def solution(mesh):
    rows = P(("rep", "ep", "dp"), None)
    weights = P("ep", "dp", None)
    return jax.shard_map(
        local,
        mesh=mesh,
        in_specs=(rows,) * 4 + (weights,) * 3,
        out_specs=(rows, rows, weights),
        check_vma=False,
    )
```

```python
import functools

import jax
import jax.numpy as jnp
from jax import lax
from jax.experimental import pallas as pl
from jax.experimental.pallas import tpu as pltpu
from jax.sharding import PartitionSpec as P

LANES = 128
VMEM_BYTES = 48 * 1024 * 1024
f32, bf16 = jnp.float32, jnp.bfloat16


def dot(left, right, contract):
    return lax.dot_general(left, right, ((contract[0:1], contract[1:2]), ((), ())), preferred_element_type=f32)


def swap(value, axis, mask):
    return lax.ppermute(value, axis, [(i, i ^ mask) for i in range(lax.axis_size(axis))])


def kernel_call(body, inputs, outputs, flops=0, **kwargs):
    whole = pl.BlockSpec(memory_space=pltpu.VMEM)
    moved = sum(a.size * a.dtype.itemsize for a in inputs + outputs)
    return pl.pallas_call(
        body,
        out_shape=outputs,
        in_specs=kwargs.pop("in_specs", [whole] * len(inputs)),
        out_specs=[whole] * len(outputs),
        cost_estimate=pl.CostEstimate(flops=flops, bytes_accessed=moved, transcendentals=0),
        compiler_params=pltpu.CompilerParams(vmem_limit_bytes=VMEM_BYTES),
        **kwargs,
    )(*inputs)


def iota(shape, dim):
    return lax.broadcasted_iota(jnp.int32, shape, dim)


def dispatch_kernel(experts, cap, chunk_count, *refs):
    tokens, upstream, ids, route_weight, gate, up, down = refs[:7]
    chunks = refs[7 : 7 + chunk_count]
    slot_out, first, second, sems = refs[7 + chunk_count :]
    hidden, half = first.shape[0] // 3, first.shape[1]
    rep = lax.axis_index("rep")
    copies = []
    for i, weight in enumerate((gate, up, down)):
        for j, piece in enumerate((first, second)):
            copies.append(
                pltpu.make_async_copy(
                    weight.at[0, pl.ds(pl.multiple_of(rep * hidden, hidden), hidden), pl.ds(j * half, half)],
                    piece.at[pl.ds(i * hidden, hidden)],
                    sems.at[2 * i + j],
                )
            )
            copies[-1].start()

    tok_dev, top = ids.shape
    rows = experts * cap // chunk_count
    me = lax.axis_index("ep")
    wide = -(-experts // LANES) * LANES
    expert_of_lane = iota((tok_dev, wide), 1)
    named = [(expert_of_lane == ids[:, k : k + 1]).astype(f32) for k in range(top)]
    earlier = (iota((tok_dev, tok_dev), 0) > iota((tok_dev, tok_dev), 1)).astype(bf16)
    before = dot(earlier, sum(named).astype(bf16), (1, 0))
    lane = iota((tok_dev, 2 * experts * cap), 1)
    take_x = jnp.zeros(lane.shape, f32)
    take_dy = jnp.zeros(lane.shape, f32)
    scale = jnp.zeros((2 * experts * cap, LANES), f32)
    for k in range(top):
        rank = jnp.sum(before * named[k], axis=1, keepdims=True).astype(jnp.int32)
        expert = ids[:, k : k + 1]
        if chunk_count > 1:
            chunk = expert ^ me
            slot = chunk * cap + rank
            x_lane = slot + chunk * cap
        else:
            slot = expert * cap + rank
            x_lane = slot
        slot_out[:, k : k + 1] = slot
        take_x += (lane == x_lane).astype(f32)
        here = (lane == x_lane + rows).astype(f32)
        take_dy += here
        weight = jnp.broadcast_to(route_weight[:, k : k + 1], (tok_dev, LANES))
        scale += dot(here.astype(bf16), weight, (0, 0))
    scale += dot(take_x.astype(bf16), jnp.ones((tok_dev, LANES), bf16), (0, 0))
    picked = dot(take_x.astype(bf16), tokens[...], (0, 0)) + dot(take_dy.astype(bf16), upstream[...], (0, 0))
    picked = picked * scale[:, :1]
    for c in range(chunk_count):
        chunks[c][...] = picked[2 * rows * c : 2 * rows * (c + 1)].astype(bf16)
    for copy in copies:
        copy.wait()


def expert_math(x_rows, d_rows, pieces):
    width = x_rows.shape[1]
    half = width // 2
    acts, mixed, gates = [], [], []
    prob = 0.0
    for first, second in pieces:
        hidden = first.shape[0] // 3
        both, down = pl.ds(0, 2 * hidden), pl.ds(2 * hidden, hidden)
        pre = dot(x_rows[:, :half], first[both], (1, 1)) + dot(x_rows[:, half:], second[both], (1, 1))
        d_act = dot(d_rows[:, :half], first[down], (1, 1)) + dot(d_rows[:, half:], second[down], (1, 1))
        gate_pre, up_pre = pre[:, :hidden], pre[:, hidden:]
        sig = jax.nn.sigmoid(gate_pre)
        silu = gate_pre * sig
        act = silu * up_pre
        prob = prob + jnp.sum(act * d_act, axis=1, keepdims=True)
        acts.append(act)
        mixed += [d_act * up_pre * sig * (1.0 + gate_pre * (1.0 - sig)), d_act * silu]
        gates.append((first[both], second[both]))
    mixed = jnp.concatenate(mixed, axis=1).astype(bf16)
    acts = jnp.concatenate(acts, axis=1).astype(bf16)
    dx = [dot(mixed, jnp.concatenate([g[j] for g in gates]), (1, 0)) for j in range(2)]
    return dx, prob, dot(acts, d_rows, (0, 0))


def early_kernel(chunk_count, piece_count, *refs):
    chunks, refs = refs[:chunk_count], refs[chunk_count:]
    pieces, refs = refs[:piece_count], refs[piece_count:]
    x_out, d_out, dx_out, grad_own, *grads = refs
    rows = chunks[0].shape[0] // 2
    values = [c[...].astype(f32) for c in chunks]
    x_out[...] = jnp.concatenate([v[:rows] for v in values]).astype(bf16)
    d_out[...] = jnp.concatenate([v[rows:] for v in values]).astype(bf16)
    pairs = [(pieces[i], pieces[i + 1]) for i in range(0, piece_count, 2)]
    dx, prob, grad = expert_math(x_out[...], d_out[...], pairs)
    width = x_out.shape[1]
    dx_out[:, : width // 2] = dx[0]
    dx_out[:, width // 2 : width] = dx[1]
    dx_out[:, width:] = jnp.broadcast_to(prob, (prob.shape[0], LANES))
    hidden = grad_own.shape[0]
    grad_own[...] = grad[:hidden]
    for i, out in enumerate(grads):
        out[...] = grad[hidden * (i + 1) : hidden * (i + 2)].astype(bf16)


def late_kernel(x_ref, d_ref, dx_ref, first, second, keep, give, grad_out):
    dx, prob, grad = expert_math(x_ref[...], d_ref[...], [(first, second)])
    half, slots = dx[0].shape[1], keep.shape[0]
    for j, value in enumerate((dx[0], dx[1], jnp.broadcast_to(prob, (prob.shape[0], LANES)))):
        columns = slice(j * half, j * half + value.shape[1])
        total = value + dx_ref[:, columns]
        keep[:, columns] = total[:slots]
        give[:, columns] = total[slots:].astype(bf16)
    grad_out[...] = grad.astype(bf16)


def add_kernel(keep, got, *chunks):
    rows = chunks[0].shape[0]
    total = keep[...] + got[...].astype(f32)
    for c, chunk in enumerate(chunks):
        chunk[...] = total[c * rows : (c + 1) * rows].astype(bf16)


def combine_kernel(chunk_count, *refs):
    chunks, (slot, route_weight, tokens_out, probs_out) = refs[:chunk_count], refs[chunk_count:]
    rows = chunks[0].shape[0]
    tok_dev, width = tokens_out.shape
    top = slot.shape[1]
    total = 0.0
    probs = [0.0] * top
    for c in range(chunk_count):
        slot_of_lane = iota((tok_dev, rows), 1) + c * rows
        hits = [(slot_of_lane == slot[:, k : k + 1]).astype(f32) for k in range(top)]
        total = total + dot(sum(hits).astype(bf16), chunks[c][:, :width], (1, 0))
        for k in range(top):
            probs[k] = probs[k] + dot(hits[k].astype(bf16), chunks[c][:, width:], (1, 0))
    tokens_out[...] = total.astype(bf16)
    for k in range(top):
        weight = route_weight[:, k : k + 1].astype(f32)
        probs_out[:, k : k + 1] = (probs[k][:, :1] / weight).astype(bf16)


def local(tokens, upstream, expert_ids, route_weight, gate_weight, up_weight, down_weight):
    tok_dev, width = tokens.shape
    top = expert_ids.shape[1]
    experts, shards, reps = lax.axis_size("ep"), lax.axis_size("dp"), lax.axis_size("rep")
    cap = 2 * ((5 * tok_dev * top + 8 * experts - 1) // (8 * experts))
    slots = experts * cap
    chunk_count = experts if experts <= 8 else 1
    rows = slots // chunk_count
    hidden = gate_weight.shape[1] // reps
    shape = jax.ShapeDtypeStruct
    in_vmem, anywhere = pl.BlockSpec(memory_space=pltpu.VMEM), pl.BlockSpec(memory_space=pl.ANY)

    *chunks, slot, first, second = kernel_call(
        functools.partial(dispatch_kernel, experts, cap, chunk_count),
        [tokens, upstream, expert_ids, route_weight, gate_weight, up_weight, down_weight],
        [shape((2 * rows, width), bf16)] * chunk_count
        + [shape((tok_dev, top), jnp.int32)]
        + [shape((3 * hidden, width // 2), bf16)] * 2,
        in_specs=[in_vmem] * 4 + [anywhere] * 3,
        scratch_shapes=[pltpu.SemaphoreType.DMA((6,))],
    )

    if shards == 4:
        near = [[swap(piece, "dp", m) for piece in (first, second)] for m in (1, 2)]
        diagonal = [swap(near[0][0], "dp", 2), swap(near[1][1], "dp", 1)]
        blocks = [[first, second]] + near + [diagonal]
    else:
        blocks = [[first, second]] + [[swap(p, "dp", m) for p in (first, second)] for m in range(1, shards)]

    if chunk_count > 1:
        chunks = [chunks[0]] + [swap(chunks[m], "ep", m) for m in range(1, experts)]
    else:
        moved = chunks[0].reshape(2, experts, cap, width)
        moved = lax.all_to_all(moved, "ep", split_axis=1, concat_axis=1, tiled=True)
        chunks = [moved.reshape(2 * rows, width)]
    chunks = chunks + [swap(c, "rep", 1) for c in chunks]

    pieces = [p for block in blocks[:-1] for p in block]
    wide = width + LANES
    flops = 14 * 2 * slots * width * hidden
    x_rows, d_rows, dx, grad_own, *grads = kernel_call(
        functools.partial(early_kernel, 2 * chunk_count, len(pieces)),
        chunks + pieces,
        [shape((2 * slots, width), bf16)] * 2
        + [shape((2 * slots, wide), f32), shape((hidden, width), f32)]
        + [shape((hidden, width), bf16)] * (shards - 2),
        flops=flops * (shards - 1),
    )
    keep, give, grad_last = kernel_call(
        late_kernel,
        [x_rows, d_rows, dx] + blocks[-1],
        [shape((slots, wide), f32), shape((slots, wide), bf16), shape((hidden, width), bf16)],
        flops=flops,
    )
    back = kernel_call(add_kernel, [keep, swap(give, "rep", 1)], [shape((rows, wide), bf16)] * chunk_count)
    if chunk_count > 1:
        back = [back[0]] + [swap(back[m], "ep", m) for m in range(1, experts)]
    else:
        moved = back[0].reshape(experts, cap, wide)
        moved = lax.all_to_all(moved, "ep", split_axis=0, concat_axis=0, tiled=True)
        back = [moved.reshape(rows, wide)]
    d_tokens, d_probs = kernel_call(
        functools.partial(combine_kernel, chunk_count),
        back + [slot, route_weight],
        [shape((tok_dev, width), bf16), shape((tok_dev, top), bf16)],
    )

    total = grad_own
    for m, grad in enumerate(grads + [grad_last]):
        total = total + swap(grad, "dp", m + 1).astype(f32)
    total = total.astype(bf16)
    theirs = swap(total, "rep", 1)
    lower = lax.axis_index("rep") == 0
    grad_total = jnp.concatenate([jnp.where(lower, total, theirs), jnp.where(lower, theirs, total)])
    return (d_tokens, d_probs, grad_total.astype(f32)[None])


def solution(mesh):
    rows = P(("rep", "ep", "dp"), None)
    weights = P("ep", "dp", None)
    return jax.shard_map(
        local,
        mesh=mesh,
        in_specs=(rows,) * 4 + (weights,) * 3,
        out_specs=(rows, rows, weights),
        check_vma=False,
    )
```

```python
import functools

import jax
import jax.numpy as jnp
from jax import lax
from jax.experimental import pallas as pl
from jax.experimental.pallas import tpu as pltpu
from jax.sharding import PartitionSpec as P

LANES = 128
VMEM_BYTES = 32 * 1024 * 1024
f32, bf16 = jnp.float32, jnp.bfloat16


def dot(left, right, contract):
    return lax.dot_general(left, right, ((contract[0:1], contract[1:2]), ((), ())), preferred_element_type=f32)


def swap(value, axis, mask):
    return lax.ppermute(value, axis, [(i, i ^ mask) for i in range(lax.axis_size(axis))])


def kernel_call(body, inputs, outputs, flops=0, **kwargs):
    whole = pl.BlockSpec(memory_space=pltpu.VMEM)
    moved = sum(a.size * a.dtype.itemsize for a in inputs + outputs)
    return pl.pallas_call(
        body,
        out_shape=outputs,
        in_specs=kwargs.pop("in_specs", [whole] * len(inputs)),
        out_specs=[whole] * len(outputs),
        cost_estimate=pl.CostEstimate(flops=flops, bytes_accessed=moved, transcendentals=0),
        compiler_params=pltpu.CompilerParams(vmem_limit_bytes=VMEM_BYTES),
        **kwargs,
    )(*inputs)


def iota(shape, dim):
    return lax.broadcasted_iota(jnp.int32, shape, dim)


def dispatch_kernel(experts, cap, chunk_count, *refs):
    small, (gate, up, down), refs = refs[:4], refs[4:7], refs[7:]
    chunks, (slot_out, packed), refs = refs[:chunk_count], refs[chunk_count : chunk_count + 2], refs[chunk_count + 2 :]
    held, sems = refs[:4], refs[4]
    hidden = packed.shape[0] // 3
    rep = lax.axis_index("rep")
    half = pl.ds(pl.multiple_of(rep * hidden, hidden), hidden)
    loads = [pltpu.make_async_copy(*pair, sems.at[i]) for i, pair in enumerate(zip(small, held))]
    packs = [
        pltpu.make_async_copy(weight.at[0, half], packed.at[pl.ds(i * hidden, hidden)], sems.at[4 + i])
        for i, weight in enumerate((gate, up, down))
    ]
    for copy in loads + packs:
        copy.start()
    for copy in loads:
        copy.wait()

    tokens, upstream, ids, route_weight = held
    top, tok_dev = ids.shape
    rows = experts * cap // chunk_count
    me = lax.axis_index("ep")
    expert_of_row = iota((experts, tok_dev), 0)
    named = [(expert_of_row == ids[k : k + 1, :]).astype(f32) for k in range(top)]
    earlier = (iota((tok_dev, tok_dev), 0) < iota((tok_dev, tok_dev), 1)).astype(bf16)
    before = dot(sum(named).astype(bf16), earlier, (1, 0))
    row = iota((2 * experts * cap, tok_dev), 0)
    take_x = jnp.zeros(row.shape, f32)
    take_dy = jnp.zeros(row.shape, f32)
    scale = jnp.zeros(row.shape, f32)
    for k in range(top):
        rank = jnp.sum(before * named[k], axis=0, keepdims=True).astype(jnp.int32)
        expert = ids[k : k + 1, :]
        if chunk_count > 1:
            chunk = expert ^ me
            slot = chunk * cap + rank
            x_row = slot + chunk * cap
        else:
            slot = expert * cap + rank
            x_row = slot
        slot_out[k : k + 1, :] = slot
        here_x = (row == x_row).astype(f32)
        here_dy = (row == x_row + rows).astype(f32)
        take_x += here_x
        take_dy += here_dy
        scale += here_x + here_dy * route_weight[k : k + 1, :].astype(f32)
    picked = dot(take_x.astype(bf16), tokens[...], (1, 0)) + dot(take_dy.astype(bf16), upstream[...], (1, 0))
    picked = picked * jnp.sum(scale, axis=1, keepdims=True)
    for c in range(chunk_count):
        chunks[c][...] = picked[2 * rows * c : 2 * rows * (c + 1)].astype(bf16)
    for copy in packs:
        copy.wait()


def expert_math(x_rows, d_rows, pieces):
    width = x_rows.shape[1]
    half = width // 2
    acts, mixed, gates = [], [], []
    prob = 0.0
    for first, second in pieces:
        hidden = first.shape[0] // 3
        both, down = pl.ds(0, 2 * hidden), pl.ds(2 * hidden, hidden)
        pre = dot(x_rows[:, :half], first[both], (1, 1)) + dot(x_rows[:, half:], second[both], (1, 1))
        d_act = dot(d_rows[:, :half], first[down], (1, 1)) + dot(d_rows[:, half:], second[down], (1, 1))
        gate_pre, up_pre = pre[:, :hidden], pre[:, hidden:]
        sig = jax.nn.sigmoid(gate_pre)
        silu = gate_pre * sig
        act = silu * up_pre
        prob = prob + jnp.sum(act * d_act, axis=1, keepdims=True)
        acts.append(act)
        mixed += [d_act * up_pre * sig * (1.0 + gate_pre * (1.0 - sig)), d_act * silu]
        gates.append((first[both], second[both]))
    mixed = jnp.concatenate(mixed, axis=1).astype(bf16)
    acts = jnp.concatenate(acts, axis=1).astype(bf16)
    dx = [dot(mixed, jnp.concatenate([g[j] for g in gates]), (1, 0)) for j in range(2)]
    return dx, prob, dot(acts, d_rows, (0, 0))


def early_kernel(chunk_count, piece_count, *refs):
    chunks, refs = refs[:chunk_count], refs[chunk_count:]
    pieces, refs = refs[:piece_count], refs[piece_count:]
    x_out, d_out, dx_out, grad_own, *grads = refs
    rows = chunks[0].shape[0] // 2
    values = [c[...].astype(f32) for c in chunks]
    x_out[...] = jnp.concatenate([v[:rows] for v in values]).astype(bf16)
    d_out[...] = jnp.concatenate([v[rows:] for v in values]).astype(bf16)
    width = x_out.shape[1]
    pairs = [[p.at[:, pl.ds(j, width // 2)] for j in (0, width // 2)] for p in pieces]
    dx, prob, grad = expert_math(x_out[...], d_out[...], pairs)
    dx_out[:, : width // 2] = dx[0]
    dx_out[:, width // 2 : width] = dx[1]
    dx_out[:, width:] = jnp.broadcast_to(prob, (prob.shape[0], LANES))
    hidden = grad_own.shape[0]
    grad_own[...] = grad[:hidden]
    for i, out in enumerate(grads):
        out[...] = grad[hidden * (i + 1) : hidden * (i + 2)].astype(bf16)


def late_kernel(x_ref, d_ref, dx_ref, first, second, keep, give, grad_out):
    dx, prob, grad = expert_math(x_ref[...], d_ref[...], [(first, second)])
    half, slots = dx[0].shape[1], keep.shape[0]
    for j, value in enumerate((dx[0], dx[1], jnp.broadcast_to(prob, (prob.shape[0], LANES)))):
        columns = slice(j * half, j * half + value.shape[1])
        total = value + dx_ref[:, columns]
        keep[:, columns] = total[:slots]
        give[:, columns] = total[slots:].astype(bf16)
    grad_out[...] = grad.astype(bf16)


def add_kernel(keep, got, *chunks):
    rows = chunks[0].shape[0]
    total = keep[...] + got[...].astype(f32)
    for c, chunk in enumerate(chunks):
        chunk[...] = total[c * rows : (c + 1) * rows].astype(bf16)


def combine_kernel(chunk_count, *refs):
    chunks, (slot, route_weight, tokens_out, probs_out) = refs[:chunk_count], refs[chunk_count:]
    rows = chunks[0].shape[0]
    tok_dev, width = tokens_out.shape
    top = slot.shape[0]
    total = 0.0
    probs = [0.0] * top
    for c in range(chunk_count):
        slot_of_row = iota((rows, tok_dev), 0) + c * rows
        hits = [(slot_of_row == slot[k : k + 1, :]).astype(f32) for k in range(top)]
        total = total + dot(sum(hits).astype(bf16), chunks[c][:, :width], (0, 0))
        prob = chunks[c][:, width : width + 1].astype(f32)
        for k in range(top):
            probs[k] = probs[k] + jnp.sum(hits[k] * prob, axis=0, keepdims=True)
    tokens_out[...] = total.astype(bf16)
    for k in range(top):
        probs_out[k : k + 1, :] = (probs[k] / route_weight[k : k + 1, :].astype(f32)).astype(bf16)


def local(tokens, upstream, expert_ids, route_weight, gate_weight, up_weight, down_weight):
    tok_dev, width = tokens.shape
    top = expert_ids.shape[1]
    experts, shards, reps = lax.axis_size("ep"), lax.axis_size("dp"), lax.axis_size("rep")
    cap = 2 * ((5 * tok_dev * top + 8 * experts - 1) // (8 * experts))
    slots = experts * cap
    chunk_count = experts if experts <= 8 else 1
    rows = slots // chunk_count
    hidden = gate_weight.shape[1] // reps
    shape = jax.ShapeDtypeStruct
    in_hbm = pl.BlockSpec(memory_space=pltpu.HBM)

    small = [tokens, upstream, expert_ids.T, route_weight.T]
    *chunks, slot, packed = kernel_call(
        functools.partial(dispatch_kernel, experts, cap, chunk_count),
        [pltpu.with_memory_space_constraint(a, pltpu.HBM) for a in small + [gate_weight, up_weight, down_weight]],
        [shape((2 * rows, width), bf16)] * chunk_count
        + [shape((top, tok_dev), jnp.int32), shape((3 * hidden, width), bf16)],
        in_specs=[in_hbm] * 7,
        scratch_shapes=[pltpu.VMEM(a.shape, a.dtype) for a in small] + [pltpu.SemaphoreType.DMA((7,))],
    )

    half = width // 2
    if shards == 4:
        near = [packed] + [swap(packed, "dp", m) for m in (1, 2)]
        last = [swap(near[1][:, :half], "dp", 2), swap(near[2][:, half:], "dp", 1)]
    else:
        near = [packed] + [swap(packed, "dp", m) for m in range(1, shards - 1)]
        last = swap(packed, "dp", shards - 1)
        last = [last[:, :half], last[:, half:]]

    if chunk_count > 1:
        chunks = [chunks[0]] + [swap(chunks[m], "ep", m) for m in range(1, experts)]
    else:
        moved = chunks[0].reshape(2, experts, cap, width)
        moved = lax.all_to_all(moved, "ep", split_axis=1, concat_axis=1, tiled=True)
        chunks = [moved.reshape(2 * rows, width)]
    chunks = chunks + [swap(c, "rep", 1) for c in chunks]

    wide = width + LANES
    flops = 14 * 2 * slots * width * hidden
    x_rows, d_rows, dx, grad_own, *grads = kernel_call(
        functools.partial(early_kernel, 2 * chunk_count, len(near)),
        chunks + near,
        [shape((2 * slots, width), bf16)] * 2
        + [shape((2 * slots, wide), f32), shape((hidden, width), f32)]
        + [shape((hidden, width), bf16)] * (shards - 2),
        flops=flops * (shards - 1),
    )
    keep, give, grad_last = kernel_call(
        late_kernel,
        [x_rows, d_rows, dx] + last,
        [shape((slots, wide), f32), shape((slots, wide), bf16), shape((hidden, width), bf16)],
        flops=flops,
    )
    back = kernel_call(add_kernel, [keep, swap(give, "rep", 1)], [shape((rows, wide), bf16)] * chunk_count)
    grad_last, back = lax.optimization_barrier((grad_last, back))
    if chunk_count > 1:
        back = [back[0]] + [swap(back[m], "ep", m) for m in range(1, experts)]
    else:
        moved = back[0].reshape(experts, cap, wide)
        moved = lax.all_to_all(moved, "ep", split_axis=0, concat_axis=0, tiled=True)
        back = [moved.reshape(rows, wide)]
    d_tokens, d_probs = kernel_call(
        functools.partial(combine_kernel, chunk_count),
        back + [slot, route_weight.T],
        [shape((tok_dev, width), bf16), shape((top, tok_dev), bf16)],
    )

    arrived = [swap(grad, "dp", m + 1) for m, grad in enumerate(grads + [grad_last])]
    arrived, _ = lax.optimization_barrier((arrived, back[1:]))
    total = (grad_own + sum(a.astype(f32) for a in arrived)).astype(bf16)
    theirs = swap(total, "rep", 1)
    lower = lax.axis_index("rep") == 0
    grad_total = jnp.concatenate([jnp.where(lower, total, theirs), jnp.where(lower, theirs, total)])
    return (d_tokens, d_probs.T, grad_total.astype(f32)[None])


def solution(mesh):
    rows = P(("rep", "ep", "dp"), None)
    weights = P("ep", "dp", None)
    return jax.shard_map(
        local,
        mesh=mesh,
        in_specs=(rows,) * 4 + (weights,) * 3,
        out_specs=(rows, rows, weights),
        check_vma=False,
    )
```

```python
import functools

import jax
import jax.numpy as jnp
from jax import lax
from jax.experimental import pallas as pl
from jax.experimental.pallas import tpu as pltpu
from jax.sharding import PartitionSpec as P

LANES = 128
VMEM_BYTES = 32 * 1024 * 1024
f32, bf16 = jnp.float32, jnp.bfloat16


def dot(left, right, contract):
    return lax.dot_general(left, right, ((contract[0:1], contract[1:2]), ((), ())), preferred_element_type=f32)


def swap(value, axis, mask):
    return lax.ppermute(value, axis, [(i, i ^ mask) for i in range(lax.axis_size(axis))])


def kernel_call(body, inputs, outputs, flops=0, **kwargs):
    whole = pl.BlockSpec(memory_space=pltpu.VMEM)
    moved = sum(a.size * a.dtype.itemsize for a in inputs + outputs)
    return pl.pallas_call(
        body,
        out_shape=outputs,
        in_specs=kwargs.pop("in_specs", [whole] * len(inputs)),
        out_specs=[whole] * len(outputs),
        cost_estimate=pl.CostEstimate(flops=flops, bytes_accessed=moved, transcendentals=0),
        compiler_params=pltpu.CompilerParams(vmem_limit_bytes=VMEM_BYTES),
        **kwargs,
    )(*inputs)


def iota(shape, dim):
    return lax.broadcasted_iota(jnp.int32, shape, dim)


def dispatch_kernel(experts, cap, *refs):
    small, (gate, up, down), refs = refs[:4], refs[4:7], refs[7:]
    send, slot_out, packed, *held, sems = refs
    hidden = packed.shape[0] // 3
    rep = lax.axis_index("rep")
    half = pl.ds(pl.multiple_of(rep * hidden, hidden), hidden)
    loads = [pltpu.make_async_copy(*pair, sems.at[i]) for i, pair in enumerate(zip(small, held))]
    packs = [
        pltpu.make_async_copy(weight.at[0, half], packed.at[pl.ds(i * hidden, hidden)], sems.at[4 + i])
        for i, weight in enumerate((gate, up, down))
    ]
    for copy in loads + packs:
        copy.start()
    for copy in loads:
        copy.wait()

    tokens, upstream, ids, route_weight = held
    top, tok_dev = ids.shape
    expert_of_row = iota((experts, tok_dev), 0)
    named = [(expert_of_row == ids[k : k + 1, :]).astype(f32) for k in range(top)]
    earlier = (iota((tok_dev, tok_dev), 0) < iota((tok_dev, tok_dev), 1)).astype(bf16)
    before = dot(sum(named).astype(bf16), earlier, (1, 0))
    row = iota((2 * experts * cap, tok_dev), 0)
    take_x = jnp.zeros(row.shape, f32)
    take_dy = jnp.zeros(row.shape, f32)
    scale = jnp.zeros(row.shape, f32)
    for k in range(top):
        rank = jnp.sum(before * named[k], axis=0, keepdims=True).astype(jnp.int32)
        expert = ids[k : k + 1, :]
        slot = expert * cap + rank
        x_row = slot + expert * cap
        slot_out[k : k + 1, :] = slot
        here_x = (row == x_row).astype(f32)
        here_dy = (row == x_row + cap).astype(f32)
        take_x += here_x
        take_dy += here_dy
        scale += here_x + here_dy * route_weight[k : k + 1, :].astype(f32)
    picked = dot(take_x.astype(bf16), tokens[...], (1, 0)) + dot(take_dy.astype(bf16), upstream[...], (1, 0))
    picked = picked * jnp.sum(scale, axis=1, keepdims=True)
    send[...] = picked.astype(bf16)
    for copy in packs:
        copy.wait()


def expert_math(x_rows, d_rows, pieces):
    acts, mixed, held = [], [], []
    prob = 0.0
    for piece in pieces:
        hidden = piece[0].shape[0] // 3
        both, down = pl.ds(0, 2 * hidden), pl.ds(2 * hidden, hidden)
        pre = sum(dot(x, p[both], (1, 1)) for x, p in zip(x_rows, piece))
        d_act = sum(dot(d, p[down], (1, 1)) for d, p in zip(d_rows, piece))
        gate_pre, up_pre = pre[:, :hidden], pre[:, hidden:]
        sig = jax.nn.sigmoid(gate_pre)
        silu = gate_pre * sig
        act = silu * up_pre
        prob = prob + jnp.sum(act * d_act, axis=1, keepdims=True)
        acts.append(act)
        mixed += [d_act * up_pre * sig * (1.0 + gate_pre * (1.0 - sig)), d_act * silu]
        held.append([p[both] for p in piece])
    mixed = jnp.concatenate(mixed, axis=1).astype(bf16)
    acts = jnp.concatenate(acts, axis=1).astype(bf16)
    dx = [dot(mixed, jnp.concatenate([h[j] for h in held]), (1, 0)) for j in range(2)]
    return dx, prob, [dot(acts, d, (0, 0)) for d in d_rows]


def gather_kernel(*refs):
    chunks, *outs = refs
    rows, half = chunks.shape[1] // 2, outs[0].shape[1]
    values = [chunks[c].astype(f32) for c in range(chunks.shape[0])]
    for i, out in enumerate(outs):
        kind, side = slice(i // 2 * rows, (i // 2 + 1) * rows), slice(i % 2 * half, (i % 2 + 1) * half)
        out[...] = jnp.concatenate([v[kind, side] for v in values]).astype(bf16)


def both_cores(own, other):
    rows = [jnp.concatenate([a[...], b[...]]) for a, b in zip(own, other)]
    return rows[:2], rows[2:]


def early_kernel(*refs):
    x_rows, d_rows = both_cores(refs[:4], refs[4:8])
    count = (len(refs) - 9) // 2
    pieces, (dx_out, grad_own, *grads) = refs[8 : 8 + count], refs[8 + count :]
    half = x_rows[0].shape[1]
    sides = [slice(0, half), slice(half, 2 * half)]
    dx, prob, grad = expert_math(x_rows, d_rows, [[p.at[:, pl.ds(j * half, half)] for j in range(2)] for p in pieces])
    dx_out[:, 2 * half :] = jnp.broadcast_to(prob, (prob.shape[0], LANES))
    hidden = grad_own.shape[0]
    for j, side in enumerate(sides):
        dx_out[:, side] = dx[j]
        grad_own[:, side] = grad[j][:hidden]
        for i, out in enumerate(grads):
            out[:, side] = grad[j][hidden * (i + 1) : hidden * (i + 2)].astype(bf16)


def late_kernel(*refs):
    dx_ref, first, second, keep, give, grad_out = refs[8:]
    dx, prob, grad = expert_math(*both_cores(refs[:4], refs[4:8]), [(first, second)])
    half, slots = first.shape[1], keep.shape[0]
    for j, value in enumerate((dx[0], dx[1], jnp.broadcast_to(prob, (prob.shape[0], LANES)))):
        columns = slice(j * half, j * half + value.shape[1])
        total = value + dx_ref[:, columns]
        keep[:, columns] = total[:slots]
        give[:, columns] = total[slots:].astype(bf16)
    for j in range(2):
        grad_out[:, j * half : (j + 1) * half] = grad[j].astype(bf16)


def add_kernel(keep, got, out):
    out[...] = (keep[...] + got[...].astype(f32)).astype(bf16)


def combine_kernel(back, slot, route_weight, tokens_out, probs_out):
    slots = back.shape[0]
    tok_dev, width = tokens_out.shape
    top = slot.shape[0]
    slot_of_row = iota((slots, tok_dev), 0)
    hits = [(slot_of_row == slot[k : k + 1, :]).astype(f32) for k in range(top)]
    total = dot(sum(hits).astype(bf16), back[:, :width], (0, 0))
    prob = back[:, width : width + 1].astype(f32)
    probs = [jnp.sum(hit * prob, axis=0, keepdims=True) for hit in hits]
    tokens_out[...] = total.astype(bf16)
    for k in range(top):
        probs_out[k : k + 1, :] = (probs[k] / route_weight[k : k + 1, :].astype(f32)).astype(bf16)


def local(tokens, upstream, expert_ids, route_weight, gate_weight, up_weight, down_weight):
    tok_dev, width = tokens.shape
    top = expert_ids.shape[1]
    experts, shards, reps = lax.axis_size("ep"), lax.axis_size("dp"), lax.axis_size("rep")
    cap = 2 * ((5 * tok_dev * top + 8 * experts - 1) // (8 * experts))
    slots = experts * cap
    hidden = gate_weight.shape[1] // reps
    shape = jax.ShapeDtypeStruct
    in_hbm = pl.BlockSpec(memory_space=pltpu.HBM)

    small = [tokens, upstream, expert_ids.T, route_weight.T]
    send, slot, packed = kernel_call(
        functools.partial(dispatch_kernel, experts, cap),
        [pltpu.with_memory_space_constraint(a, pltpu.HBM) for a in small + [gate_weight, up_weight, down_weight]],
        [shape((2 * slots, width), bf16), shape((top, tok_dev), jnp.int32), shape((3 * hidden, width), bf16)],
        in_specs=[in_hbm] * 7,
        scratch_shapes=[pltpu.VMEM(a.shape, a.dtype) for a in small] + [pltpu.SemaphoreType.DMA((7,))],
    )

    half = width // 2
    if shards == 4:
        near = [packed] + [swap(packed, "dp", m) for m in (1, 2)]
        onward = [near[1][:, :half], near[2][:, half:]]
        last = [swap(onward[0], "dp", 2), swap(onward[1], "dp", 1)]
    else:
        near = [packed] + [swap(packed, "dp", m) for m in range(1, shards - 1)]
        onward = near
        last = swap(packed, "dp", shards - 1)
        last = [last[:, :half], last[:, half:]]

    moved = lax.all_to_all(send.reshape(experts, 2 * cap, width), "ep", split_axis=0, concat_axis=0, tiled=True)
    own = kernel_call(gather_kernel, [moved], [shape((slots, half), bf16)] * 4)
    other = [swap(part, "rep", 1) for part in own]

    wide = width + LANES
    flops = 14 * 2 * slots * width * hidden
    dx, grad_own, *grads = kernel_call(
        early_kernel,
        [*own, *other, *near],
        [shape((2 * slots, wide), f32), shape((hidden, width), f32)]
        + [shape((hidden, width), bf16)] * (shards - 2),
        flops=flops * (shards - 1),
    )
    keep, give, grad_last = kernel_call(
        late_kernel,
        [*own, *other, dx, *last],
        [shape((slots, wide), f32), shape((slots, wide), bf16), shape((hidden, width), bf16)],
        flops=flops,
    )
    (back,) = kernel_call(add_kernel, [keep, swap(give, "rep", 1)], [shape((slots, wide), bf16)])
    grads, grad_last, back = lax.optimization_barrier((grads, grad_last, back))
    back = lax.all_to_all(back.reshape(experts, cap, wide), "ep", split_axis=0, concat_axis=0, tiled=True)
    back = back.reshape(slots, wide)
    d_tokens, d_probs = kernel_call(
        combine_kernel,
        [back, slot, route_weight.T],
        [shape((tok_dev, width), bf16), shape((top, tok_dev), bf16)],
    )

    arrived = [swap(grad, "dp", m + 1) for m, grad in enumerate([*grads, grad_last])]
    arrived, _ = lax.optimization_barrier((arrived, back))
    total = (grad_own + sum(a.astype(f32) for a in arrived)).astype(bf16)
    theirs = swap(total, "rep", 1)
    lower = lax.axis_index("rep") == 0
    grad_total = jnp.concatenate([jnp.where(lower, total, theirs), jnp.where(lower, theirs, total)])
    return (d_tokens, d_probs.T, grad_total.astype(f32)[None])


def solution(mesh):
    rows = P(("rep", "ep", "dp"), None)
    weights = P("ep", "dp", None)
    return jax.shard_map(
        local,
        mesh=mesh,
        in_specs=(rows,) * 4 + (weights,) * 3,
        out_specs=(rows, rows, weights),
        check_vma=False,
    )
```

```python
import functools

import jax
import jax.numpy as jnp
from jax import lax
from jax.experimental import pallas as pl
from jax.experimental.pallas import tpu as pltpu
from jax.sharding import PartitionSpec as P

LANES = 128
VMEM_BYTES = 32 * 1024 * 1024
f32, bf16 = jnp.float32, jnp.bfloat16


def dot(left, right, contract):
    return lax.dot_general(left, right, ((contract[0:1], contract[1:2]), ((), ())), preferred_element_type=f32)


def swap(value, axis, mask):
    return lax.ppermute(value, axis, [(i, i ^ mask) for i in range(lax.axis_size(axis))])


def swap_by_core(value, masks):
    count = lax.axis_size("dp")
    pairs = [(r * count + i, r * count + (i ^ mask)) for r, mask in enumerate(masks) for i in range(count)]
    return lax.ppermute(value, ("rep", "dp"), pairs)


def kernel_call(body, inputs, outputs, flops=0, **kwargs):
    whole = pl.BlockSpec(memory_space=pltpu.VMEM)
    moved = sum(a.size * a.dtype.itemsize for a in inputs + outputs)
    return pl.pallas_call(
        body,
        out_shape=outputs,
        in_specs=kwargs.pop("in_specs", [whole] * len(inputs)),
        out_specs=[whole] * len(outputs),
        cost_estimate=pl.CostEstimate(flops=flops, bytes_accessed=moved, transcendentals=0),
        compiler_params=pltpu.CompilerParams(vmem_limit_bytes=VMEM_BYTES),
        **kwargs,
    )(*inputs)


def iota(shape, dim):
    return lax.broadcasted_iota(jnp.int32, shape, dim)


def dispatch_kernel(experts, cap, chunk_count, *refs):
    small, (gate, up, down), refs = refs[:4], refs[4:7], refs[7:]
    chunks, (slot_out, *held, sems) = refs[:chunk_count], refs[chunk_count:]
    packed, held = held[:2], held[2:]
    hidden = packed[0].shape[0] // 3
    rep = lax.axis_index("rep")
    loads = [pltpu.make_async_copy(*pair, sems.at[i]) for i, pair in enumerate(zip(small, held))]
    packs = []
    for j, half in enumerate((rep, 1 - rep)):
        rows = pl.ds(pl.multiple_of(half * hidden, hidden), hidden)
        packs += [
            pltpu.make_async_copy(weight.at[0, rows], packed[j].at[pl.ds(i * hidden, hidden)], sems.at[4 + 3 * j + i])
            for i, weight in enumerate((gate, up, down))
        ]
    for copy in loads + packs:
        copy.start()
    for copy in loads:
        copy.wait()

    tokens, upstream, ids, route_weight = held
    top, tok_dev = ids.shape
    rows = experts * cap // chunk_count
    me = lax.axis_index("ep")
    expert_of_row = iota((experts, tok_dev), 0)
    named = [(expert_of_row == ids[k : k + 1, :]).astype(f32) for k in range(top)]
    earlier = (iota((tok_dev, tok_dev), 0) < iota((tok_dev, tok_dev), 1)).astype(bf16)
    before = dot(sum(named).astype(bf16), earlier, (1, 0))
    row = iota((2 * experts * cap, tok_dev), 0)
    take_x = jnp.zeros(row.shape, f32)
    take_dy = jnp.zeros(row.shape, f32)
    scale = jnp.zeros(row.shape, f32)
    for k in range(top):
        rank = jnp.sum(before * named[k], axis=0, keepdims=True).astype(jnp.int32)
        expert = ids[k : k + 1, :]
        if chunk_count > 1:
            chunk = expert ^ me
            slot = chunk * cap + rank
            x_row = slot + chunk * cap
        else:
            slot = expert * cap + rank
            x_row = slot
        slot_out[k : k + 1, :] = slot
        here_x = (row == x_row).astype(f32)
        here_dy = (row == x_row + rows).astype(f32)
        take_x += here_x
        take_dy += here_dy
        scale += here_x + here_dy * route_weight[k : k + 1, :].astype(f32)
    picked = dot(take_x.astype(bf16), tokens[...], (1, 0)) + dot(take_dy.astype(bf16), upstream[...], (1, 0))
    picked = picked * jnp.sum(scale, axis=1, keepdims=True)
    for c in range(chunk_count):
        chunks[c][...] = picked[2 * rows * c : 2 * rows * (c + 1)].astype(bf16)
    for copy in packs:
        copy.wait()


def expert_math(x_rows, d_rows, pieces):
    acts, mixed = [], []
    prob = 0.0
    for piece in pieces:
        hidden = piece.shape[0] // 3
        pre = dot(x_rows, piece[: 2 * hidden], (1, 1))
        d_act = dot(d_rows, piece[2 * hidden :], (1, 1))
        gate_pre, up_pre = pre[:, :hidden], pre[:, hidden:]
        sig = jax.nn.sigmoid(gate_pre)
        silu = gate_pre * sig
        act = silu * up_pre
        prob = prob + jnp.sum(act * d_act, axis=1, keepdims=True)
        acts.append(act)
        mixed += [d_act * up_pre * sig * (1.0 + gate_pre * (1.0 - sig)), d_act * silu]
    mixed = jnp.concatenate(mixed, axis=1).astype(bf16)
    acts = jnp.concatenate(acts, axis=1).astype(bf16)
    gates = jnp.concatenate([piece[: 2 * hidden] for piece in pieces])
    return dot(mixed, gates, (1, 0)), prob, dot(acts, d_rows, (0, 0))


def early_kernel(chunk_count, *refs):
    chunks, (own, near, x_out, d_out, dx_out, grad_own, grad_near) = refs[:chunk_count], refs[chunk_count:]
    rows = chunks[0].shape[0] // 2
    values = [c[...].astype(f32) for c in chunks]
    x_out[...] = jnp.concatenate([v[:rows] for v in values]).astype(bf16)
    d_out[...] = jnp.concatenate([v[rows:] for v in values]).astype(bf16)
    dx, prob, grad = expert_math(x_out[...], d_out[...], [own, near])
    width, hidden = dx.shape[1], grad_own.shape[0]
    dx_out[:, :width] = dx
    dx_out[:, width:] = jnp.broadcast_to(prob, (prob.shape[0], LANES))
    grad_own[...] = grad[:hidden]
    grad_near[...] = grad[hidden:].astype(bf16)


def late_kernel(x_ref, d_ref, dx_ref, grad_ref, near, far, keep, give, grad_near, grad_far):
    dx, prob, grad = expert_math(x_ref[...], d_ref[...], [near, far])
    width, slots, hidden = dx.shape[1], keep.shape[0], grad_far.shape[0]
    for side, value in ((slice(0, width), dx), (slice(width, None), jnp.broadcast_to(prob, (prob.shape[0], LANES)))):
        total = value + dx_ref[:, side]
        keep[:, side] = total[:slots]
        give[:, side] = total[slots:].astype(bf16)
    grad_near[:hidden] = grad_ref[...]
    grad_near[hidden:] = grad[:hidden].astype(bf16)
    grad_far[...] = grad[hidden:].astype(bf16)


def grad_kernel(own, near, far, out):
    hidden = own.shape[0]
    out[:hidden] = (own[...] + near[:hidden].astype(f32) + far[...].astype(f32)).astype(bf16)
    out[hidden:] = near[hidden:]


def total_kernel(mine, theirs, out):
    hidden = mine.shape[0] // 2
    rep = lax.axis_index("rep")
    for i, half in enumerate((rep, 1 - rep)):
        here, there = slice(i * hidden, (i + 1) * hidden), slice((1 - i) * hidden, (2 - i) * hidden)
        rows = pl.ds(pl.multiple_of(half * hidden, hidden), hidden)
        out[0, rows] = mine[here].astype(f32) + theirs[there].astype(f32)


def add_kernel(keep, got, *chunks):
    rows = chunks[0].shape[0]
    total = keep[...] + got[...].astype(f32)
    for c, chunk in enumerate(chunks):
        chunk[...] = total[c * rows : (c + 1) * rows].astype(bf16)


def combine_kernel(chunk_count, *refs):
    chunks, (slot, route_weight, tokens_out, probs_out) = refs[:chunk_count], refs[chunk_count:]
    rows = chunks[0].shape[0]
    tok_dev, width = tokens_out.shape
    top = slot.shape[0]
    total = 0.0
    probs = [0.0] * top
    for c in range(chunk_count):
        slot_of_row = iota((rows, tok_dev), 0) + c * rows
        hits = [(slot_of_row == slot[k : k + 1, :]).astype(f32) for k in range(top)]
        total = total + dot(sum(hits).astype(bf16), chunks[c][:, :width], (0, 0))
        prob = chunks[c][:, width : width + 1].astype(f32)
        for k in range(top):
            probs[k] = probs[k] + jnp.sum(hits[k] * prob, axis=0, keepdims=True)
    tokens_out[...] = total.astype(bf16)
    for k in range(top):
        probs_out[k : k + 1, :] = (probs[k] / route_weight[k : k + 1, :].astype(f32)).astype(bf16)


def local(tokens, upstream, expert_ids, route_weight, gate_weight, up_weight, down_weight):
    tok_dev, width = tokens.shape
    top = expert_ids.shape[1]
    experts, reps = lax.axis_size("ep"), lax.axis_size("rep")
    cap = 2 * ((5 * tok_dev * top + 8 * experts - 1) // (8 * experts))
    slots = experts * cap
    chunk_count = experts if experts <= 8 else 1
    rows = slots // chunk_count
    hidden = gate_weight.shape[1] // reps
    shape = jax.ShapeDtypeStruct
    in_hbm = pl.BlockSpec(memory_space=pltpu.HBM)

    small = [tokens, upstream, expert_ids.T, route_weight.T]
    *chunks, slot, first, second = kernel_call(
        functools.partial(dispatch_kernel, experts, cap, chunk_count),
        [pltpu.with_memory_space_constraint(a, pltpu.HBM) for a in small + [gate_weight, up_weight, down_weight]],
        [shape((2 * rows, width), bf16)] * chunk_count
        + [shape((top, tok_dev), jnp.int32)]
        + [shape((3 * hidden, width), bf16)] * 2,
        in_specs=[in_hbm] * 7,
        scratch_shapes=[pltpu.VMEM(a.shape, a.dtype) for a in small] + [pltpu.SemaphoreType.DMA((10,))],
    )

    along, across = (1, 2), (2, 1)
    near = [swap_by_core(first, along), swap_by_core(second, along)]
    far = swap_by_core(near[0], across)

    if chunk_count > 1:
        chunks = [chunks[0]] + [swap(chunks[m], "ep", m) for m in range(1, experts)]
    else:
        moved = chunks[0].reshape(2, experts, cap, width)
        moved = lax.all_to_all(moved, "ep", split_axis=1, concat_axis=1, tiled=True)
        chunks = [moved.reshape(2 * rows, width)]
    chunks = chunks + [swap(c, "rep", 1) for c in chunks]

    wide = width + LANES
    x_rows, d_rows, dx, grad_own, grad_near = kernel_call(
        functools.partial(early_kernel, 2 * chunk_count),
        chunks + [first, near[0]],
        [shape((2 * slots, width), bf16)] * 2
        + [shape((2 * slots, wide), f32), shape((hidden, width), f32), shape((hidden, width), bf16)],
        flops=4 * 10**9,
    )
    keep, give, grad_near, grad_far = kernel_call(
        late_kernel,
        [x_rows, d_rows, dx, grad_near, near[1], far],
        [shape((slots, wide), f32), shape((slots, wide), bf16)]
        + [shape((2 * hidden, width), bf16), shape((hidden, width), bf16)],
    )
    back = kernel_call(add_kernel, [keep, swap(give, "rep", 1)], [shape((rows, wide), bf16)] * chunk_count)
    if chunk_count > 1:
        back = [back[0]] + [swap(back[m], "ep", m) for m in range(1, experts)]
    else:
        moved = back[0].reshape(experts, cap, wide)
        moved = lax.all_to_all(moved, "ep", split_axis=0, concat_axis=0, tiled=True)
        back = [moved.reshape(rows, wide)]
    d_tokens, d_probs = kernel_call(
        functools.partial(combine_kernel, chunk_count),
        back + [slot, route_weight.T],
        [shape((tok_dev, width), bf16), shape((top, tok_dev), bf16)],
    )

    arrived = swap_by_core(grad_near, along), swap_by_core(grad_far, (3, 3))
    arrived, _ = lax.optimization_barrier((arrived, back[1:]))
    (mine,) = kernel_call(grad_kernel, [grad_own, *arrived], [shape((2 * hidden, width), bf16)])
    (grad_total,) = kernel_call(
        total_kernel, [mine, swap(mine, "rep", 1)], [shape((1, 2 * hidden, width), f32)]
    )
    return d_tokens, d_probs.T, grad_total


def solution(mesh):
    rows = P(("rep", "ep", "dp"), None)
    weights = P("ep", "dp", None)
    return jax.shard_map(
        local,
        mesh=mesh,
        in_specs=(rows,) * 4 + (weights,) * 3,
        out_specs=(rows, rows, weights),
        check_vma=False,
    )
```

```python
import functools

import jax
import jax.numpy as jnp
from jax import lax
from jax.experimental import pallas as pl
from jax.experimental.pallas import tpu as pltpu
from jax.sharding import PartitionSpec as P

LANES = 128
VMEM_BYTES = 32 * 1024 * 1024
f32, bf16 = jnp.float32, jnp.bfloat16


def dot(left, right, contract):
    return lax.dot_general(left, right, ((contract[0:1], contract[1:2]), ((), ())), preferred_element_type=f32)


def swap(value, axis, mask):
    return lax.ppermute(value, axis, [(i, i ^ mask) for i in range(lax.axis_size(axis))])


def exchange(chunks):
    count = len(chunks)
    return [chunks[0]] + [swap(chunks[c], "ep", count - c) for c in range(1, count)]


def swap_by_core(value, masks):
    count = lax.axis_size("dp")
    pairs = [(r * count + i, r * count + (i ^ mask)) for r, mask in enumerate(masks) for i in range(count)]
    return lax.ppermute(value, ("rep", "dp"), pairs)


def kernel_call(body, inputs, outputs, flops=0, **kwargs):
    whole = pl.BlockSpec(memory_space=pltpu.VMEM)
    moved = sum(a.size * a.dtype.itemsize for a in inputs + outputs)
    return pl.pallas_call(
        body,
        out_shape=outputs,
        in_specs=kwargs.pop("in_specs", [whole] * len(inputs)),
        out_specs=[whole] * len(outputs),
        cost_estimate=pl.CostEstimate(flops=flops, bytes_accessed=moved, transcendentals=0),
        compiler_params=pltpu.CompilerParams(vmem_limit_bytes=VMEM_BYTES),
        **kwargs,
    )(*inputs)


def iota(shape, dim):
    return lax.broadcasted_iota(jnp.int32, shape, dim)


def dispatch_kernel(experts, cap, chunk_count, *refs):
    small, (gate, up, down), refs = refs[:4], refs[4:7], refs[7:]
    chunks, (slot_out, *held, sems) = refs[:chunk_count], refs[chunk_count:]
    packed, held = held[:2], held[2:]
    hidden = packed[0].shape[0] // 3
    rep = lax.axis_index("rep")
    loads = [pltpu.make_async_copy(*pair, sems.at[i]) for i, pair in enumerate(zip(small, held))]
    packs = []
    for j, half in enumerate((rep, 1 - rep)):
        rows = pl.ds(pl.multiple_of(half * hidden, hidden), hidden)
        packs += [
            pltpu.make_async_copy(weight.at[0, rows], packed[j].at[pl.ds(i * hidden, hidden)], sems.at[4 + 3 * j + i])
            for i, weight in enumerate((gate, up, down))
        ]
    for copy in loads + packs:
        copy.start()
    for copy in loads:
        copy.wait()

    tokens, upstream, ids, route_weight = held
    top, tok_dev = ids.shape
    rows = experts * cap // chunk_count
    me = lax.axis_index("ep")
    expert_of_row = iota((experts, tok_dev), 0)
    named = [(expert_of_row == ids[k : k + 1, :]).astype(f32) for k in range(top)]
    earlier = (iota((tok_dev, tok_dev), 0) < iota((tok_dev, tok_dev), 1)).astype(bf16)
    before = dot(sum(named).astype(bf16), earlier, (1, 0))
    row = iota((2 * experts * cap, tok_dev), 0)
    take_x = jnp.zeros(row.shape, f32)
    take_dy = jnp.zeros(row.shape, f32)
    scale = jnp.zeros(row.shape, f32)
    for k in range(top):
        rank = jnp.sum(before * named[k], axis=0, keepdims=True).astype(jnp.int32)
        expert = ids[k : k + 1, :]
        if chunk_count > 1:
            mask = expert ^ me
            chunk = jnp.where(mask == 0, 0, experts - mask)
            slot = chunk * cap + rank
            x_row = slot + chunk * cap
        else:
            slot = expert * cap + rank
            x_row = slot
        slot_out[k : k + 1, :] = slot
        here_x = (row == x_row).astype(f32)
        here_dy = (row == x_row + rows).astype(f32)
        take_x += here_x
        take_dy += here_dy
        scale += here_x + here_dy * route_weight[k : k + 1, :].astype(f32)
    picked = dot(take_x.astype(bf16), tokens[...], (1, 0)) + dot(take_dy.astype(bf16), upstream[...], (1, 0))
    picked = picked * jnp.sum(scale, axis=1, keepdims=True)
    for c in range(chunk_count):
        chunks[c][...] = picked[2 * rows * c : 2 * rows * (c + 1)].astype(bf16)
    for copy in packs:
        copy.wait()


def expert_math(x_rows, d_rows, pieces):
    acts, mixed = [], []
    prob = 0.0
    for piece in pieces:
        hidden = piece.shape[0] // 3
        pre = dot(x_rows, piece[: 2 * hidden], (1, 1))
        d_act = dot(d_rows, piece[2 * hidden :], (1, 1))
        gate_pre, up_pre = pre[:, :hidden], pre[:, hidden:]
        sig = jax.nn.sigmoid(gate_pre)
        silu = gate_pre * sig
        act = silu * up_pre
        prob = prob + jnp.sum(act * d_act, axis=1, keepdims=True)
        acts.append(act)
        mixed += [d_act * up_pre * sig * (1.0 + gate_pre * (1.0 - sig)), d_act * silu]
    mixed = jnp.concatenate(mixed, axis=1).astype(bf16)
    acts = jnp.concatenate(acts, axis=1).astype(bf16)
    gates = jnp.concatenate([piece[: 2 * hidden] for piece in pieces])
    return dot(mixed, gates, (1, 0)), prob, dot(acts, d_rows, (0, 0))


def early_kernel(chunk_count, *refs):
    chunks, (*pieces, x_out, d_out, dx_out, grad_own, grad_near) = refs[:chunk_count], refs[chunk_count:]
    rows = chunks[0].shape[0] // 2
    values = [c[...].astype(f32) for c in chunks]
    x_out[...] = jnp.concatenate([v[:rows] for v in values]).astype(bf16)
    d_out[...] = jnp.concatenate([v[rows:] for v in values]).astype(bf16)
    dx, prob, grad = expert_math(x_out[...], d_out[...], pieces)
    width, hidden = dx.shape[1], grad_own.shape[0]
    dx_out[:, :width] = dx
    dx_out[:, width:] = jnp.broadcast_to(prob, (prob.shape[0], LANES))
    grad_own[...] = grad[:hidden]
    grad_near[...] = grad[hidden:].astype(bf16)


def late_kernel(x_ref, d_ref, dx_ref, far, keep, give, grad_far):
    dx, prob, grad = expert_math(x_ref[...], d_ref[...], [far])
    width, slots = dx.shape[1], keep.shape[0]
    for side, value in ((slice(0, width), dx), (slice(width, None), jnp.broadcast_to(prob, (prob.shape[0], LANES)))):
        total = value + dx_ref[:, side]
        keep[:, side] = total[:slots]
        give[:, side] = total[slots:].astype(bf16)
    grad_far[...] = grad.astype(bf16)


def grad_kernel(own, near, far, out):
    hidden = own.shape[0]
    out[:hidden] = (own[...] + near[:hidden].astype(f32) + far[...].astype(f32)).astype(bf16)
    out[hidden:] = near[hidden:]


def total_kernel(mine, theirs, out):
    hidden = mine.shape[0] // 2
    rep = lax.axis_index("rep")
    for i, half in enumerate((rep, 1 - rep)):
        here, there = slice(i * hidden, (i + 1) * hidden), slice((1 - i) * hidden, (2 - i) * hidden)
        rows = pl.ds(pl.multiple_of(half * hidden, hidden), hidden)
        out[0, rows] = mine[here].astype(f32) + theirs[there].astype(f32)


def add_kernel(keep, got, *chunks):
    rows = chunks[0].shape[0]
    total = keep[...] + got[...].astype(f32)
    for c, chunk in enumerate(chunks):
        chunk[...] = total[c * rows : (c + 1) * rows].astype(bf16)


def combine_kernel(chunk_count, *refs):
    chunks, (slot, route_weight, tokens_out, probs_out) = refs[:chunk_count], refs[chunk_count:]
    rows = chunks[0].shape[0]
    tok_dev, width = tokens_out.shape
    top = slot.shape[0]
    total = 0.0
    probs = [0.0] * top
    for c in range(chunk_count):
        slot_of_row = iota((rows, tok_dev), 0) + c * rows
        hits = [(slot_of_row == slot[k : k + 1, :]).astype(f32) for k in range(top)]
        total = total + dot(sum(hits).astype(bf16), chunks[c][:, :width], (0, 0))
        prob = chunks[c][:, width : width + 1].astype(f32)
        for k in range(top):
            probs[k] = probs[k] + jnp.sum(hits[k] * prob, axis=0, keepdims=True)
    tokens_out[...] = total.astype(bf16)
    for k in range(top):
        probs_out[k : k + 1, :] = (probs[k] / route_weight[k : k + 1, :].astype(f32)).astype(bf16)


def local(tokens, upstream, expert_ids, route_weight, gate_weight, up_weight, down_weight):
    tok_dev, width = tokens.shape
    top = expert_ids.shape[1]
    experts, reps = lax.axis_size("ep"), lax.axis_size("rep")
    cap = 2 * ((5 * tok_dev * top + 8 * experts - 1) // (8 * experts))
    slots = experts * cap
    chunk_count = experts if experts <= 8 else 1
    rows = slots // chunk_count
    hidden = gate_weight.shape[1] // reps
    shape = jax.ShapeDtypeStruct
    in_hbm = pl.BlockSpec(memory_space=pltpu.HBM)

    small = [tokens, upstream, expert_ids.T, route_weight.T]
    *chunks, slot, first, second = kernel_call(
        functools.partial(dispatch_kernel, experts, cap, chunk_count),
        [pltpu.with_memory_space_constraint(a, pltpu.HBM) for a in small + [gate_weight, up_weight, down_weight]],
        [shape((2 * rows, width), bf16)] * chunk_count
        + [shape((top, tok_dev), jnp.int32)]
        + [shape((3 * hidden, width), bf16)] * 2,
        in_specs=[in_hbm] * 7,
        scratch_shapes=[pltpu.VMEM(a.shape, a.dtype) for a in small] + [pltpu.SemaphoreType.DMA((10,))],
    )

    along, across = (1, 2), (2, 1)
    near = [swap_by_core(first, along), swap_by_core(second, along)]
    far = swap_by_core(near[0], across)

    if chunk_count > 1:
        chunks = exchange(chunks)
    else:
        moved = chunks[0].reshape(2, experts, cap, width)
        moved = lax.all_to_all(moved, "ep", split_axis=1, concat_axis=1, tiled=True)
        chunks = [moved.reshape(2 * rows, width)]
    chunks = chunks + [swap(c, "rep", 1) for c in chunks]

    wide = width + LANES
    x_rows, d_rows, dx, grad_own, grad_near = kernel_call(
        functools.partial(early_kernel, 2 * chunk_count),
        chunks + [first, *near],
        [shape((2 * slots, width), bf16)] * 2
        + [shape((2 * slots, wide), f32), shape((hidden, width), f32), shape((2 * hidden, width), bf16)],
        flops=4*10**9,
    )
    keep, give, grad_far = kernel_call(
        late_kernel,
        [x_rows, d_rows, dx, far],
        [shape((slots, wide), f32), shape((slots, wide), bf16), shape((hidden, width), bf16)],
    )
    back = kernel_call(add_kernel, [keep, swap(give, "rep", 1)], [shape((rows, wide), bf16)] * chunk_count)
    grad_far, back = lax.optimization_barrier((grad_far, back))
    if chunk_count > 1:
        back = exchange(back)
    else:
        moved = back[0].reshape(experts, cap, wide)
        moved = lax.all_to_all(moved, "ep", split_axis=0, concat_axis=0, tiled=True)
        back = [moved.reshape(rows, wide)]
    d_tokens, d_probs = kernel_call(
        functools.partial(combine_kernel, chunk_count),
        back + [slot, route_weight.T],
        [shape((tok_dev, width), bf16), shape((top, tok_dev), bf16)],
        flops=8*10**9,
    )

    arrived = swap_by_core(grad_near, along), swap_by_core(grad_far, (3, 3))
    (mine,) = kernel_call(grad_kernel, [grad_own, *arrived], [shape((2 * hidden, width), bf16)])
    (grad_total,) = kernel_call(
        total_kernel, [mine, swap(mine, "rep", 1)], [shape((1, 2 * hidden, width), f32)]
    )
    return d_tokens, d_probs.T, grad_total


def solution(mesh):
    rows = P(("rep", "ep", "dp"), None)
    weights = P("ep", "dp", None)
    return jax.shard_map(
        local,
        mesh=mesh,
        in_specs=(rows,) * 4 + (weights,) * 3,
        out_specs=(rows, rows, weights),
        check_vma=False,
    )
```

```python
import functools

import jax
import jax.numpy as jnp
from jax import lax
from jax.experimental import pallas as pl
from jax.experimental.pallas import tpu as pltpu
from jax.sharding import PartitionSpec as P

LANES = 128
VMEM_BYTES = 32 * 1024 * 1024
f32, bf16 = jnp.float32, jnp.bfloat16


def dot(left, right, contract):
    return lax.dot_general(left, right, ((contract[0:1], contract[1:2]), ((), ())), preferred_element_type=f32)


def swap(value, axis, mask):
    return lax.ppermute(value, axis, [(i, i ^ mask) for i in range(lax.axis_size(axis))])


def exchange(chunks, masks):
    return [chunks[0]] + [swap(chunk, "ep", mask) for chunk, mask in zip(chunks[1:], masks[1:])]


def swap_by_core(value, masks):
    count = lax.axis_size("dp")
    pairs = [(r * count + i, r * count + (i ^ mask)) for r, mask in enumerate(masks) for i in range(count)]
    return lax.ppermute(value, ("rep", "dp"), pairs)


def kernel_call(body, inputs, outputs, flops=0, **kwargs):
    whole = pl.BlockSpec(memory_space=pltpu.VMEM)
    moved = sum(a.size * a.dtype.itemsize for a in inputs + outputs)
    return pl.pallas_call(
        body,
        out_shape=outputs,
        in_specs=kwargs.pop("in_specs", [whole] * len(inputs)),
        out_specs=[whole] * len(outputs),
        cost_estimate=pl.CostEstimate(flops=flops, bytes_accessed=moved, transcendentals=0),
        compiler_params=pltpu.CompilerParams(vmem_limit_bytes=VMEM_BYTES),
        **kwargs,
    )(*inputs)


def iota(shape, dim):
    return lax.broadcasted_iota(jnp.int32, shape, dim)


def dispatch_kernel(experts, cap, chunk_count, *refs):
    small, (gate, up, down), refs = refs[:4], refs[4:7], refs[7:]
    chunks, (slot_out, *held, sems) = refs[:chunk_count], refs[chunk_count:]
    packed, held = held[:2], held[2:]
    hidden = packed[0].shape[0] // 3
    rep = lax.axis_index("rep")
    loads = [pltpu.make_async_copy(*pair, sems.at[i]) for i, pair in enumerate(zip(small, held))]
    packs = []
    for j, half in enumerate((rep, 1 - rep)):
        rows = pl.ds(pl.multiple_of(half * hidden, hidden), hidden)
        packs += [
            pltpu.make_async_copy(weight.at[0, rows], packed[j].at[pl.ds(i * hidden, hidden)], sems.at[4 + 3 * j + i])
            for i, weight in enumerate((gate, up, down))
        ]
    for copy in loads + packs:
        copy.start()
    for copy in loads:
        copy.wait()

    tokens, upstream, ids, route_weight = held
    top, tok_dev = ids.shape
    rows = experts * cap // chunk_count
    me = lax.axis_index("ep")
    expert_of_row = iota((experts, tok_dev), 0)
    named = [(expert_of_row == ids[k : k + 1, :]).astype(f32) for k in range(top)]
    earlier = (iota((tok_dev, tok_dev), 0) < iota((tok_dev, tok_dev), 1)).astype(bf16)
    before = dot(sum(named).astype(bf16), earlier, (1, 0))
    row = iota((2 * experts * cap, tok_dev), 0)
    take_x = jnp.zeros(row.shape, f32)
    take_dy = jnp.zeros(row.shape, f32)
    scale = jnp.zeros(row.shape, f32)
    for k in range(top):
        rank = jnp.sum(before * named[k], axis=0, keepdims=True).astype(jnp.int32)
        expert = ids[k : k + 1, :]
        if chunk_count > 1:
            mask = expert ^ me
            chunk = jnp.where(mask < 2, mask, experts + 1 - mask)
            slot = chunk * cap + rank
            x_row = slot + chunk * cap
        else:
            slot = expert * cap + rank
            x_row = slot
        slot_out[k : k + 1, :] = slot
        here_x = (row == x_row).astype(f32)
        here_dy = (row == x_row + rows).astype(f32)
        take_x += here_x
        take_dy += here_dy
        scale += here_x + here_dy * route_weight[k : k + 1, :].astype(f32)
    picked = dot(take_x.astype(bf16), tokens[...], (1, 0)) + dot(take_dy.astype(bf16), upstream[...], (1, 0))
    picked = picked * jnp.sum(scale, axis=1, keepdims=True)
    for c in range(chunk_count):
        chunks[c][...] = picked[2 * rows * c : 2 * rows * (c + 1)].astype(bf16)
    for copy in packs:
        copy.wait()


def expert_math(x_rows, d_rows, pieces):
    acts, mixed = [], []
    prob = 0.0
    for piece in pieces:
        hidden = piece.shape[0] // 3
        pre = dot(x_rows, piece[: 2 * hidden], (1, 1))
        d_act = dot(d_rows, piece[2 * hidden :], (1, 1))
        gate_pre, up_pre = pre[:, :hidden], pre[:, hidden:]
        sig = jax.nn.sigmoid(gate_pre)
        silu = gate_pre * sig
        act = silu * up_pre
        prob = prob + jnp.sum(act * d_act, axis=1, keepdims=True)
        acts.append(act)
        mixed += [d_act * up_pre * sig * (1.0 + gate_pre * (1.0 - sig)), d_act * silu]
    mixed = jnp.concatenate(mixed, axis=1).astype(bf16)
    acts = jnp.concatenate(acts, axis=1).astype(bf16)
    gates = jnp.concatenate([piece[: 2 * hidden] for piece in pieces])
    return dot(mixed, gates, (1, 0)), prob, dot(acts, d_rows, (0, 0))


def early_kernel(chunk_count, *refs):
    chunks, (*pieces, x_out, d_out, dx_out, grad_own, grad_near) = refs[:chunk_count], refs[chunk_count:]
    rows = chunks[0].shape[0] // 2
    values = [c[...].astype(f32) for c in chunks]
    x_out[...] = jnp.concatenate([v[:rows] for v in values]).astype(bf16)
    d_out[...] = jnp.concatenate([v[rows:] for v in values]).astype(bf16)
    dx, prob, grad = expert_math(x_out[...], d_out[...], pieces)
    width, hidden = dx.shape[1], grad_own.shape[0]
    dx_out[:, :width] = dx
    dx_out[:, width:] = jnp.broadcast_to(prob, (prob.shape[0], LANES))
    grad_own[...] = grad[:hidden]
    grad_near[...] = grad[hidden:].astype(bf16)


def late_kernel(x_ref, d_ref, dx_ref, far, keep, give, grad_far):
    dx, prob, grad = expert_math(x_ref[...], d_ref[...], [far])
    width, slots = dx.shape[1], keep.shape[0]
    for side, value in ((slice(0, width), dx), (slice(width, None), jnp.broadcast_to(prob, (prob.shape[0], LANES)))):
        total = value + dx_ref[:, side]
        keep[:, side] = total[:slots]
        give[:, side] = total[slots:].astype(bf16)
    grad_far[...] = grad.astype(bf16)


def grad_kernel(own, near, far, out):
    hidden = own.shape[0]
    out[:hidden] = (own[...] + near[:hidden].astype(f32) + far[...].astype(f32)).astype(bf16)
    out[hidden:] = near[hidden:]


def total_kernel(mine, theirs, out):
    hidden = mine.shape[0] // 2
    rep = lax.axis_index("rep")
    for i, half in enumerate((rep, 1 - rep)):
        here, there = slice(i * hidden, (i + 1) * hidden), slice((1 - i) * hidden, (2 - i) * hidden)
        rows = pl.ds(pl.multiple_of(half * hidden, hidden), hidden)
        out[0, rows] = mine[here].astype(f32) + theirs[there].astype(f32)


def add_kernel(keep, got, *chunks):
    rows = chunks[0].shape[0]
    total = keep[...] + got[...].astype(f32)
    for c, chunk in enumerate(chunks):
        chunk[...] = total[c * rows : (c + 1) * rows].astype(bf16)


def combine_kernel(chunk_count, *refs):
    chunks, (slot, route_weight, tokens_out, probs_out) = refs[:chunk_count], refs[chunk_count:]
    rows = chunks[0].shape[0]
    tok_dev, width = tokens_out.shape
    top = slot.shape[0]
    total = 0.0
    probs = [0.0] * top
    places = [0, *range(2, chunk_count), 1][:chunk_count]
    for c, place in enumerate(places):
        slot_of_row = iota((rows, tok_dev), 0) + place * rows
        hits = [(slot_of_row == slot[k : k + 1, :]).astype(f32) for k in range(top)]
        total = total + dot(sum(hits).astype(bf16), chunks[c][:, :width], (0, 0))
        prob = chunks[c][:, width : width + 1].astype(f32)
        for k in range(top):
            probs[k] = probs[k] + jnp.sum(hits[k] * prob, axis=0, keepdims=True)
    tokens_out[...] = total.astype(bf16)
    for k in range(top):
        probs_out[k : k + 1, :] = (probs[k] / route_weight[k : k + 1, :].astype(f32)).astype(bf16)


def local(tokens, upstream, expert_ids, route_weight, gate_weight, up_weight, down_weight):
    tok_dev, width = tokens.shape
    top = expert_ids.shape[1]
    experts, reps = lax.axis_size("ep"), lax.axis_size("rep")
    cap = 2 * ((5 * tok_dev * top + 8 * experts - 1) // (8 * experts))
    slots = experts * cap
    chunk_count = experts if experts <= 8 else 1
    rows = slots // chunk_count
    masks = [0, 1, *range(experts - 1, 1, -1)]
    hidden = gate_weight.shape[1] // reps
    shape = jax.ShapeDtypeStruct
    in_hbm = pl.BlockSpec(memory_space=pltpu.HBM)

    small = [tokens, upstream, expert_ids.T, route_weight.T]
    *chunks, slot, first, second = kernel_call(
        functools.partial(dispatch_kernel, experts, cap, chunk_count),
        [pltpu.with_memory_space_constraint(a, pltpu.HBM) for a in small + [gate_weight, up_weight, down_weight]],
        [shape((2 * rows, width), bf16)] * chunk_count
        + [shape((top, tok_dev), jnp.int32)]
        + [shape((3 * hidden, width), bf16)] * 2,
        in_specs=[in_hbm] * 7,
        scratch_shapes=[pltpu.VMEM(a.shape, a.dtype) for a in small] + [pltpu.SemaphoreType.DMA((10,))],
    )

    along, across = (1, 2), (2, 1)
    near = [swap_by_core(first, along), swap_by_core(second, along)]
    far = swap_by_core(near[0], across)

    if chunk_count > 1:
        chunks = exchange(chunks, masks)
    else:
        moved = chunks[0].reshape(2, experts, cap, width)
        moved = lax.all_to_all(moved, "ep", split_axis=1, concat_axis=1, tiled=True)
        chunks = [moved.reshape(2 * rows, width)]
    chunks = chunks + [swap(c, "rep", 1) for c in chunks]

    wide = width + LANES
    x_rows, d_rows, dx, grad_own, grad_near = kernel_call(
        functools.partial(early_kernel, 2 * chunk_count),
        chunks + [first, *near],
        [shape((2 * slots, width), bf16)] * 2
        + [shape((2 * slots, wide), f32), shape((hidden, width), f32), shape((2 * hidden, width), bf16)],
        flops=4 * 10**9,
    )
    keep, give, grad_far = kernel_call(
        late_kernel,
        [x_rows, d_rows, dx, far],
        [shape((slots, wide), f32), shape((slots, wide), bf16), shape((hidden, width), bf16)],
    )
    back = kernel_call(add_kernel, [keep, swap(give, "rep", 1)], [shape((rows, wide), bf16)] * chunk_count)
    if chunk_count > 1:
        back = exchange(back, masks)
        back = [back[0], *back[2:], back[1]]
    else:
        moved = back[0].reshape(experts, cap, wide)
        moved = lax.all_to_all(moved, "ep", split_axis=0, concat_axis=0, tiled=True)
        back = [moved.reshape(rows, wide)]
    d_tokens, d_probs = kernel_call(
        functools.partial(combine_kernel, chunk_count),
        back + [slot, route_weight.T],
        [shape((tok_dev, width), bf16), shape((top, tok_dev), bf16)],
        flops=8 * 10**9,
    )

    arrived = swap_by_core(grad_near, along), swap_by_core(grad_far, (3, 3))
    (mine,) = kernel_call(grad_kernel, [grad_own, *arrived], [shape((2 * hidden, width), bf16)])
    (grad_total,) = kernel_call(
        total_kernel, [mine, swap(mine, "rep", 1)], [shape((1, 2 * hidden, width), f32)]
    )
    return d_tokens, d_probs.T, grad_total


def solution(mesh):
    rows = P(("rep", "ep", "dp"), None)
    weights = P("ep", "dp", None)
    return jax.shard_map(
        local,
        mesh=mesh,
        in_specs=(rows,) * 4 + (weights,) * 3,
        out_specs=(rows, rows, weights),
        check_vma=False,
    )
```

```python
import functools

import jax
import jax.numpy as jnp
from jax import lax
from jax.experimental import pallas as pl
from jax.experimental.pallas import tpu as pltpu
from jax.sharding import PartitionSpec as P

LANES = 128
VMEM_BYTES = 32 * 1024 * 1024
f32, bf16 = jnp.float32, jnp.bfloat16


def dot(left, right, contract):
    return lax.dot_general(left, right, ((contract[0:1], contract[1:2]), ((), ())), preferred_element_type=f32)


def swap(value, axis, mask):
    return lax.ppermute(value, axis, [(i, i ^ mask) for i in range(lax.axis_size(axis))])


def exchange(chunks, masks):
    return [chunks[0]] + [swap(chunk, "ep", mask) for chunk, mask in zip(chunks[1:], masks[1:])]


def swap_by_core(value, masks):
    count = lax.axis_size("dp")
    pairs = [(r * count + i, r * count + (i ^ mask)) for r, mask in enumerate(masks) for i in range(count)]
    return lax.ppermute(value, ("rep", "dp"), pairs)


def kernel_call(body, inputs, outputs, flops=0, **kwargs):
    whole = pl.BlockSpec(memory_space=pltpu.VMEM)
    moved = sum(a.size * a.dtype.itemsize for a in inputs + outputs)
    return pl.pallas_call(
        body,
        out_shape=outputs,
        in_specs=kwargs.pop("in_specs", [whole] * len(inputs)),
        out_specs=[whole] * len(outputs),
        cost_estimate=pl.CostEstimate(flops=flops, bytes_accessed=moved, transcendentals=0),
        compiler_params=pltpu.CompilerParams(vmem_limit_bytes=VMEM_BYTES),
        **kwargs,
    )(*inputs)


def iota(shape, dim):
    return lax.broadcasted_iota(jnp.int32, shape, dim)


def pack_kernel(gate, up, down, first, second, sems):
    hidden = first.shape[0] // 3
    rep = lax.axis_index("rep")
    copies = []
    for j, (half, packed) in enumerate(((rep, first), (1 - rep, second))):
        rows = pl.ds(pl.multiple_of(half * hidden, hidden), hidden)
        copies += [
            pltpu.make_async_copy(weight.at[0, rows], packed.at[pl.ds(i * hidden, hidden)], sems.at[3 * j + i])
            for i, weight in enumerate((gate, up, down))
        ]
    for copy in copies:
        copy.start()
    for copy in copies:
        copy.wait()


def dispatch_kernel(experts, cap, chunk_count, *refs):
    given, refs = refs[:4], refs[4:]
    chunks, (slot_out, ids, route_weight, tokens, upstream, sems) = refs[:chunk_count], refs[chunk_count:]
    held = (ids, route_weight, tokens, upstream)
    loads = [pltpu.make_async_copy(*pair, sems.at[i]) for i, pair in enumerate(zip(given, held))]
    for copy in loads:
        copy.start()
    for copy in loads[:2]:
        copy.wait()

    top, tok_dev = ids.shape
    rows = experts * cap // chunk_count
    me = lax.axis_index("ep")
    expert_of_row = iota((experts, tok_dev), 0)
    named = [(expert_of_row == ids[k : k + 1, :]).astype(f32) for k in range(top)]
    earlier = (iota((tok_dev, tok_dev), 0) < iota((tok_dev, tok_dev), 1)).astype(bf16)
    before = dot(sum(named).astype(bf16), earlier, (1, 0))
    row = iota((2 * experts * cap, tok_dev), 0)
    take_x = jnp.zeros(row.shape, f32)
    take_dy = jnp.zeros(row.shape, f32)
    scale = jnp.zeros(row.shape, f32)
    for k in range(top):
        rank = jnp.sum(before * named[k], axis=0, keepdims=True).astype(jnp.int32)
        expert = ids[k : k + 1, :]
        if chunk_count > 1:
            mask = expert ^ me
            chunk = jnp.where(mask < 2, mask, experts + 1 - mask)
            slot = chunk * cap + rank
            x_row = slot + chunk * cap
        else:
            slot = expert * cap + rank
            x_row = slot
        slot_out[k : k + 1, :] = slot
        here_x = (row == x_row).astype(f32)
        here_dy = (row == x_row + rows).astype(f32)
        take_x += here_x
        take_dy += here_dy
        scale += here_x + here_dy * route_weight[k : k + 1, :].astype(f32)
    scale = jnp.sum(scale, axis=1, keepdims=True)
    take_x, take_dy = take_x.astype(bf16), take_dy.astype(bf16)
    for copy in loads[2:]:
        copy.wait()
    picked = dot(take_x, tokens[...], (1, 0)) + dot(take_dy, upstream[...], (1, 0))
    picked = picked * scale
    for c in range(chunk_count):
        chunks[c][...] = picked[2 * rows * c : 2 * rows * (c + 1)].astype(bf16)


def expert_math(x_rows, d_rows, pieces):
    hidden = pieces[0].shape[0] // 3
    gate, up, down = [[piece[i * hidden : (i + 1) * hidden] for piece in pieces] for i in range(3)]
    mixers = jnp.concatenate(gate + up)
    pre = dot(x_rows, mixers, (1, 1))
    d_act = dot(d_rows, jnp.concatenate(down), (1, 1))
    gate_pre, up_pre = pre[:, : hidden * len(pieces)], pre[:, hidden * len(pieces) :]
    sig = jax.nn.sigmoid(gate_pre)
    silu = gate_pre * sig
    act = silu * up_pre
    prob = jnp.sum(act * d_act, axis=1, keepdims=True)
    d_gate = d_act * up_pre * sig * (1.0 + gate_pre * (1.0 - sig))
    d_pre = jnp.concatenate([d_gate, d_act * silu], axis=1).astype(bf16)
    return dot(d_pre, mixers, (1, 0)), prob, dot(act.astype(bf16), d_rows, (0, 0))


def join_kernel(one, two, out):
    out[...] = jnp.concatenate([one[...].astype(f32), two[...].astype(f32)]).astype(bf16)


def early_kernel(chunk_count, *refs):
    chunks, (*pieces, x_out, d_out, dx_out, grad_own, grad_near) = refs[:chunk_count], refs[chunk_count:]
    rows = chunks[0].shape[0] // 2
    values = [c[i : i + 2 * rows] for c in [c[...].astype(f32) for c in chunks] for i in range(0, c.shape[0], 2 * rows)]
    x_out[...] = jnp.concatenate([v[:rows] for v in values]).astype(bf16)
    d_out[...] = jnp.concatenate([v[rows:] for v in values]).astype(bf16)
    dx, prob, grad = expert_math(x_out[...], d_out[...], pieces)
    width, hidden = dx.shape[1], grad_own.shape[0]
    dx_out[:, :width] = dx
    dx_out[:, width:] = jnp.broadcast_to(prob, (prob.shape[0], LANES))
    grad_own[...] = grad[:hidden]
    grad_near[...] = grad[hidden:].astype(bf16)


def late_kernel(x_ref, d_ref, dx_ref, far, keep, give, grad_far):
    dx, prob, grad = expert_math(x_ref[...], d_ref[...], [far])
    width, slots = dx.shape[1], keep.shape[0]
    for side, value in ((slice(0, width), dx), (slice(width, None), jnp.broadcast_to(prob, (prob.shape[0], LANES)))):
        total = value + dx_ref[:, side]
        keep[:, side] = total[:slots]
        give[:, side] = total[slots:].astype(bf16)
    grad_far[...] = grad.astype(bf16)


def grad_kernel(own, near, far, out):
    hidden = own.shape[0]
    out[:hidden] = (own[...] + near[:hidden].astype(f32) + far[...].astype(f32)).astype(bf16)
    out[hidden:] = near[hidden:]


def total_kernel(mine, theirs, out):
    hidden = mine.shape[0] // 2
    rep = lax.axis_index("rep")
    for i, half in enumerate((rep, 1 - rep)):
        here, there = slice(i * hidden, (i + 1) * hidden), slice((1 - i) * hidden, (2 - i) * hidden)
        rows = pl.ds(pl.multiple_of(half * hidden, hidden), hidden)
        out[0, rows] = mine[here].astype(f32) + theirs[there].astype(f32)


def add_kernel(keep, got, *chunks):
    rows = chunks[0].shape[0]
    total = keep[...] + got[...].astype(f32)
    for c, chunk in enumerate(chunks):
        chunk[...] = total[c * rows : (c + 1) * rows].astype(bf16)


def combine_kernel(chunk_count, *refs):
    chunks, (slot, route_weight, tokens_out, probs_out) = refs[:chunk_count], refs[chunk_count:]
    rows = chunks[0].shape[0]
    tok_dev, width = tokens_out.shape
    top = slot.shape[0]
    total = 0.0
    probs = [0.0] * top
    places = [0, *range(2, chunk_count), 1][:chunk_count]
    for c, place in enumerate(places):
        slot_of_row = iota((rows, tok_dev), 0) + place * rows
        hits = [(slot_of_row == slot[k : k + 1, :]).astype(f32) for k in range(top)]
        total = total + dot(sum(hits).astype(bf16), chunks[c][:, :width], (0, 0))
        prob = chunks[c][:, width : width + 1].astype(f32)
        for k in range(top):
            probs[k] = probs[k] + jnp.sum(hits[k] * prob, axis=0, keepdims=True)
    tokens_out[...] = total.astype(bf16)
    for k in range(top):
        probs_out[k : k + 1, :] = (probs[k] / route_weight[k : k + 1, :].astype(f32)).astype(bf16)


def local(tokens, upstream, expert_ids, route_weight, gate_weight, up_weight, down_weight):
    tok_dev, width = tokens.shape
    top = expert_ids.shape[1]
    experts, reps = lax.axis_size("ep"), lax.axis_size("rep")
    cap = 2 * ((5 * tok_dev * top + 8 * experts - 1) // (8 * experts))
    slots = experts * cap
    chunk_count = experts if experts <= 8 else 1
    rows = slots // chunk_count
    masks = [0, 1, *range(experts - 1, 1, -1)]
    hidden = gate_weight.shape[1] // reps
    shape = jax.ShapeDtypeStruct
    in_hbm = pl.BlockSpec(memory_space=pltpu.HBM)

    first, second = kernel_call(
        pack_kernel,
        [pltpu.with_memory_space_constraint(a, pltpu.HBM) for a in (gate_weight, up_weight, down_weight)],
        [shape((3 * hidden, width), bf16)] * 2,
        in_specs=[in_hbm] * 3,
        scratch_shapes=[pltpu.SemaphoreType.DMA((6,))],
    )
    given = [expert_ids.T, route_weight.T, tokens, upstream]
    *chunks, slot = kernel_call(
        functools.partial(dispatch_kernel, experts, cap, chunk_count),
        [pltpu.with_memory_space_constraint(a, pltpu.HBM) for a in given],
        [shape((2 * rows, width), bf16)] * chunk_count + [shape((top, tok_dev), jnp.int32)],
        in_specs=[in_hbm] * 4,
        scratch_shapes=[pltpu.VMEM(a.shape, a.dtype) for a in given] + [pltpu.SemaphoreType.DMA((4,))],
    )

    along, across = (1, 2), (2, 1)
    near = [swap_by_core(first, along), swap_by_core(second, along)]
    far = swap_by_core(near[0], across)

    if chunk_count > 1:
        chunks = exchange(chunks, masks)
    else:
        moved = chunks[0].reshape(2, experts, cap, width)
        moved = lax.all_to_all(moved, "ep", split_axis=1, concat_axis=1, tiled=True)
        chunks = [moved.reshape(2 * rows, width)]
    early = chunks[:2]
    if len(early) > 1:
        early = kernel_call(join_kernel, early, [shape((4 * rows, width), bf16)])
    chunks = chunks + [swap(c, "rep", 1) for c in [*early, *chunks[2:]]]

    wide = width + LANES
    x_rows, d_rows, dx, grad_own, grad_near = kernel_call(
        functools.partial(early_kernel, len(chunks)),
        chunks + [first, *near],
        [shape((2 * slots, width), bf16)] * 2
        + [shape((2 * slots, wide), f32), shape((hidden, width), f32), shape((2 * hidden, width), bf16)],
        flops=4 * 10**9,
    )
    keep, give, grad_far = kernel_call(
        late_kernel,
        [x_rows, d_rows, dx, far],
        [shape((slots, wide), f32), shape((slots, wide), bf16), shape((hidden, width), bf16)],
    )
    back = kernel_call(add_kernel, [keep, swap(give, "rep", 1)], [shape((rows, wide), bf16)] * chunk_count)
    if chunk_count > 1:
        back = exchange(back, masks)
        back = [back[0], *back[2:], back[1]]
    else:
        moved = back[0].reshape(experts, cap, wide)
        moved = lax.all_to_all(moved, "ep", split_axis=0, concat_axis=0, tiled=True)
        back = [moved.reshape(rows, wide)]
    d_tokens, d_probs = kernel_call(
        functools.partial(combine_kernel, chunk_count),
        back + [slot, route_weight.T],
        [shape((tok_dev, width), bf16), shape((top, tok_dev), bf16)],
        flops=8 * 10**9,
    )

    arrived = swap_by_core(grad_near, along), swap_by_core(grad_far, (3, 3))
    (mine,) = kernel_call(grad_kernel, [grad_own, *arrived], [shape((2 * hidden, width), bf16)])
    (grad_total,) = kernel_call(
        total_kernel, [mine, swap(mine, "rep", 1)], [shape((1, 2 * hidden, width), f32)]
    )
    return d_tokens, d_probs.T, grad_total


def solution(mesh):
    rows = P(("rep", "ep", "dp"), None)
    weights = P("ep", "dp", None)
    return jax.shard_map(
        local,
        mesh=mesh,
        in_specs=(rows,) * 4 + (weights,) * 3,
        out_specs=(rows, rows, weights),
        check_vma=False,
    )
```

```python
import functools

import jax
import jax.numpy as jnp
from jax import lax
from jax.experimental import pallas as pl
from jax.experimental.pallas import tpu as pltpu
from jax.sharding import PartitionSpec as P

LANES = 128
VMEM_BYTES = 32 * 1024 * 1024
f32, bf16 = jnp.float32, jnp.bfloat16


def dot(left, right, contract):
    return lax.dot_general(left, right, ((contract[0:1], contract[1:2]), ((), ())), preferred_element_type=f32)


def swap(value, axis, mask):
    return lax.ppermute(value, axis, [(i, i ^ mask) for i in range(lax.axis_size(axis))])


def exchange(chunks, masks):
    return [chunks[0]] + [swap(chunk, "ep", mask) for chunk, mask in zip(chunks[1:], masks[1:])]


def swap_by_core(value, masks):
    count = lax.axis_size("dp")
    pairs = [(r * count + i, r * count + (i ^ mask)) for r, mask in enumerate(masks) for i in range(count)]
    return lax.ppermute(value, ("rep", "dp"), pairs)


def kernel_call(body, inputs, outputs, flops=0, **kwargs):
    whole = pl.BlockSpec(memory_space=pltpu.VMEM)
    moved = sum(a.size * a.dtype.itemsize for a in inputs + outputs)
    return pl.pallas_call(
        body,
        out_shape=outputs,
        in_specs=kwargs.pop("in_specs", [whole] * len(inputs)),
        out_specs=[whole] * len(outputs),
        cost_estimate=pl.CostEstimate(flops=flops, bytes_accessed=moved, transcendentals=0),
        compiler_params=pltpu.CompilerParams(vmem_limit_bytes=VMEM_BYTES),
        **kwargs,
    )(*inputs)


def iota(shape, dim):
    return lax.broadcasted_iota(jnp.int32, shape, dim)


def dispatch_kernel(experts, cap, chunk_count, *refs):
    given, weights, refs = refs[:4], refs[4:7], refs[7:]
    chunks, (slot_out, *packed), (*held, sems) = refs[:chunk_count], refs[chunk_count:-5], refs[-5:]
    hidden = packed[0].shape[0] // 3
    rep = lax.axis_index("rep")
    loads = [pltpu.make_async_copy(*pair, sems.at[i]) for i, pair in enumerate(zip(given, held))]
    packs = []
    for j, half in enumerate((rep, 1 - rep)):
        rows = pl.ds(pl.multiple_of(half * hidden, hidden), hidden)
        packs += [
            pltpu.make_async_copy(weight.at[0, rows], packed[j].at[pl.ds(i * hidden, hidden)], sems.at[4 + 3 * j + i])
            for i, weight in enumerate(weights)
        ]
    for copy in loads + packs:
        copy.start()
    for copy in loads[:2]:
        copy.wait()

    ids, route_weight, tokens, upstream = held
    top, tok_dev = ids.shape
    rows = experts * cap // chunk_count
    me = lax.axis_index("ep")
    expert_of_row = iota((experts, tok_dev), 0)
    named = [(expert_of_row == ids[k : k + 1, :]).astype(f32) for k in range(top)]
    earlier = (iota((tok_dev, tok_dev), 0) < iota((tok_dev, tok_dev), 1)).astype(bf16)
    before = dot(sum(named).astype(bf16), earlier, (1, 0))
    row = iota((2 * experts * cap, tok_dev), 0)
    take_x = jnp.zeros(row.shape, f32)
    take_dy = jnp.zeros(row.shape, f32)
    scale = jnp.zeros(row.shape, f32)
    for k in range(top):
        rank = jnp.sum(before * named[k], axis=0, keepdims=True).astype(jnp.int32)
        expert = ids[k : k + 1, :]
        if chunk_count > 1:
            mask = expert ^ me
            chunk = jnp.where(mask == 0, 0, experts - mask)
            slot = chunk * cap + rank
            x_row = slot + chunk * cap
        else:
            slot = expert * cap + rank
            x_row = slot
        slot_out[k : k + 1, :] = slot
        here_x = (row == x_row).astype(f32)
        here_dy = (row == x_row + rows).astype(f32)
        take_x += here_x
        take_dy += here_dy
        scale += here_x + here_dy * route_weight[k : k + 1, :].astype(f32)
    scale = jnp.sum(scale, axis=1, keepdims=True)
    take_x, take_dy = take_x.astype(bf16), take_dy.astype(bf16)
    for copy in loads[2:]:
        copy.wait()
    picked = dot(take_x, tokens[...], (1, 0)) + dot(take_dy, upstream[...], (1, 0))
    picked = picked * scale
    for c in range(chunk_count):
        chunks[c][...] = picked[2 * rows * c : 2 * rows * (c + 1)].astype(bf16)
    for copy in packs:
        copy.wait()


def expert_math(x_rows, d_rows, pieces):
    hidden = pieces[0].shape[0] // 3
    gate, up, down = [[piece[i * hidden : (i + 1) * hidden] for piece in pieces] for i in range(3)]
    mixers = jnp.concatenate(gate + up)
    pre = dot(x_rows, mixers, (1, 1))
    d_act = dot(d_rows, jnp.concatenate(down), (1, 1))
    gate_pre, up_pre = pre[:, : hidden * len(pieces)], pre[:, hidden * len(pieces) :]
    sig = jax.nn.sigmoid(gate_pre)
    silu = gate_pre * sig
    act = silu * up_pre
    prob = jnp.sum(act * d_act, axis=1, keepdims=True)
    d_gate = d_act * up_pre * sig * (1.0 + gate_pre * (1.0 - sig))
    d_pre = jnp.concatenate([d_gate, d_act * silu], axis=1).astype(bf16)
    return dot(d_pre, mixers, (1, 0)), prob, dot(act.astype(bf16), d_rows, (0, 0))


def gather_kernel(*refs):
    *chunks, x_out, d_out = refs
    rows = chunks[0].shape[0] // 2
    values = [c[...].astype(f32) for c in chunks]
    x_out[...] = jnp.concatenate([v[:rows] for v in values]).astype(bf16)
    d_out[...] = jnp.concatenate([v[rows:] for v in values]).astype(bf16)


def both_cores(x_own, d_own, x_other, d_other):
    return [jnp.concatenate([a[...], b[...]]) for a, b in ((x_own, x_other), (d_own, d_other))]


def early_kernel(*refs):
    *pieces, dx_out, grad_own, grad_near = refs[4:]
    dx, prob, grad = expert_math(*both_cores(*refs[:4]), pieces)
    width, hidden = dx.shape[1], grad_own.shape[0]
    dx_out[:, :width] = dx
    dx_out[:, width:] = jnp.broadcast_to(prob, (prob.shape[0], LANES))
    grad_own[...] = grad[:hidden]
    grad_near[...] = grad[hidden:].astype(bf16)


def late_kernel(*refs):
    dx_ref, far, keep, give, grad_far = refs[4:]
    dx, prob, grad = expert_math(*both_cores(*refs[:4]), [far])
    width, slots = dx.shape[1], keep.shape[0]
    for side, value in ((slice(0, width), dx), (slice(width, None), jnp.broadcast_to(prob, (prob.shape[0], LANES)))):
        total = value + dx_ref[:, side]
        keep[:, side] = total[:slots]
        give[:, side] = total[slots:].astype(bf16)
    grad_far[...] = grad.astype(bf16)


def grad_kernel(own, near, far, out):
    hidden = own.shape[0]
    out[:hidden] = (own[...] + near[:hidden].astype(f32) + far[...].astype(f32)).astype(bf16)
    out[hidden:] = near[hidden:]


def total_kernel(mine, theirs, out):
    hidden = mine.shape[0] // 2
    rep = lax.axis_index("rep")
    for i, half in enumerate((rep, 1 - rep)):
        here, there = slice(i * hidden, (i + 1) * hidden), slice((1 - i) * hidden, (2 - i) * hidden)
        rows = pl.ds(pl.multiple_of(half * hidden, hidden), hidden)
        out[0, rows] = mine[here].astype(f32) + theirs[there].astype(f32)


def add_kernel(places, keep, got, *chunks):
    rows = chunks[0].shape[0]
    total = keep[...] + got[...].astype(f32)
    for place, chunk in zip(places, chunks):
        chunk[...] = total[place * rows : (place + 1) * rows].astype(bf16)


def combine_kernel(places, *refs):
    chunks, (slot, route_weight, tokens_out, probs_out) = refs[: len(places)], refs[len(places) :]
    rows = chunks[0].shape[0]
    tok_dev, width = tokens_out.shape
    top = slot.shape[0]
    total = 0.0
    probs = [0.0] * top
    for c, place in enumerate(places):
        slot_of_row = iota((rows, tok_dev), 0) + place * rows
        hits = [(slot_of_row == slot[k : k + 1, :]).astype(f32) for k in range(top)]
        total = total + dot(sum(hits).astype(bf16), chunks[c][:, :width], (0, 0))
        prob = chunks[c][:, width : width + 1].astype(f32)
        for k in range(top):
            probs[k] = probs[k] + jnp.sum(hits[k] * prob, axis=0, keepdims=True)
    tokens_out[...] = total.astype(bf16)
    for k in range(top):
        probs_out[k : k + 1, :] = (probs[k] / route_weight[k : k + 1, :].astype(f32)).astype(bf16)


def local(tokens, upstream, expert_ids, route_weight, gate_weight, up_weight, down_weight):
    tok_dev, width = tokens.shape
    top = expert_ids.shape[1]
    experts, reps = lax.axis_size("ep"), lax.axis_size("rep")
    cap = 2 * ((5 * tok_dev * top + 8 * experts - 1) // (8 * experts))
    slots = experts * cap
    chunk_count = experts if experts <= 8 else 1
    rows = slots // chunk_count
    masks = [0, *range(experts - 1, 0, -1)]
    hidden = gate_weight.shape[1] // reps
    shape = jax.ShapeDtypeStruct
    in_hbm = pl.BlockSpec(memory_space=pltpu.HBM)

    given = [expert_ids.T, route_weight.T, tokens, upstream]
    *chunks, slot, first, second = kernel_call(
        functools.partial(dispatch_kernel, experts, cap, chunk_count),
        [pltpu.with_memory_space_constraint(a, pltpu.HBM) for a in [*given, gate_weight, up_weight, down_weight]],
        [shape((2 * rows, width), bf16)] * chunk_count
        + [shape((top, tok_dev), jnp.int32)]
        + [shape((3 * hidden, width), bf16)] * 2,
        in_specs=[in_hbm] * 7,
        scratch_shapes=[pltpu.VMEM(a.shape, a.dtype) for a in given] + [pltpu.SemaphoreType.DMA((10,))],
    )

    along, across = (1, 2), (2, 1)
    near = [swap_by_core(first, along), swap_by_core(second, along)]
    far = swap_by_core(near[0], across)

    if chunk_count > 1:
        chunks = exchange(chunks, masks)
    else:
        moved = chunks[0].reshape(2, experts, cap, width)
        moved = lax.all_to_all(moved, "ep", split_axis=1, concat_axis=1, tiled=True)
        chunks = [moved.reshape(2 * rows, width)]
    own = kernel_call(gather_kernel, chunks, [shape((slots, width), bf16)] * 2, flops=2 * 10**9)
    other = [swap(part, "rep", 1) for part in own]

    wide = width + LANES
    dx, grad_own, grad_near = kernel_call(
        early_kernel,
        [*own, *other, first, *near],
        [shape((2 * slots, wide), f32), shape((hidden, width), f32), shape((2 * hidden, width), bf16)],
        flops=2 * 10**9,
    )
    keep, give, grad_far = kernel_call(
        late_kernel,
        [*own, *other, dx, far],
        [shape((slots, wide), f32), shape((slots, wide), bf16), shape((hidden, width), bf16)],
    )
    places = [0, chunk_count - 1, *range(1, chunk_count - 1)][:chunk_count]
    back = kernel_call(
        functools.partial(add_kernel, places),
        [keep, swap(give, "rep", 1)],
        [shape((rows, wide), bf16)] * chunk_count,
    )
    if chunk_count > 1:
        back = exchange(back, [masks[place] for place in places])
    else:
        moved = back[0].reshape(experts, cap, wide)
        moved = lax.all_to_all(moved, "ep", split_axis=0, concat_axis=0, tiled=True)
        back = [moved.reshape(rows, wide)]
    d_tokens, d_probs = kernel_call(
        functools.partial(combine_kernel, places),
        back + [slot, route_weight.T],
        [shape((tok_dev, width), bf16), shape((top, tok_dev), bf16)],
        flops=8 * 10**9,
    )

    arrived = swap_by_core(grad_near, along), swap_by_core(grad_far, (3, 3))
    (mine,) = kernel_call(grad_kernel, [grad_own, *arrived], [shape((2 * hidden, width), bf16)])
    (grad_total,) = kernel_call(
        total_kernel, [mine, swap(mine, "rep", 1)], [shape((1, 2 * hidden, width), f32)]
    )
    return d_tokens, d_probs.T, grad_total


def solution(mesh):
    rows = P(("rep", "ep", "dp"), None)
    weights = P("ep", "dp", None)
    return jax.shard_map(
        local,
        mesh=mesh,
        in_specs=(rows,) * 4 + (weights,) * 3,
        out_specs=(rows, rows, weights),
        check_vma=False,
    )
```

```python
import functools

import jax
import jax.numpy as jnp
from jax import lax
from jax.experimental import pallas as pl
from jax.experimental.pallas import tpu as pltpu
from jax.sharding import PartitionSpec as P

LANES = 128
VMEM_BYTES = 32 * 1024 * 1024
f32, bf16 = jnp.float32, jnp.bfloat16


def dot(left, right, contract):
    return lax.dot_general(left, right, ((contract[0:1], contract[1:2]), ((), ())), preferred_element_type=f32)


def swap(value, axis, mask):
    return lax.ppermute(value, axis, [(i, i ^ mask) for i in range(lax.axis_size(axis))])


def exchange(chunks):
    return chunks[:1] + [swap(chunks[c], "ep", c) for c in range(1, len(chunks))]


def swap_by_core(value, masks):
    count = lax.axis_size("dp")
    pairs = [(r * count + i, r * count + (i ^ mask)) for r, mask in enumerate(masks) for i in range(count)]
    return lax.ppermute(value, ("rep", "dp"), pairs)


def kernel_call(body, inputs, outputs, flops=0, **kwargs):
    whole = pl.BlockSpec(memory_space=pltpu.VMEM)
    moved = sum(a.size * a.dtype.itemsize for a in inputs + outputs)
    return pl.pallas_call(
        body,
        out_shape=outputs,
        in_specs=kwargs.pop("in_specs", [whole] * len(inputs)),
        out_specs=[whole] * len(outputs),
        cost_estimate=pl.CostEstimate(flops=flops, bytes_accessed=moved, transcendentals=0),
        compiler_params=pltpu.CompilerParams(vmem_limit_bytes=VMEM_BYTES),
        **kwargs,
    )(*inputs)


def iota(shape, dim):
    return lax.broadcasted_iota(jnp.int32, shape, dim)


def dispatch_kernel(experts, cap, chunk_count, *refs):
    given, weights, refs = refs[:4], refs[4:7], refs[7:]
    chunks, (slot_out, *packed), (*held, sems) = refs[:chunk_count], refs[chunk_count:-5], refs[-5:]
    hidden = packed[0].shape[0] // 3
    rep = lax.axis_index("rep")
    loads = [pltpu.make_async_copy(*pair, sems.at[i]) for i, pair in enumerate(zip(given, held))]
    packs = []
    for j, half in enumerate((rep, 1 - rep)):
        rows = pl.ds(pl.multiple_of(half * hidden, hidden), hidden)
        packs += [
            pltpu.make_async_copy(weight.at[0, rows], packed[j].at[pl.ds(i * hidden, hidden)], sems.at[4 + 3 * j + i])
            for i, weight in enumerate(weights)
        ]
    for copy in loads + packs:
        copy.start()
    for copy in loads[:2]:
        copy.wait()

    ids, route_weight, tokens, upstream = held
    top, tok_dev = ids.shape
    rows = experts * cap // chunk_count
    me = lax.axis_index("ep")
    expert_of_row = iota((experts, tok_dev), 0)
    named = [(expert_of_row == ids[k : k + 1, :]).astype(f32) for k in range(top)]
    earlier = (iota((tok_dev, tok_dev), 0) < iota((tok_dev, tok_dev), 1)).astype(bf16)
    before = dot(sum(named).astype(bf16), earlier, (1, 0))
    row = iota((2 * experts * cap, tok_dev), 0)
    take_x = jnp.zeros(row.shape, f32)
    take_dy = jnp.zeros(row.shape, f32)
    scale = jnp.zeros(row.shape, f32)
    for k in range(top):
        rank = jnp.sum(before * named[k], axis=0, keepdims=True).astype(jnp.int32)
        expert = ids[k : k + 1, :]
        if chunk_count > 1:
            chunk = expert ^ me
            slot = chunk * cap + rank
            x_row = slot + chunk * cap
        else:
            slot = expert * cap + rank
            x_row = slot
        slot_out[k : k + 1, :] = slot
        here_x = (row == x_row).astype(f32)
        here_dy = (row == x_row + rows).astype(f32)
        take_x += here_x
        take_dy += here_dy
        scale += here_x + here_dy * route_weight[k : k + 1, :].astype(f32)
    scale = jnp.sum(scale, axis=1, keepdims=True)
    take_x, take_dy = take_x.astype(bf16), take_dy.astype(bf16)
    for copy in loads[2:]:
        copy.wait()
    picked = dot(take_x, tokens[...], (1, 0)) + dot(take_dy, upstream[...], (1, 0))
    picked = picked * scale
    for c in range(chunk_count):
        chunks[c][...] = picked[2 * rows * c : 2 * rows * (c + 1)].astype(bf16)
    for copy in packs:
        copy.wait()


def expert_math(x_rows, d_rows, pieces):
    hidden = pieces[0].shape[0] // 3
    gate, up, down = [[piece[i * hidden : (i + 1) * hidden] for piece in pieces] for i in range(3)]
    mixers = jnp.concatenate(gate + up)
    pre = dot(x_rows, mixers, (1, 1))
    d_act = dot(d_rows, jnp.concatenate(down), (1, 1))
    gate_pre, up_pre = pre[:, : hidden * len(pieces)], pre[:, hidden * len(pieces) :]
    sig = jax.nn.sigmoid(gate_pre)
    silu = gate_pre * sig
    act = silu * up_pre
    prob = jnp.sum(act * d_act, axis=1, keepdims=True)
    d_gate = d_act * up_pre * sig * (1.0 + gate_pre * (1.0 - sig))
    d_pre = jnp.concatenate([d_gate, d_act * silu], axis=1).astype(bf16)
    return dot(d_pre, mixers, (1, 0)), prob, dot(act.astype(bf16), d_rows, (0, 0))


def gather_kernel(*refs):
    *chunks, x_out, d_out = refs
    rows = chunks[0].shape[0] // 2
    values = [c[...].astype(f32) for c in reversed(chunks)]
    x_out[...] = jnp.concatenate([v[:rows] for v in values]).astype(bf16)
    d_out[...] = jnp.concatenate([v[rows:] for v in values]).astype(bf16)


def both_cores(x_own, d_own, x_other, d_other):
    return [jnp.concatenate([a[...], b[...]]) for a, b in ((x_own, x_other), (d_own, d_other))]


def early_kernel(*refs):
    *pieces, dx_out, grad_own, grad_near = refs[4:]
    dx, prob, grad = expert_math(*both_cores(*refs[:4]), pieces)
    width, hidden = dx.shape[1], grad_own.shape[0]
    dx_out[:, :width] = dx
    dx_out[:, width:] = jnp.broadcast_to(prob, (prob.shape[0], LANES))
    grad_own[...] = grad[:hidden]
    grad_near[...] = grad[hidden:].astype(bf16)


def late_kernel(*refs):
    dx_ref, far, keep, *gives, grad_far = refs[4:]
    dx, prob, grad = expert_math(*both_cores(*refs[:4]), [far])
    width, slots = dx.shape[1], keep.shape[0]
    for side, value in ((slice(0, width), dx), (slice(width, None), jnp.broadcast_to(prob, (prob.shape[0], LANES)))):
        total = value + dx_ref[:, side]
        keep[:, side] = total[:slots]
        for i, give in enumerate(gives):
            rows = give.shape[0]
            give[:, side] = total[slots + rows * i : slots + rows * (i + 1)].astype(bf16)
    grad_far[...] = grad.astype(bf16)


def grad_kernel(own, near, far, out):
    hidden = own.shape[0]
    out[:hidden] = (own[...] + near[:hidden].astype(f32) + far[...].astype(f32)).astype(bf16)
    out[hidden:] = near[hidden:]


def total_kernel(mine, theirs, out):
    hidden = mine.shape[0] // 2
    rep = lax.axis_index("rep")
    for i, half in enumerate((rep, 1 - rep)):
        here, there = slice(i * hidden, (i + 1) * hidden), slice((1 - i) * hidden, (2 - i) * hidden)
        rows = pl.ds(pl.multiple_of(half * hidden, hidden), hidden)
        out[0, rows] = mine[here].astype(f32) + theirs[there].astype(f32)


def add_kernel(start, keep, got, *chunks):
    rows = chunks[0].shape[0]
    total = keep[start : start + got.shape[0]] + got[...].astype(f32)
    for c, chunk in enumerate(chunks):
        chunk[...] = total[c * rows : (c + 1) * rows].astype(bf16)


def combine_kernel(chunk_count, *refs):
    chunks, (slot, route_weight, tokens_out, probs_out) = refs[:chunk_count], refs[chunk_count:]
    rows = chunks[0].shape[0]
    tok_dev, width = tokens_out.shape
    top = slot.shape[0]
    total = 0.0
    probs = [0.0] * top
    for c in range(chunk_count):
        slot_of_row = iota((rows, tok_dev), 0) + c * rows
        hits = [(slot_of_row == slot[k : k + 1, :]).astype(f32) for k in range(top)]
        total = total + dot(sum(hits).astype(bf16), chunks[c][:, :width], (0, 0))
        prob = chunks[c][:, width : width + 1].astype(f32)
        for k in range(top):
            probs[k] = probs[k] + jnp.sum(hits[k] * prob, axis=0, keepdims=True)
    tokens_out[...] = total.astype(bf16)
    for k in range(top):
        probs_out[k : k + 1, :] = (probs[k] / route_weight[k : k + 1, :].astype(f32)).astype(bf16)


def local(tokens, upstream, expert_ids, route_weight, gate_weight, up_weight, down_weight):
    tok_dev, width = tokens.shape
    top = expert_ids.shape[1]
    experts, reps = lax.axis_size("ep"), lax.axis_size("rep")
    cap = 2 * ((5 * tok_dev * top + 8 * experts - 1) // (8 * experts))
    slots = experts * cap
    chunk_count = experts if experts <= 8 else 1
    rows = slots // chunk_count
    hidden = gate_weight.shape[1] // reps
    shape = jax.ShapeDtypeStruct
    in_hbm = pl.BlockSpec(memory_space=pltpu.HBM)

    given = [expert_ids.T, route_weight.T, tokens, upstream]
    *chunks, slot, first, second = kernel_call(
        functools.partial(dispatch_kernel, experts, cap, chunk_count),
        [pltpu.with_memory_space_constraint(a, pltpu.HBM) for a in [*given, gate_weight, up_weight, down_weight]],
        [shape((2 * rows, width), bf16)] * chunk_count
        + [shape((top, tok_dev), jnp.int32)]
        + [shape((3 * hidden, width), bf16)] * 2,
        in_specs=[in_hbm] * 7,
        scratch_shapes=[pltpu.VMEM(a.shape, a.dtype) for a in given] + [pltpu.SemaphoreType.DMA((10,))],
    )

    along, across = (1, 2), (2, 1)
    near = [swap_by_core(first, along), swap_by_core(second, along)]
    far = swap_by_core(near[0], across)

    if chunk_count > 1:
        chunks = exchange(chunks)
    else:
        moved = chunks[0].reshape(2, experts, cap, width)
        moved = lax.all_to_all(moved, "ep", split_axis=1, concat_axis=1, tiled=True)
        chunks = [moved.reshape(2 * rows, width)]
    own = kernel_call(gather_kernel, chunks[::-1], [shape((slots, width), bf16)] * 2, flops=2 * 10**9)
    other = [swap(part, "rep", 1) for part in own]

    wide = width + LANES
    dx, grad_own, grad_near = kernel_call(
        early_kernel,
        [*own, *other, first, *near],
        [shape((2 * slots, wide), f32), shape((hidden, width), f32), shape((2 * hidden, width), bf16)],
        flops=10**9,
    )
    parts = 2 if chunk_count % 2 == 0 else 1
    keep, *gives, grad_far = kernel_call(
        late_kernel,
        [*own, *other, dx, far],
        [shape((slots, wide), f32)]
        + [shape((slots // parts, wide), bf16)] * parts
        + [shape((hidden, width), bf16)],
    )
    back = []
    for i, give in enumerate(gives):
        back += kernel_call(
            functools.partial(add_kernel, i * slots // parts),
            [keep, swap(give, "rep", 1)],
            [shape((rows, wide), bf16)] * (chunk_count // parts),
        )
    if chunk_count > 1:
        back = exchange(back)
    else:
        moved = back[0].reshape(experts, cap, wide)
        moved = lax.all_to_all(moved, "ep", split_axis=0, concat_axis=0, tiled=True)
        back = [moved.reshape(rows, wide)]
    d_tokens, d_probs = kernel_call(
        functools.partial(combine_kernel, chunk_count),
        back + [slot, route_weight.T],
        [shape((tok_dev, width), bf16), shape((top, tok_dev), bf16)],
        flops=8 * 10**9,
    )

    arrived = swap_by_core(grad_near, along), swap_by_core(grad_far, (3, 3))
    (mine,) = kernel_call(grad_kernel, [grad_own, *arrived], [shape((2 * hidden, width), bf16)])
    (grad_total,) = kernel_call(
        total_kernel, [mine, swap(mine, "rep", 1)], [shape((1, 2 * hidden, width), f32)]
    )
    return d_tokens, d_probs.T, grad_total


def solution(mesh):
    rows = P(("rep", "ep", "dp"), None)
    weights = P("ep", "dp", None)
    return jax.shard_map(
        local,
        mesh=mesh,
        in_specs=(rows,) * 4 + (weights,) * 3,
        out_specs=(rows, rows, weights),
        check_vma=False,
    )
```

```python
import functools

import jax
import jax.numpy as jnp
from jax import lax
from jax.experimental import pallas as pl
from jax.experimental.pallas import tpu as pltpu
from jax.sharding import PartitionSpec as P

LANES = 128
VMEM_BYTES = 32 * 1024 * 1024
f32, bf16 = jnp.float32, jnp.bfloat16


def dot(left, right, contract):
    return lax.dot_general(left, right, ((contract[0:1], contract[1:2]), ((), ())), preferred_element_type=f32)


def swap(value, axis, mask):
    return lax.ppermute(value, axis, [(i, i ^ mask) for i in range(lax.axis_size(axis))])


def exchange(chunks, masks):
    return [chunks[0]] + [swap(chunk, "ep", mask) for chunk, mask in zip(chunks[1:], masks[1:])]


def swap_by_core(value, masks):
    count = lax.axis_size("dp")
    pairs = [(r * count + i, r * count + (i ^ mask)) for r, mask in enumerate(masks) for i in range(count)]
    return lax.ppermute(value, ("rep", "dp"), pairs)


def kernel_call(body, inputs, outputs, flops=0, **kwargs):
    whole = pl.BlockSpec(memory_space=pltpu.VMEM)
    moved = sum(a.size * a.dtype.itemsize for a in inputs + outputs)
    return pl.pallas_call(
        body,
        out_shape=outputs,
        in_specs=kwargs.pop("in_specs", [whole] * len(inputs)),
        out_specs=[whole] * len(outputs),
        cost_estimate=pl.CostEstimate(flops=flops, bytes_accessed=moved, transcendentals=0),
        compiler_params=pltpu.CompilerParams(vmem_limit_bytes=VMEM_BYTES),
        **kwargs,
    )(*inputs)


def iota(shape, dim):
    return lax.broadcasted_iota(jnp.int32, shape, dim)


def pack_copies(weights, packed, half, sems):
    hidden = packed.shape[0] // 3
    rows = pl.ds(pl.multiple_of(half * hidden, hidden), hidden)
    return [
        pltpu.make_async_copy(weight.at[0, rows], packed.at[pl.ds(i * hidden, hidden)], sems.at[i])
        for i, weight in enumerate(weights)
    ]


def pack_kernel(gate, up, down, packed, sems):
    copies = pack_copies((gate, up, down), packed, lax.axis_index("rep"), sems)
    for copy in copies:
        copy.start()
    for copy in copies:
        copy.wait()


def dispatch_kernel(experts, cap, chunk_count, *refs):
    given, weights, refs = refs[:4], refs[4:7], refs[7:]
    chunks, (slot_out, packed, *held), sems = refs[:chunk_count], refs[chunk_count:-1], refs[-1]
    loads = [pltpu.make_async_copy(*pair, sems.at[3 + i]) for i, pair in enumerate(zip(given, held))]
    packs = pack_copies(weights, packed, 1 - lax.axis_index("rep"), sems)
    for copy in loads + packs:
        copy.start()
    for copy in loads[:2]:
        copy.wait()

    ids, route_weight, tokens, upstream = held
    top, tok_dev = ids.shape
    rows = experts * cap // chunk_count
    me = lax.axis_index("ep")
    expert_of_row = iota((experts, tok_dev), 0)
    named = [(expert_of_row == ids[k : k + 1, :]).astype(f32) for k in range(top)]
    earlier = (iota((tok_dev, tok_dev), 0) < iota((tok_dev, tok_dev), 1)).astype(bf16)
    before = dot(sum(named).astype(bf16), earlier, (1, 0))
    row = iota((2 * experts * cap, tok_dev), 0)
    take_x = jnp.zeros(row.shape, f32)
    take_dy = jnp.zeros(row.shape, f32)
    scale = jnp.zeros(row.shape, f32)
    for k in range(top):
        rank = jnp.sum(before * named[k], axis=0, keepdims=True).astype(jnp.int32)
        expert = ids[k : k + 1, :]
        if chunk_count > 1:
            mask = expert ^ me
            chunk = jnp.where(mask == 0, 0, experts - mask)
            slot = chunk * cap + rank
            x_row = slot + chunk * cap
        else:
            slot = expert * cap + rank
            x_row = slot
        slot_out[k : k + 1, :] = slot
        here_x = (row == x_row).astype(f32)
        here_dy = (row == x_row + rows).astype(f32)
        take_x += here_x
        take_dy += here_dy
        scale += here_x + here_dy * route_weight[k : k + 1, :].astype(f32)
    scale = jnp.sum(scale, axis=1, keepdims=True)
    take_x, take_dy = take_x.astype(bf16), take_dy.astype(bf16)
    for copy in loads[2:]:
        copy.wait()
    picked = dot(take_x, tokens[...], (1, 0)) + dot(take_dy, upstream[...], (1, 0))
    picked = picked * scale
    for c in range(chunk_count):
        chunks[c][...] = picked[2 * rows * c : 2 * rows * (c + 1)].astype(bf16)
    for copy in packs:
        copy.wait()


def expert_math(x_rows, d_rows, pieces):
    hidden = pieces[0].shape[0] // 3
    gate, up, down = [[piece[i * hidden : (i + 1) * hidden] for piece in pieces] for i in range(3)]
    mixers = jnp.concatenate(gate + up)
    pre = dot(x_rows, mixers, (1, 1))
    d_act = dot(d_rows, jnp.concatenate(down), (1, 1))
    gate_pre, up_pre = pre[:, : hidden * len(pieces)], pre[:, hidden * len(pieces) :]
    sig = jax.nn.sigmoid(gate_pre)
    silu = gate_pre * sig
    act = silu * up_pre
    prob = jnp.sum(act * d_act, axis=1, keepdims=True)
    d_gate = d_act * up_pre * sig * (1.0 + gate_pre * (1.0 - sig))
    d_pre = jnp.concatenate([d_gate, d_act * silu], axis=1).astype(bf16)
    return dot(d_pre, mixers, (1, 0)), prob, act.astype(bf16)


def gather_kernel(*refs):
    *chunks, x_out, d_out = refs
    rows = chunks[0].shape[0] // 2
    values = [c[...].astype(f32) for c in chunks]
    x_out[...] = jnp.concatenate([v[:rows] for v in values]).astype(bf16)
    d_out[...] = jnp.concatenate([v[rows:] for v in values]).astype(bf16)


def both_cores(x_own, d_own, x_other, d_other):
    return [jnp.concatenate([a[...], b[...]]) for a, b in ((x_own, x_other), (d_own, d_other))]


def early_kernel(*refs):
    *pieces, dx_out, act_out = refs[4:]
    dx, prob, act_out[...] = expert_math(*both_cores(*refs[:4]), pieces)
    width = dx.shape[1]
    dx_out[:, :width] = dx
    dx_out[:, width:] = jnp.broadcast_to(prob, (prob.shape[0], LANES))


def late_kernel(*refs):
    dx_ref, far, keep, give, act_out = refs[4:]
    dx, prob, act_out[...] = expert_math(*both_cores(*refs[:4]), [far])
    width, slots = dx.shape[1], keep.shape[0]
    for side, value in ((slice(0, width), dx), (slice(width, None), jnp.broadcast_to(prob, (prob.shape[0], LANES)))):
        total = value + dx_ref[:, side]
        keep[:, side] = total[:slots]
        give[:, side] = total[slots:].astype(bf16)


def down_kernel(act, d_own, d_other, *grads):
    total = dot(act[...], jnp.concatenate([d_own[...], d_other[...]]), (0, 0))
    start = 0
    for grad in grads:
        grad[...] = total[start : start + grad.shape[0]].astype(grad.dtype)
        start += grad.shape[0]


def grad_kernel(own, near, far, out):
    hidden = own.shape[0]
    out[:hidden] = (own[...] + near[:hidden].astype(f32) + far[...].astype(f32)).astype(bf16)
    out[hidden:] = near[hidden:]


def total_kernel(mine, theirs, out):
    hidden = mine.shape[0] // 2
    rep = lax.axis_index("rep")
    for i, half in enumerate((rep, 1 - rep)):
        here, there = slice(i * hidden, (i + 1) * hidden), slice((1 - i) * hidden, (2 - i) * hidden)
        rows = pl.ds(pl.multiple_of(half * hidden, hidden), hidden)
        out[0, rows] = mine[here].astype(f32) + theirs[there].astype(f32)


def add_kernel(places, keep, got, *chunks):
    rows = chunks[0].shape[0]
    total = keep[...] + got[...].astype(f32)
    for place, chunk in zip(places, chunks):
        chunk[...] = total[place * rows : (place + 1) * rows].astype(bf16)


def combine_kernel(places, *refs):
    chunks, (slot, route_weight, tokens_out, probs_out) = refs[: len(places)], refs[len(places) :]
    rows = chunks[0].shape[0]
    tok_dev, width = tokens_out.shape
    top = slot.shape[0]
    total = 0.0
    probs = [0.0] * top
    for c, place in enumerate(places):
        slot_of_row = iota((rows, tok_dev), 0) + place * rows
        hits = [(slot_of_row == slot[k : k + 1, :]).astype(f32) for k in range(top)]
        total = total + dot(sum(hits).astype(bf16), chunks[c][:, :width], (0, 0))
        prob = chunks[c][:, width : width + 1].astype(f32)
        for k in range(top):
            probs[k] = probs[k] + jnp.sum(hits[k] * prob, axis=0, keepdims=True)
    tokens_out[...] = total.astype(bf16)
    for k in range(top):
        probs_out[k : k + 1, :] = (probs[k] / route_weight[k : k + 1, :].astype(f32)).astype(bf16)


def local(tokens, upstream, expert_ids, route_weight, gate_weight, up_weight, down_weight):
    tok_dev, width = tokens.shape
    top = expert_ids.shape[1]
    experts, reps = lax.axis_size("ep"), lax.axis_size("rep")
    cap = 2 * ((5 * tok_dev * top + 8 * experts - 1) // (8 * experts))
    slots = experts * cap
    chunk_count = experts if experts <= 8 else 1
    rows = slots // chunk_count
    masks = [0, *range(experts - 1, 0, -1)]
    hidden = gate_weight.shape[1] // reps
    shape = jax.ShapeDtypeStruct
    in_hbm = pl.BlockSpec(memory_space=pltpu.HBM)

    given = [expert_ids.T, route_weight.T, tokens, upstream]
    given, weights = [
        [pltpu.with_memory_space_constraint(a, pltpu.HBM) for a in arrays]
        for arrays in (given, (gate_weight, up_weight, down_weight))
    ]
    (first,) = kernel_call(
        pack_kernel,
        weights,
        [shape((3 * hidden, width), bf16)],
        in_specs=[in_hbm] * 3,
        scratch_shapes=[pltpu.SemaphoreType.DMA((3,))],
    )
    *chunks, slot, second = kernel_call(
        functools.partial(dispatch_kernel, experts, cap, chunk_count),
        given + weights,
        [shape((2 * rows, width), bf16)] * chunk_count
        + [shape((top, tok_dev), jnp.int32), shape((3 * hidden, width), bf16)],
        in_specs=[in_hbm] * 7,
        scratch_shapes=[pltpu.VMEM(a.shape, a.dtype) for a in given] + [pltpu.SemaphoreType.DMA((7,))],
    )

    along, across = (1, 2), (2, 1)
    near = [swap_by_core(first, along), swap_by_core(second, along)]
    far = swap_by_core(near[0], across)

    if chunk_count > 1:
        chunks = exchange(chunks, masks)
    else:
        moved = chunks[0].reshape(2, experts, cap, width)
        moved = lax.all_to_all(moved, "ep", split_axis=1, concat_axis=1, tiled=True)
        chunks = [moved.reshape(2 * rows, width)]
    own = kernel_call(gather_kernel, chunks, [shape((slots, width), bf16)] * 2, flops=2 * 10**9)
    other = [swap(part, "rep", 1) for part in own]

    wide = width + LANES
    dx, act = kernel_call(
        early_kernel,
        [*own, *other, first, *near],
        [shape((2 * slots, wide), f32), shape((2 * slots, 3 * hidden), bf16)],
        flops=2 * 10**9,
    )
    grad_own, grad_near = kernel_call(
        down_kernel, [act, own[1], other[1]], [shape((hidden, width), f32), shape((2 * hidden, width), bf16)]
    )
    keep, give, act = kernel_call(
        late_kernel,
        [*own, *other, dx, far],
        [shape((slots, wide), f32), shape((slots, wide), bf16), shape((2 * slots, hidden), bf16)],
    )
    (grad_far,) = kernel_call(down_kernel, [act, own[1], other[1]], [shape((hidden, width), bf16)])
    places = [0, chunk_count - 1, *range(1, chunk_count - 1)][:chunk_count]
    back = kernel_call(
        functools.partial(add_kernel, places),
        [keep, swap(give, "rep", 1)],
        [shape((rows, wide), bf16)] * chunk_count,
    )
    if chunk_count > 1:
        back = exchange(back, [masks[place] for place in places])
    else:
        moved = back[0].reshape(experts, cap, wide)
        moved = lax.all_to_all(moved, "ep", split_axis=0, concat_axis=0, tiled=True)
        back = [moved.reshape(rows, wide)]
    d_tokens, d_probs = kernel_call(
        functools.partial(combine_kernel, places),
        back + [slot, route_weight.T],
        [shape((tok_dev, width), bf16), shape((top, tok_dev), bf16)],
        flops=8 * 10**9,
    )

    arrived = swap_by_core(grad_near, along), swap_by_core(grad_far, (3, 3))
    (mine,) = kernel_call(grad_kernel, [grad_own, *arrived], [shape((2 * hidden, width), bf16)])
    (grad_total,) = kernel_call(
        total_kernel, [mine, swap(mine, "rep", 1)], [shape((1, 2 * hidden, width), f32)]
    )
    return d_tokens, d_probs.T, grad_total


def solution(mesh):
    rows = P(("rep", "ep", "dp"), None)
    weights = P("ep", "dp", None)
    return jax.shard_map(
        local,
        mesh=mesh,
        in_specs=(rows,) * 4 + (weights,) * 3,
        out_specs=(rows, rows, weights),
        check_vma=False,
    )
```

```python
import functools

import jax
import jax.numpy as jnp
from jax import lax
from jax.experimental import pallas as pl
from jax.experimental.pallas import tpu as pltpu
from jax.sharding import PartitionSpec as P

LANES = 128
VMEM_BYTES = 32 * 1024 * 1024
f32, bf16 = jnp.float32, jnp.bfloat16


def dot(left, right, contract):
    return lax.dot_general(left, right, ((contract[0:1], contract[1:2]), ((), ())), preferred_element_type=f32)


def swap(value, axis, mask):
    return lax.ppermute(value, axis, [(i, i ^ mask) for i in range(lax.axis_size(axis))])


def exchange(chunks):
    return chunks[:1] + [swap(chunks[c], "ep", c) for c in range(1, len(chunks))]


def swap_by_core(value, masks):
    count = lax.axis_size("dp")
    pairs = [(r * count + i, r * count + (i ^ mask)) for r, mask in enumerate(masks) for i in range(count)]
    return lax.ppermute(value, ("rep", "dp"), pairs)


def kernel_call(body, inputs, outputs, flops=0, **kwargs):
    whole = pl.BlockSpec(memory_space=pltpu.VMEM)
    moved = sum(a.size * a.dtype.itemsize for a in inputs + outputs)
    return pl.pallas_call(
        body,
        out_shape=outputs,
        in_specs=kwargs.pop("in_specs", [whole] * len(inputs)),
        out_specs=[whole] * len(outputs),
        cost_estimate=pl.CostEstimate(flops=flops, bytes_accessed=moved, transcendentals=0),
        compiler_params=pltpu.CompilerParams(vmem_limit_bytes=VMEM_BYTES),
        **kwargs,
    )(*inputs)


def iota(shape, dim):
    return lax.broadcasted_iota(jnp.int32, shape, dim)


def dispatch_kernel(experts, cap, chunk_count, *refs):
    given, weights, refs = refs[:4], refs[4:7], refs[7:]
    chunks, (slot_out, *packed), (*held, sems) = refs[:chunk_count], refs[chunk_count:-5], refs[-5:]
    hidden = packed[0].shape[0] // 3
    rep = lax.axis_index("rep")
    loads = [pltpu.make_async_copy(*pair, sems.at[i]) for i, pair in enumerate(zip(given, held))]
    packs = []
    for j, half in enumerate((rep, 1 - rep)):
        rows = pl.ds(pl.multiple_of(half * hidden, hidden), hidden)
        packs += [
            pltpu.make_async_copy(weight.at[0, rows], packed[j].at[pl.ds(i * hidden, hidden)], sems.at[4 + 3 * j + i])
            for i, weight in enumerate(weights)
        ]
    for copy in loads + packs:
        copy.start()
    for copy in loads[:2]:
        copy.wait()

    ids, route_weight, tokens, upstream = held
    top, tok_dev = ids.shape
    rows = experts * cap // chunk_count
    me = lax.axis_index("ep")
    expert_of_row = iota((experts, tok_dev), 0)
    named = [(expert_of_row == ids[k : k + 1, :]).astype(f32) for k in range(top)]
    earlier = (iota((tok_dev, tok_dev), 0) < iota((tok_dev, tok_dev), 1)).astype(bf16)
    before = dot(sum(named).astype(bf16), earlier, (1, 0))
    row = iota((2 * experts * cap, tok_dev), 0)
    take_x = jnp.zeros(row.shape, f32)
    take_dy = jnp.zeros(row.shape, f32)
    scale = jnp.zeros(row.shape, f32)
    for k in range(top):
        rank = jnp.sum(before * named[k], axis=0, keepdims=True).astype(jnp.int32)
        expert = ids[k : k + 1, :]
        if chunk_count > 1:
            chunk = expert ^ me
            slot = chunk * cap + rank
            x_row = slot + chunk * cap
        else:
            slot = expert * cap + rank
            x_row = slot
        slot_out[k : k + 1, :] = slot
        here_x = (row == x_row).astype(f32)
        here_dy = (row == x_row + rows).astype(f32)
        take_x += here_x
        take_dy += here_dy
        scale += here_x + here_dy * route_weight[k : k + 1, :].astype(f32)
    scale = jnp.sum(scale, axis=1, keepdims=True)
    take_x, take_dy = take_x.astype(bf16), take_dy.astype(bf16)
    for copy in loads[2:]:
        copy.wait()
    picked = dot(take_x, tokens[...], (1, 0)) + dot(take_dy, upstream[...], (1, 0))
    picked = picked * scale
    for c in range(chunk_count):
        chunks[c][...] = picked[2 * rows * c : 2 * rows * (c + 1)].astype(bf16)
    for copy in packs:
        copy.wait()


def expert_math(x_rows, d_rows, pieces):
    hidden = pieces[0].shape[0] // 3
    gate, up, down = [[piece[i * hidden : (i + 1) * hidden] for piece in pieces] for i in range(3)]
    mixers = jnp.concatenate(gate + up)
    pre = dot(x_rows, mixers, (1, 1))
    d_act = dot(d_rows, jnp.concatenate(down), (1, 1))
    gate_pre, up_pre = pre[:, : hidden * len(pieces)], pre[:, hidden * len(pieces) :]
    sig = jax.nn.sigmoid(gate_pre)
    silu = gate_pre * sig
    act = silu * up_pre
    prob = jnp.sum(act * d_act, axis=1, keepdims=True)
    d_gate = d_act * up_pre * sig * (1.0 + gate_pre * (1.0 - sig))
    d_pre = jnp.concatenate([d_gate, d_act * silu], axis=1).astype(bf16)
    return dot(d_pre, mixers, (1, 0)), prob, dot(act.astype(bf16), d_rows, (0, 0))


def gather_kernel(*refs):
    *chunks, x_out, d_out = refs
    rows = chunks[0].shape[0] // 2
    values = [c[...].astype(f32) for c in reversed(chunks)]
    x_out[...] = jnp.concatenate([v[:rows] for v in values]).astype(bf16)
    d_out[...] = jnp.concatenate([v[rows:] for v in values]).astype(bf16)


def both_cores(x_own, d_own, x_other, d_other):
    return [jnp.concatenate([a[...], b[...]]) for a, b in ((x_own, x_other), (d_own, d_other))]


def early_kernel(*refs):
    *pieces, dx_out, grad_own, grad_near = refs[4:]
    dx, prob, grad = expert_math(*both_cores(*refs[:4]), pieces)
    width, hidden = dx.shape[1], grad_own.shape[0]
    dx_out[:, :width] = dx
    dx_out[:, width:] = jnp.broadcast_to(prob, (prob.shape[0], LANES))
    grad_own[...] = grad[:hidden]
    grad_near[...] = grad[hidden:].astype(bf16)


def middle_kernel(*refs):
    dx_ref, grad_ref, piece, dx_out, grad_out = refs[4:]
    dx, prob, grad = expert_math(*both_cores(*refs[:4]), [piece])
    width, hidden = dx.shape[1], grad.shape[0]
    dx_out[:, :width] = dx_ref[:, :width] + dx
    dx_out[:, width:] = dx_ref[:, width:] + prob
    grad_out[:hidden] = grad_ref[...]
    grad_out[hidden:] = grad.astype(bf16)


def late_kernel(*refs):
    dx_ref, far, keep, *gives, grad_far = refs[4:]
    dx, prob, grad = expert_math(*both_cores(*refs[:4]), [far])
    width, slots = dx.shape[1], keep.shape[0]
    for side, value in ((slice(0, width), dx), (slice(width, None), jnp.broadcast_to(prob, (prob.shape[0], LANES)))):
        total = value + dx_ref[:, side]
        keep[:, side] = total[:slots]
        for i, give in enumerate(reversed(gives)):
            rows = give.shape[0]
            give[:, side] = total[slots + rows * i : slots + rows * (i + 1)].astype(bf16)
    grad_far[...] = grad.astype(bf16)


def grad_kernel(own, near, far, out):
    hidden = own.shape[0]
    out[:hidden] = (own[...] + near[:hidden].astype(f32) + far[...].astype(f32)).astype(bf16)
    out[hidden:] = near[hidden:]


def total_kernel(mine, theirs, out):
    hidden = mine.shape[0] // 2
    rep = lax.axis_index("rep")
    for i, half in enumerate((rep, 1 - rep)):
        here, there = slice(i * hidden, (i + 1) * hidden), slice((1 - i) * hidden, (2 - i) * hidden)
        rows = pl.ds(pl.multiple_of(half * hidden, hidden), hidden)
        out[0, rows] = mine[here].astype(f32) + theirs[there].astype(f32)


def add_kernel(start, keep, got, *chunks):
    rows = chunks[0].shape[0]
    total = keep[start : start + got.shape[0]] + got[...].astype(f32)
    for c, chunk in enumerate(chunks):
        chunk[...] = total[c * rows : (c + 1) * rows].astype(bf16)


def combine_kernel(chunk_count, *refs):
    chunks, (slot, route_weight, tokens_out, probs_out) = refs[:chunk_count], refs[chunk_count:]
    rows = chunks[0].shape[0]
    tok_dev, width = tokens_out.shape
    top = slot.shape[0]
    total = 0.0
    probs = [0.0] * top
    for c, place in enumerate(reversed(range(chunk_count))):
        slot_of_row = iota((rows, tok_dev), 0) + place * rows
        hits = [(slot_of_row == slot[k : k + 1, :]).astype(f32) for k in range(top)]
        total = total + dot(sum(hits).astype(bf16), chunks[c][:, :width], (0, 0))
        prob = chunks[c][:, width : width + 1].astype(f32)
        for k in range(top):
            probs[k] = probs[k] + jnp.sum(hits[k] * prob, axis=0, keepdims=True)
    tokens_out[...] = total.astype(bf16)
    for k in range(top):
        probs_out[k : k + 1, :] = (probs[k] / route_weight[k : k + 1, :].astype(f32)).astype(bf16)


def local(tokens, upstream, expert_ids, route_weight, gate_weight, up_weight, down_weight):
    tok_dev, width = tokens.shape
    top = expert_ids.shape[1]
    experts, reps = lax.axis_size("ep"), lax.axis_size("rep")
    cap = 2 * ((5 * tok_dev * top + 8 * experts - 1) // (8 * experts))
    slots = experts * cap
    chunk_count = experts if experts <= 8 else 1
    rows = slots // chunk_count
    hidden = gate_weight.shape[1] // reps
    shape = jax.ShapeDtypeStruct
    in_hbm = pl.BlockSpec(memory_space=pltpu.HBM)

    given = [expert_ids.T, route_weight.T, tokens, upstream]
    *chunks, slot, first, second = kernel_call(
        functools.partial(dispatch_kernel, experts, cap, chunk_count),
        [pltpu.with_memory_space_constraint(a, pltpu.HBM) for a in [*given, gate_weight, up_weight, down_weight]],
        [shape((2 * rows, width), bf16)] * chunk_count
        + [shape((top, tok_dev), jnp.int32)]
        + [shape((3 * hidden, width), bf16)] * 2,
        in_specs=[in_hbm] * 7,
        scratch_shapes=[pltpu.VMEM(a.shape, a.dtype) for a in given] + [pltpu.SemaphoreType.DMA((10,))],
    )

    along, across = (1, 2), (2, 1)
    near = [swap_by_core(first, along), swap_by_core(second, along)]
    far = swap_by_core(near[0], across)

    if chunk_count > 1:
        chunks = exchange(chunks)
    else:
        moved = chunks[0].reshape(2, experts, cap, width)
        moved = lax.all_to_all(moved, "ep", split_axis=1, concat_axis=1, tiled=True)
        chunks = [moved.reshape(2 * rows, width)]
    own = kernel_call(gather_kernel, chunks[::-1], [shape((slots, width), bf16)] * 2, flops=2 * 10**9)
    other = [swap(part, "rep", 1) for part in own]

    wide = width + LANES
    dx, grad_own, grad_near = kernel_call(
        early_kernel,
        [*own, *other, first, near[0]],
        [shape((2 * slots, wide), f32), shape((hidden, width), f32), shape((hidden, width), bf16)],
        flops=10**9,
    )
    dx, grad_near = kernel_call(
        middle_kernel,
        [*own, *other, dx, grad_near, near[1]],
        [shape((2 * slots, wide), f32), shape((2 * hidden, width), bf16)],
        flops=0,
    )
    parts = 2 if chunk_count % 2 == 0 else 1
    keep, *gives, grad_far = kernel_call(
        late_kernel,
        [*own, *other, dx, far],
        [shape((slots, wide), f32)]
        + [shape((slots // parts, wide), bf16)] * parts
        + [shape((hidden, width), bf16)],
    )
    back = []
    for i, give in enumerate(gives):
        sums = kernel_call(
            functools.partial(add_kernel, (parts - 1 - i) * slots // parts),
            [keep, swap(give, "rep", 1)],
            [shape((rows, wide), bf16)] * (chunk_count // parts),
        )
        back = [*sums, *back]
    if chunk_count > 1:
        back = exchange(back)
    else:
        moved = back[0].reshape(experts, cap, wide)
        moved = lax.all_to_all(moved, "ep", split_axis=0, concat_axis=0, tiled=True)
        back = [moved.reshape(rows, wide)]
    d_tokens, d_probs = kernel_call(
        functools.partial(combine_kernel, chunk_count),
        back[::-1] + [slot, route_weight.T],
        [shape((tok_dev, width), bf16), shape((top, tok_dev), bf16)],
        flops=8 * 10**9,
    )

    arrived = swap_by_core(grad_near, along), swap_by_core(grad_far, (3, 3))
    (mine,) = kernel_call(grad_kernel, [grad_own, *arrived], [shape((2 * hidden, width), bf16)])
    (grad_total,) = kernel_call(
        total_kernel, [mine, swap(mine, "rep", 1)], [shape((1, 2 * hidden, width), f32)]
    )
    return d_tokens, d_probs.T, grad_total


def solution(mesh):
    rows = P(("rep", "ep", "dp"), None)
    weights = P("ep", "dp", None)
    return jax.shard_map(
        local,
        mesh=mesh,
        in_specs=(rows,) * 4 + (weights,) * 3,
        out_specs=(rows, rows, weights),
        check_vma=False,
    )
```

```python
import functools

import jax
import jax.numpy as jnp
from jax import lax
from jax.experimental import pallas as pl
from jax.experimental.pallas import tpu as pltpu
from jax.sharding import PartitionSpec as P

LANES = 128
FOLD = 256
VMEM_BYTES = 32 * 1024 * 1024
f32, bf16 = jnp.float32, jnp.bfloat16


def dot(left, right, contract):
    return lax.dot_general(left, right, ((contract[0:1], contract[1:2]), ((), ())), preferred_element_type=f32)


def swap(value, axis, mask):
    return lax.ppermute(value, axis, [(i, i ^ mask) for i in range(lax.axis_size(axis))])


def exchange(chunks):
    return chunks[:1] + [swap(chunks[c], "ep", c) for c in range(1, len(chunks))]


def swap_by_core(value, masks):
    count = lax.axis_size("dp")
    pairs = [(r * count + i, r * count + (i ^ mask)) for r, mask in enumerate(masks) for i in range(count)]
    return lax.ppermute(value, ("rep", "dp"), pairs)


def kernel_call(body, inputs, outputs, flops=0, **kwargs):
    whole = pl.BlockSpec(memory_space=pltpu.VMEM)
    moved = sum(a.size * a.dtype.itemsize for a in inputs + outputs)
    return pl.pallas_call(
        body,
        out_shape=outputs,
        in_specs=kwargs.pop("in_specs", [whole] * len(inputs)),
        out_specs=[whole] * len(outputs),
        cost_estimate=pl.CostEstimate(flops=flops, bytes_accessed=moved, transcendentals=0),
        compiler_params=pltpu.CompilerParams(vmem_limit_bytes=VMEM_BYTES),
        **kwargs,
    )(*inputs)


def iota(shape, dim):
    return lax.broadcasted_iota(jnp.int32, shape, dim)


def dispatch_kernel(experts, cap, chunk_count, *refs):
    given, weights, refs = refs[:4], refs[4:7], refs[7:]
    chunks, (slot_out, *packed), (*held, sems) = refs[:chunk_count], refs[chunk_count:-5], refs[-5:]
    hidden = packed[0].shape[0] // 3
    rep = lax.axis_index("rep")
    loads = [pltpu.make_async_copy(*pair, sems.at[i]) for i, pair in enumerate(zip(given, held))]
    packs = []
    for j, half in enumerate((rep, 1 - rep)):
        rows = pl.ds(pl.multiple_of(half * hidden, hidden), hidden)
        packs += [
            pltpu.make_async_copy(weight.at[0, rows], packed[j].at[pl.ds(i * hidden, hidden)], sems.at[4 + 3 * j + i])
            for i, weight in enumerate(weights)
        ]
    for copy in loads + packs:
        copy.start()
    for copy in loads[:2]:
        copy.wait()

    ids, route_weight, tokens, upstream = held
    top, tok_dev = ids.shape
    rows = experts * cap // chunk_count
    me = lax.axis_index("ep")
    expert_of_row = iota((experts, tok_dev), 0)
    named = [(expert_of_row == ids[k : k + 1, :]).astype(f32) for k in range(top)]
    earlier = (iota((tok_dev, tok_dev), 0) < iota((tok_dev, tok_dev), 1)).astype(bf16)
    before = dot(sum(named).astype(bf16), earlier, (1, 0))
    row = iota((2 * experts * cap, tok_dev), 0)
    take_x = jnp.zeros(row.shape, f32)
    take_dy = jnp.zeros(row.shape, f32)
    scale = jnp.zeros(row.shape, f32)
    for k in range(top):
        rank = jnp.sum(before * named[k], axis=0, keepdims=True).astype(jnp.int32)
        expert = ids[k : k + 1, :]
        if chunk_count > 1:
            chunk = expert ^ me
            slot = chunk * cap + rank
            x_row = slot + chunk * cap
        else:
            slot = expert * cap + rank
            x_row = slot
        slot_out[k : k + 1, :] = slot
        here_x = (row == x_row).astype(f32)
        here_dy = (row == x_row + rows).astype(f32)
        take_x += here_x
        take_dy += here_dy
        scale += here_x + here_dy * route_weight[k : k + 1, :].astype(f32)
    scale = jnp.sum(scale, axis=1, keepdims=True)
    take_x, take_dy = take_x.astype(bf16), take_dy.astype(bf16)
    for copy in loads[2:]:
        copy.wait()
    picked = dot(take_x, tokens[...], (1, 0)) + dot(take_dy, upstream[...], (1, 0))
    picked = picked * scale
    for c in range(chunk_count):
        chunks[c][...] = picked[2 * rows * c : 2 * rows * (c + 1)].astype(bf16)
    for copy in packs:
        copy.wait()


def expert_math(x_rows, d_rows, pieces):
    hidden = pieces[0].shape[0] // 3
    gate, up, down = [[piece[i * hidden : (i + 1) * hidden] for piece in pieces] for i in range(3)]
    mixers = jnp.concatenate(gate + up)
    pre = dot(x_rows, mixers, (1, 1))
    d_act = dot(d_rows, jnp.concatenate(down), (1, 1))
    gate_pre, up_pre = pre[:, : hidden * len(pieces)], pre[:, hidden * len(pieces) :]
    sig = jax.nn.sigmoid(gate_pre)
    silu = gate_pre * sig
    act = silu * up_pre
    prob = jnp.sum(act * d_act, axis=1, keepdims=True)
    d_gate = d_act * up_pre * sig * (1.0 + gate_pre * (1.0 - sig))
    d_pre = jnp.concatenate([d_gate, d_act * silu], axis=1).astype(bf16)
    return dot(d_pre, mixers, (1, 0)), prob, dot(act.astype(bf16), d_rows, (0, 0))


def gather_kernel(*refs):
    *chunks, x_out, d_out = refs
    rows = chunks[0].shape[0] // 2
    values = [c[...].astype(f32) for c in reversed(chunks)]
    x_out[...] = jnp.concatenate([v[:rows] for v in values]).astype(bf16)
    d_out[...] = jnp.concatenate([v[rows:] for v in values]).astype(bf16)


def both_cores(x_own, d_own, x_other, d_other):
    return [jnp.concatenate([a[...], b[...]]) for a, b in ((x_own, x_other), (d_own, d_other))]


def early_kernel(*refs):
    *pieces, dx_out, grad_own, grad_near = refs[4:]
    dx, prob, grad = expert_math(*both_cores(*refs[:4]), pieces)
    width, hidden = dx.shape[1], grad_own.shape[0]
    dx_out[:, :width] = dx
    dx_out[:, width:] = jnp.broadcast_to(prob, (prob.shape[0], LANES))
    grad_own[...] = grad[:hidden]
    grad_near[...] = grad[hidden:].astype(bf16)


def middle_kernel(*refs):
    dx_ref, grad_ref, piece, dx_out, grad_out = refs[4:]
    dx, prob, grad = expert_math(*both_cores(*refs[:4]), [piece])
    width, hidden = dx.shape[1], grad.shape[0]
    dx_out[:, :width] = dx_ref[:, :width] + dx
    dx_out[:, width:] = dx_ref[:, width:] + prob
    grad_out[:hidden] = grad_ref[...]
    grad_out[hidden:] = grad.astype(bf16)


def late_kernel(*refs):
    dx_ref, far, keep, *gives, grad_far = refs[4:]
    dx, prob, grad = expert_math(*both_cores(*refs[:4]), [far])
    width, slots = dx.shape[1], keep.shape[0]
    for side, value in ((slice(0, width), dx), (slice(width, None), jnp.broadcast_to(prob, (prob.shape[0], LANES)))):
        total = value + dx_ref[:, side]
        keep[:, side] = total[:slots]
        for i, give in enumerate(reversed(gives)):
            rows = give.shape[0]
            give[:, side] = total[slots + rows * i : slots + rows * (i + 1)].astype(bf16)
    grad_far[...] = grad.astype(bf16)


def grad_kernel(own, near, far, out):
    hidden = own.shape[0]
    out[:hidden] = (own[...] + near[:hidden].astype(f32) + far[...].astype(f32)).astype(bf16)
    out[hidden:] = near[hidden:]


def total_kernel(mine, theirs, out):
    hidden = mine.shape[0] // 2
    rep = lax.axis_index("rep")
    for i, half in enumerate((rep, 1 - rep)):
        here, there = slice(i * hidden, (i + 1) * hidden), slice((1 - i) * hidden, (2 - i) * hidden)
        rows = pl.ds(pl.multiple_of(half * hidden, hidden), hidden)
        out[0, rows] = mine[here].astype(f32) + theirs[there].astype(f32)


def add_kernel(start, rows, keep, got, *chunks):
    total = keep[start : start + got.shape[0]] + got[...].astype(f32)
    width = total.shape[1] - LANES
    for c, chunk in enumerate(chunks):
        value = total[c * rows : (c + 1) * rows]
        if chunk.shape[0] > rows:
            blocks = [value[:, i : i + FOLD] for i in range(0, width, FOLD)]
            diagonal = iota((rows, FOLD), 0) == iota((rows, FOLD), 1)
            prob = jnp.sum(jnp.where(diagonal, value[:, width : width + 1], 0.0), axis=0, keepdims=True)
            value = jnp.concatenate([*blocks, jnp.broadcast_to(prob, (8, FOLD))])
        chunk[...] = value.astype(bf16)


def combine_kernel(chunk_count, rows, *refs):
    chunks, (slot, route_weight, tokens_out, probs_out) = refs[:chunk_count], refs[chunk_count:]
    tok_dev, width = tokens_out.shape
    top = slot.shape[0]
    total = 0.0
    probs = [0.0] * top
    for c, place in enumerate(reversed(range(chunk_count))):
        slot_of_row = iota((rows, tok_dev), 0) + place * rows
        hits = [(slot_of_row == slot[k : k + 1, :]).astype(f32) for k in range(top)]
        value = chunks[c][...].astype(f32)
        if value.shape[0] > rows:
            blocks = [value[i : i + rows] for i in range(0, width // FOLD * rows, rows)]
            diagonal = iota((rows, FOLD), 0) == iota((rows, FOLD), 1)
            prob = value[width // FOLD * rows :][:1]
            prob = jnp.sum(jnp.where(diagonal, prob, 0.0), axis=1, keepdims=True)
            value = jnp.concatenate(blocks, axis=1)
        else:
            prob = value[:, width : width + 1]
        total = total + dot(sum(hits).astype(bf16), value[:, :width].astype(bf16), (0, 0))
        for k in range(top):
            probs[k] = probs[k] + jnp.sum(hits[k] * prob, axis=0, keepdims=True)
    tokens_out[...] = total.astype(bf16)
    for k in range(top):
        probs_out[k : k + 1, :] = (probs[k] / route_weight[k : k + 1, :].astype(f32)).astype(bf16)


def local(tokens, upstream, expert_ids, route_weight, gate_weight, up_weight, down_weight):
    tok_dev, width = tokens.shape
    top = expert_ids.shape[1]
    experts, reps = lax.axis_size("ep"), lax.axis_size("rep")
    cap = 2 * ((5 * tok_dev * top + 8 * experts - 1) // (8 * experts))
    slots = experts * cap
    chunk_count = experts if experts <= 8 else 1
    rows = slots // chunk_count
    hidden = gate_weight.shape[1] // reps
    shape = jax.ShapeDtypeStruct
    in_hbm = pl.BlockSpec(memory_space=pltpu.HBM)

    given = [expert_ids.T, route_weight.T, tokens, upstream]
    *chunks, slot, first, second = kernel_call(
        functools.partial(dispatch_kernel, experts, cap, chunk_count),
        [pltpu.with_memory_space_constraint(a, pltpu.HBM) for a in [*given, gate_weight, up_weight, down_weight]],
        [shape((2 * rows, width), bf16)] * chunk_count
        + [shape((top, tok_dev), jnp.int32)]
        + [shape((3 * hidden, width), bf16)] * 2,
        in_specs=[in_hbm] * 7,
        scratch_shapes=[pltpu.VMEM(a.shape, a.dtype) for a in given] + [pltpu.SemaphoreType.DMA((10,))],
    )

    along, across = (1, 2), (2, 1)
    near = [swap_by_core(first, along), swap_by_core(second, along)]
    far = swap_by_core(near[0], across)

    if chunk_count > 1:
        chunks = exchange(chunks)
    else:
        moved = chunks[0].reshape(2, experts, cap, width)
        moved = lax.all_to_all(moved, "ep", split_axis=1, concat_axis=1, tiled=True)
        chunks = [moved.reshape(2 * rows, width)]
    own = kernel_call(gather_kernel, chunks[::-1], [shape((slots, width), bf16)] * 2, flops=2 * 10**9)
    other = [swap(part, "rep", 1) for part in own]

    wide = width + LANES
    dx, grad_own, grad_near = kernel_call(
        early_kernel,
        [*own, *other, first, near[0]],
        [shape((2 * slots, wide), f32), shape((hidden, width), f32), shape((hidden, width), bf16)],
        flops=10**9,
    )
    dx, grad_near = kernel_call(
        middle_kernel,
        [*own, *other, dx, grad_near, near[1]],
        [shape((2 * slots, wide), f32), shape((2 * hidden, width), bf16)],
        flops=0,
    )
    parts = 2 if chunk_count % 2 == 0 else 1
    keep, *gives, grad_far = kernel_call(
        late_kernel,
        [*own, *other, dx, far],
        [shape((slots, wide), f32)]
        + [shape((slots // parts, wide), bf16)] * parts
        + [shape((hidden, width), bf16)],
    )
    folds = chunk_count > 1 and rows <= FOLD and width % FOLD == 0 and rows * width // FOLD % 8 == 0
    returned = shape((rows * width // FOLD + 8, FOLD) if folds else (rows, wide), bf16)
    back = []
    for i, give in enumerate(gives):
        sums = kernel_call(
            functools.partial(add_kernel, (parts - 1 - i) * slots // parts, rows),
            [keep, swap(give, "rep", 1)],
            [returned] * (chunk_count // parts),
        )
        back = [*sums, *back]
    if chunk_count > 1:
        back = exchange(back)
    else:
        moved = back[0].reshape(experts, cap, wide)
        moved = lax.all_to_all(moved, "ep", split_axis=0, concat_axis=0, tiled=True)
        back = [moved.reshape(rows, wide)]
    d_tokens, d_probs = kernel_call(
        functools.partial(combine_kernel, chunk_count, rows),
        back[::-1] + [slot, route_weight.T],
        [shape((tok_dev, width), bf16), shape((top, tok_dev), bf16)],
        flops=8 * 10**9,
    )

    arrived = swap_by_core(grad_near, along), swap_by_core(grad_far, (3, 3))
    (mine,) = kernel_call(grad_kernel, [grad_own, *arrived], [shape((2 * hidden, width), bf16)])
    (grad_total,) = kernel_call(
        total_kernel, [mine, swap(mine, "rep", 1)], [shape((1, 2 * hidden, width), f32)]
    )
    return d_tokens, d_probs.T, grad_total


def solution(mesh):
    rows = P(("rep", "ep", "dp"), None)
    weights = P("ep", "dp", None)
    return jax.shard_map(
        local,
        mesh=mesh,
        in_specs=(rows,) * 4 + (weights,) * 3,
        out_specs=(rows, rows, weights),
        check_vma=False,
    )
```

```python
import functools

import jax
import jax.numpy as jnp
from jax import lax
from jax.experimental import pallas as pl
from jax.experimental.pallas import tpu as pltpu
from jax.sharding import PartitionSpec as P

LANES = 128
FOLD = 256
VMEM_BYTES = 32 * 1024 * 1024
f32, bf16 = jnp.float32, jnp.bfloat16


def dot(left, right, contract):
    return lax.dot_general(left, right, ((contract[0:1], contract[1:2]), ((), ())), preferred_element_type=f32)


def swap(value, axis, mask):
    return lax.ppermute(value, axis, [(i, i ^ mask) for i in range(lax.axis_size(axis))])


def exchange(chunks):
    return chunks[:1] + [swap(chunks[c], "ep", c) for c in range(1, len(chunks))]


def swap_by_core(value, masks):
    count = lax.axis_size("dp")
    pairs = [(r * count + i, r * count + (i ^ mask)) for r, mask in enumerate(masks) for i in range(count)]
    return lax.ppermute(value, ("rep", "dp"), pairs)


def kernel_call(body, inputs, outputs, flops=0, **kwargs):
    whole = pl.BlockSpec(memory_space=pltpu.VMEM)
    moved = sum(a.size * a.dtype.itemsize for a in inputs + outputs)
    return pl.pallas_call(
        body,
        out_shape=outputs,
        in_specs=kwargs.pop("in_specs", [whole] * len(inputs)),
        out_specs=kwargs.pop("out_specs", [whole] * len(outputs)),
        cost_estimate=pl.CostEstimate(flops=flops, bytes_accessed=moved, transcendentals=0),
        compiler_params=pltpu.CompilerParams(vmem_limit_bytes=VMEM_BYTES),
        **kwargs,
    )(*inputs)


def iota(shape, dim):
    return lax.broadcasted_iota(jnp.int32, shape, dim)


def dispatch_kernel(experts, cap, chunk_count, *refs):
    given, weights, refs = refs[:4], refs[4:7], refs[7:]
    chunks, (slot_out, *packed), (*held, sems) = refs[:chunk_count], refs[chunk_count:-5], refs[-5:]
    hidden = packed[0].shape[0] // 3
    rep = lax.axis_index("rep")
    loads = [pltpu.make_async_copy(*pair, sems.at[i]) for i, pair in enumerate(zip(given, held))]
    packs = []
    for j, half in enumerate((rep, 1 - rep)):
        rows = pl.ds(pl.multiple_of(half * hidden, hidden), hidden)
        packs += [
            pltpu.make_async_copy(weight.at[0, rows], packed[j].at[pl.ds(i * hidden, hidden)], sems.at[4 + 3 * j + i])
            for i, weight in enumerate(weights)
        ]
    for copy in loads + packs:
        copy.start()
    for copy in loads[:2]:
        copy.wait()

    ids, route_weight, tokens, upstream = held
    top, tok_dev = ids.shape
    rows = experts * cap // chunk_count
    me = lax.axis_index("ep")
    expert_of_row = iota((experts, tok_dev), 0)
    named = [(expert_of_row == ids[k : k + 1, :]).astype(f32) for k in range(top)]
    earlier = (iota((tok_dev, tok_dev), 0) < iota((tok_dev, tok_dev), 1)).astype(bf16)
    before = dot(sum(named).astype(bf16), earlier, (1, 0))
    row = iota((2 * experts * cap, tok_dev), 0)
    take_x = jnp.zeros(row.shape, f32)
    take_dy = jnp.zeros(row.shape, f32)
    scale = jnp.zeros(row.shape, f32)
    for k in range(top):
        rank = jnp.sum(before * named[k], axis=0, keepdims=True).astype(jnp.int32)
        expert = ids[k : k + 1, :]
        if chunk_count > 1:
            chunk = expert ^ me
            slot = chunk * cap + rank
            x_row = slot + chunk * cap
        else:
            slot = expert * cap + rank
            x_row = slot
        slot_out[k : k + 1, :] = slot
        here_x = (row == x_row).astype(f32)
        here_dy = (row == x_row + rows).astype(f32)
        take_x += here_x
        take_dy += here_dy
        scale += here_x + here_dy * route_weight[k : k + 1, :].astype(f32)
    scale = jnp.sum(scale, axis=1, keepdims=True)
    take_x, take_dy = take_x.astype(bf16), take_dy.astype(bf16)
    for copy in loads[2:]:
        copy.wait()
    picked = dot(take_x, tokens[...], (1, 0)) + dot(take_dy, upstream[...], (1, 0))
    picked = picked * scale
    for c in range(chunk_count):
        chunks[c][...] = picked[2 * rows * c : 2 * rows * (c + 1)].astype(bf16)
    for copy in packs:
        copy.wait()


def expert_math(x_rows, d_rows, pieces):
    hidden = pieces[0].shape[0] // 3
    gate, up, down = [[piece[i * hidden : (i + 1) * hidden] for piece in pieces] for i in range(3)]
    mixers = jnp.concatenate(gate + up)
    pre = dot(x_rows, mixers, (1, 1))
    d_act = dot(d_rows, jnp.concatenate(down), (1, 1))
    gate_pre, up_pre = pre[:, : hidden * len(pieces)], pre[:, hidden * len(pieces) :]
    sig = jax.nn.sigmoid(gate_pre)
    silu = gate_pre * sig
    act = silu * up_pre
    prob = jnp.sum(act * d_act, axis=1, keepdims=True)
    d_gate = d_act * up_pre * sig * (1.0 + gate_pre * (1.0 - sig))
    d_pre = jnp.concatenate([d_gate, d_act * silu], axis=1).astype(bf16)
    return dot(d_pre, mixers, (1, 0)), prob, dot(act.astype(bf16), d_rows, (0, 0))


def gather_kernel(*refs):
    *chunks, x_out, d_out = refs
    rows = chunks[0].shape[0] // 2
    values = [c[...].astype(f32) for c in reversed(chunks)]
    x_out[...] = jnp.concatenate([v[:rows] for v in values]).astype(bf16)
    d_out[...] = jnp.concatenate([v[rows:] for v in values]).astype(bf16)


def both_cores(x_own, d_own, x_other, d_other):
    return [jnp.concatenate([a[...], b[...]]) for a, b in ((x_own, x_other), (d_own, d_other))]


def early_kernel(*refs):
    *pieces, dx_out, grad_own, grad_near = refs[4:]
    dx, prob, grad = expert_math(*both_cores(*refs[:4]), pieces)
    width, hidden = dx.shape[1], grad_own.shape[0]
    dx_out[:, :width] = dx
    dx_out[:, width:] = jnp.broadcast_to(prob, (prob.shape[0], LANES))
    grad_own[...] = grad[:hidden]
    grad_near[...] = grad[hidden:].astype(bf16)


def middle_kernel(*refs):
    dx_ref, grad_ref, piece, dx_out, grad_out = refs[4:]
    dx, prob, grad = expert_math(*both_cores(*refs[:4]), [piece])
    width, hidden = dx.shape[1], grad.shape[0]
    dx_out[:, :width] = dx_ref[:, :width] + dx
    dx_out[:, width:] = dx_ref[:, width:] + prob
    grad_out[:hidden] = grad_ref[...]
    grad_out[hidden:] = grad.astype(bf16)


def late_kernel(*refs):
    dx_ref, far, keep, *gives, grad_far = refs[4:]
    dx, prob, grad = expert_math(*both_cores(*refs[:4]), [far])
    width, slots = dx.shape[1], keep.shape[0]
    for side, value in ((slice(0, width), dx), (slice(width, None), jnp.broadcast_to(prob, (prob.shape[0], LANES)))):
        total = value + dx_ref[:, side]
        keep[:, side] = total[:slots]
        for i, give in enumerate(reversed(gives)):
            rows = give.shape[0]
            give[:, side] = total[slots + rows * i : slots + rows * (i + 1)].astype(bf16)
    grad_far[...] = grad.astype(bf16)


def grad_kernel(own, near, far, out):
    hidden = own.shape[0]
    out[:hidden] = (own[...] + near[:hidden].astype(f32) + far[...].astype(f32)).astype(bf16)
    out[hidden:] = near[hidden:]


def finish_kernel(mine, theirs, tokens, probs, grad_out, tokens_out, probs_out, held, sems):
    hidden = mine.shape[0] // 2
    rep = lax.axis_index("rep")
    copies = [pltpu.make_async_copy(tokens, tokens_out, sems.at[0]), pltpu.make_async_copy(probs, probs_out, sems.at[1])]
    for copy in copies:
        copy.start()
    for i, half in enumerate((rep, 1 - rep)):
        here, there = slice(i * hidden, (i + 1) * hidden), slice((1 - i) * hidden, (2 - i) * hidden)
        rows = pl.ds(pl.multiple_of(half * hidden, hidden), hidden)
        held[i] = mine[here].astype(f32) + theirs[there].astype(f32)
        copies.append(pltpu.make_async_copy(held.at[i], grad_out.at[0, rows], sems.at[2 + i]))
        copies[-1].start()
    for copy in copies:
        copy.wait()


def add_kernel(start, rows, keep, got, *chunks):
    total = keep[start : start + got.shape[0]] + got[...].astype(f32)
    width = total.shape[1] - LANES
    for c, chunk in enumerate(chunks):
        value = total[c * rows : (c + 1) * rows]
        if chunk.shape[0] > rows:
            blocks = [value[:, i : i + FOLD] for i in range(0, width, FOLD)]
            diagonal = iota((rows, FOLD), 0) == iota((rows, FOLD), 1)
            prob = jnp.sum(jnp.where(diagonal, value[:, width : width + 1], 0.0), axis=0, keepdims=True)
            value = jnp.concatenate([*blocks, jnp.broadcast_to(prob, (8, FOLD))])
        chunk[...] = value.astype(bf16)


def combine_kernel(chunk_count, rows, *refs):
    chunks, (slot, route_weight, tokens_out, probs_out) = refs[:chunk_count], refs[chunk_count:]
    tok_dev, width = tokens_out.shape
    top = slot.shape[0]
    total = 0.0
    probs = [0.0] * top
    for c, place in enumerate(reversed(range(chunk_count))):
        slot_of_row = iota((rows, tok_dev), 0) + place * rows
        hits = [(slot_of_row == slot[k : k + 1, :]).astype(f32) for k in range(top)]
        value = chunks[c][...].astype(f32)
        if value.shape[0] > rows:
            blocks = [value[i : i + rows] for i in range(0, width // FOLD * rows, rows)]
            diagonal = iota((rows, FOLD), 0) == iota((rows, FOLD), 1)
            prob = value[width // FOLD * rows :][:1]
            prob = jnp.sum(jnp.where(diagonal, prob, 0.0), axis=1, keepdims=True)
            value = jnp.concatenate(blocks, axis=1)
        else:
            prob = value[:, width : width + 1]
        total = total + dot(sum(hits).astype(bf16), value[:, :width].astype(bf16), (0, 0))
        for k in range(top):
            probs[k] = probs[k] + jnp.sum(hits[k] * prob, axis=0, keepdims=True)
    tokens_out[...] = total.astype(bf16)
    for k in range(top):
        probs_out[k : k + 1, :] = (probs[k] / route_weight[k : k + 1, :].astype(f32)).astype(bf16)


def local(tokens, upstream, expert_ids, route_weight, gate_weight, up_weight, down_weight):
    tok_dev, width = tokens.shape
    top = expert_ids.shape[1]
    experts, reps = lax.axis_size("ep"), lax.axis_size("rep")
    cap = 2 * ((5 * tok_dev * top + 8 * experts - 1) // (8 * experts))
    slots = experts * cap
    chunk_count = experts if experts <= 8 else 1
    rows = slots // chunk_count
    hidden = gate_weight.shape[1] // reps
    shape = jax.ShapeDtypeStruct
    in_hbm = pl.BlockSpec(memory_space=pltpu.HBM)

    given = [expert_ids.T, route_weight.T, tokens, upstream]
    *chunks, slot, first, second = kernel_call(
        functools.partial(dispatch_kernel, experts, cap, chunk_count),
        [pltpu.with_memory_space_constraint(a, pltpu.HBM) for a in [*given, gate_weight, up_weight, down_weight]],
        [shape((2 * rows, width), bf16)] * chunk_count
        + [shape((top, tok_dev), jnp.int32)]
        + [shape((3 * hidden, width), bf16)] * 2,
        in_specs=[in_hbm] * 7,
        scratch_shapes=[pltpu.VMEM(a.shape, a.dtype) for a in given] + [pltpu.SemaphoreType.DMA((10,))],
    )

    along, across = (1, 2), (2, 1)
    near = [swap_by_core(first, along), swap_by_core(second, along)]
    far = swap_by_core(near[0], across)

    if chunk_count > 1:
        chunks = exchange(chunks)
    else:
        moved = chunks[0].reshape(2, experts, cap, width)
        moved = lax.all_to_all(moved, "ep", split_axis=1, concat_axis=1, tiled=True)
        chunks = [moved.reshape(2 * rows, width)]
    own = kernel_call(gather_kernel, chunks[::-1], [shape((slots, width), bf16)] * 2, flops=2 * 10**9)
    other = [swap(part, "rep", 1) for part in own]

    wide = width + LANES
    dx, grad_own, grad_near = kernel_call(
        early_kernel,
        [*own, *other, first, near[0]],
        [shape((2 * slots, wide), f32), shape((hidden, width), f32), shape((hidden, width), bf16)],
        flops=10**9,
    )
    dx, grad_near = kernel_call(
        middle_kernel,
        [*own, *other, dx, grad_near, near[1]],
        [shape((2 * slots, wide), f32), shape((2 * hidden, width), bf16)],
        flops=0,
    )
    parts = 2 if chunk_count % 2 == 0 else 1
    keep, *gives, grad_far = kernel_call(
        late_kernel,
        [*own, *other, dx, far],
        [shape((slots, wide), f32)]
        + [shape((slots // parts, wide), bf16)] * parts
        + [shape((hidden, width), bf16)],
    )
    folds = chunk_count > 1 and rows <= FOLD and width % FOLD == 0 and rows * width // FOLD % 8 == 0
    returned = shape((rows * width // FOLD + 8, FOLD) if folds else (rows, wide), bf16)
    back = []
    for i, give in enumerate(gives):
        sums = kernel_call(
            functools.partial(add_kernel, (parts - 1 - i) * slots // parts, rows),
            [keep, swap(give, "rep", 1)],
            [returned] * (chunk_count // parts),
        )
        back = [*sums, *back]
    if chunk_count > 1:
        back = exchange(back)
    else:
        moved = back[0].reshape(experts, cap, wide)
        moved = lax.all_to_all(moved, "ep", split_axis=0, concat_axis=0, tiled=True)
        back = [moved.reshape(rows, wide)]
    d_tokens, d_probs = kernel_call(
        functools.partial(combine_kernel, chunk_count, rows),
        back[::-1] + [slot, route_weight.T],
        [shape((tok_dev, width), bf16), shape((top, tok_dev), bf16)],
        flops=8 * 10**9,
    )

    arrived = swap_by_core(grad_near, along), swap_by_core(grad_far, (3, 3))
    (mine,) = kernel_call(grad_kernel, [grad_own, *arrived], [shape((2 * hidden, width), bf16)])
    results = [
        shape((1, 2 * hidden, width), f32),
        shape((tok_dev, width), bf16),
        shape((top, tok_dev), bf16),
    ]
    grad_total, d_tokens, d_probs = kernel_call(
        finish_kernel,
        [mine, swap(mine, "rep", 1), d_tokens, d_probs],
        results,
        out_specs=[in_hbm] * 3,
        scratch_shapes=[pltpu.VMEM((2, hidden, width), f32), pltpu.SemaphoreType.DMA((4,))],
    )
    return d_tokens, d_probs.T, grad_total


def solution(mesh):
    rows = P(("rep", "ep", "dp"), None)
    weights = P("ep", "dp", None)
    return jax.shard_map(
        local,
        mesh=mesh,
        in_specs=(rows,) * 4 + (weights,) * 3,
        out_specs=(rows, rows, weights),
        check_vma=False,
    )
```

```python
import functools

import jax
import jax.numpy as jnp
from jax import lax
from jax.experimental import pallas as pl
from jax.experimental.pallas import tpu as pltpu
from jax.sharding import PartitionSpec as P

LANES = 128
FOLD = 256
BLOCK = 16
VMEM_BYTES = 32 * 1024 * 1024
f32, bf16 = jnp.float32, jnp.bfloat16


def dot(left, right, contract):
    return lax.dot_general(left, right, ((contract[0:1], contract[1:2]), ((), ())), preferred_element_type=f32)


def swap(value, axis, mask):
    return lax.ppermute(value, axis, [(i, i ^ mask) for i in range(lax.axis_size(axis))])


def exchange(chunks):
    return chunks[:1] + [swap(chunks[c], "ep", c) for c in range(1, len(chunks))]


def swap_by_core(value, masks):
    count = lax.axis_size("dp")
    pairs = [(r * count + i, r * count + (i ^ mask)) for r, mask in enumerate(masks) for i in range(count)]
    return lax.ppermute(value, ("rep", "dp"), pairs)


def kernel_call(body, inputs, outputs, flops=0, **kwargs):
    whole = pl.BlockSpec(memory_space=pltpu.VMEM)
    moved = sum(a.size * a.dtype.itemsize for a in inputs + outputs)
    return pl.pallas_call(
        body,
        out_shape=outputs,
        in_specs=kwargs.pop("in_specs", [whole] * len(inputs)),
        out_specs=kwargs.pop("out_specs", [whole] * len(outputs)),
        cost_estimate=pl.CostEstimate(flops=flops, bytes_accessed=moved, transcendentals=0),
        compiler_params=pltpu.CompilerParams(vmem_limit_bytes=VMEM_BYTES),
        **kwargs,
    )(*inputs)


def iota(shape, dim):
    return lax.broadcasted_iota(jnp.int32, shape, dim)


def blocks(rows):
    return rows // BLOCK if rows % BLOCK == 0 else 1


def block_copies(sems, source, target, start=0, offset=0, count=None):
    count = source.shape[0] if count is None else count
    block = count // blocks(count)
    return [
        pltpu.make_async_copy(
            source.at[pl.ds(pl.multiple_of(start + i, block), block)], target.at[pl.ds(offset + i, block)], next(sems)
        )
        for i in range(0, count, block)
    ]


def dispatch_kernel(experts, cap, chunk_count, *refs):
    given, weights, refs = refs[:4], refs[4:7], refs[7:]
    chunks, (slot_out, *packed), (*held, sems) = refs[:chunk_count], refs[chunk_count:-5], refs[-5:]
    hidden = packed[0].shape[0] // 3
    rep = lax.axis_index("rep")
    free = iter([sems.at[i] for i in range(sems.shape[0])])
    small = [pltpu.make_async_copy(*pair, next(free)) for pair in zip(given[:2], held)]
    loads = [copy for pair in zip(given[2:], held[2:]) for copy in block_copies(free, *pair)]
    packs = [
        copy
        for half, target in ((rep, packed[0]), (1 - rep, packed[1]))
        for i, weight in enumerate(weights)
        for copy in block_copies(free, weight.at[0], target, half * hidden, i * hidden, hidden)
    ]
    for copy in small + loads + packs:
        copy.start()
    for copy in small:
        copy.wait()

    ids, route_weight, tokens, upstream = held
    top, tok_dev = ids.shape
    rows = experts * cap // chunk_count
    me = lax.axis_index("ep")
    expert_of_row = iota((experts, tok_dev), 0)
    named = [(expert_of_row == ids[k : k + 1, :]).astype(f32) for k in range(top)]
    earlier = (iota((tok_dev, tok_dev), 0) < iota((tok_dev, tok_dev), 1)).astype(bf16)
    before = dot(sum(named).astype(bf16), earlier, (1, 0))
    row = iota((2 * experts * cap, tok_dev), 0)
    take_x = jnp.zeros(row.shape, f32)
    take_dy = jnp.zeros(row.shape, f32)
    scale = jnp.zeros(row.shape, f32)
    for k in range(top):
        rank = jnp.sum(before * named[k], axis=0, keepdims=True).astype(jnp.int32)
        expert = ids[k : k + 1, :]
        if chunk_count > 1:
            chunk = expert ^ me
            slot = chunk * cap + rank
            x_row = slot + chunk * cap
        else:
            slot = expert * cap + rank
            x_row = slot
        slot_out[k : k + 1, :] = slot
        here_x = (row == x_row).astype(f32)
        here_dy = (row == x_row + rows).astype(f32)
        take_x += here_x
        take_dy += here_dy
        scale += here_x + here_dy * route_weight[k : k + 1, :].astype(f32)
    scale = jnp.sum(scale, axis=1, keepdims=True)
    take_x, take_dy = take_x.astype(bf16), take_dy.astype(bf16)
    for copy in loads:
        copy.wait()
    picked = dot(take_x, tokens[...], (1, 0)) + dot(take_dy, upstream[...], (1, 0))
    picked = picked * scale
    for c in range(chunk_count):
        chunks[c][...] = picked[2 * rows * c : 2 * rows * (c + 1)].astype(bf16)
    for copy in packs:
        copy.wait()


def expert_math(x_rows, d_rows, pieces):
    hidden = pieces[0].shape[0] // 3
    gate, up, down = [[piece[i * hidden : (i + 1) * hidden] for piece in pieces] for i in range(3)]
    mixers = jnp.concatenate(gate + up)
    pre = dot(x_rows, mixers, (1, 1))
    d_act = dot(d_rows, jnp.concatenate(down), (1, 1))
    gate_pre, up_pre = pre[:, : hidden * len(pieces)], pre[:, hidden * len(pieces) :]
    sig = jax.nn.sigmoid(gate_pre)
    silu = gate_pre * sig
    act = silu * up_pre
    prob = jnp.sum(act * d_act, axis=1, keepdims=True)
    d_gate = d_act * up_pre * sig * (1.0 + gate_pre * (1.0 - sig))
    d_pre = jnp.concatenate([d_gate, d_act * silu], axis=1).astype(bf16)
    return dot(d_pre, mixers, (1, 0)), prob, dot(act.astype(bf16), d_rows, (0, 0))


def gather_kernel(*refs):
    *chunks, x_out, d_out = refs
    rows = chunks[0].shape[0] // 2
    values = [c[...].astype(f32) for c in reversed(chunks)]
    x_out[...] = jnp.concatenate([v[:rows] for v in values]).astype(bf16)
    d_out[...] = jnp.concatenate([v[rows:] for v in values]).astype(bf16)


def both_cores(x_own, d_own, x_other, d_other):
    return [jnp.concatenate([a[...], b[...]]) for a, b in ((x_own, x_other), (d_own, d_other))]


def early_kernel(*refs):
    *pieces, dx_out, grad_own, grad_near = refs[4:]
    dx, prob, grad = expert_math(*both_cores(*refs[:4]), pieces)
    width, hidden = dx.shape[1], grad_own.shape[0]
    dx_out[:, :width] = dx
    dx_out[:, width:] = jnp.broadcast_to(prob, (prob.shape[0], LANES))
    grad_own[...] = grad[:hidden]
    grad_near[...] = grad[hidden:].astype(bf16)


def middle_kernel(*refs):
    dx_ref, grad_ref, piece, dx_out, grad_out = refs[4:]
    dx, prob, grad = expert_math(*both_cores(*refs[:4]), [piece])
    width, hidden = dx.shape[1], grad.shape[0]
    dx_out[:, :width] = dx_ref[:, :width] + dx
    dx_out[:, width:] = dx_ref[:, width:] + prob
    grad_out[:hidden] = grad_ref[...]
    grad_out[hidden:] = grad.astype(bf16)


def late_kernel(*refs):
    dx_ref, far, keep, *gives, grad_far = refs[4:]
    dx, prob, grad = expert_math(*both_cores(*refs[:4]), [far])
    width, slots = dx.shape[1], keep.shape[0]
    for side, value in ((slice(0, width), dx), (slice(width, None), jnp.broadcast_to(prob, (prob.shape[0], LANES)))):
        total = value + dx_ref[:, side]
        keep[:, side] = total[:slots]
        for i, give in enumerate(reversed(gives)):
            rows = give.shape[0]
            give[:, side] = total[slots + rows * i : slots + rows * (i + 1)].astype(bf16)
    grad_far[...] = grad.astype(bf16)


def grad_kernel(own, near, far, out):
    hidden = own.shape[0]
    out[:hidden] = (own[...] + near[:hidden].astype(f32) + far[...].astype(f32)).astype(bf16)
    out[hidden:] = near[hidden:]


def finish_kernel(mine, theirs, tokens, probs, grad_out, tokens_out, probs_out, held, sems):
    hidden = mine.shape[0] // 2
    rep = lax.axis_index("rep")
    copies = [pltpu.make_async_copy(tokens, tokens_out, sems.at[0]), pltpu.make_async_copy(probs, probs_out, sems.at[1])]
    for copy in copies:
        copy.start()
    block = hidden // blocks(hidden)
    for place in range(0, 2 * hidden, block):
        across = (place + hidden) % (2 * hidden)
        half = rep if place < hidden else 1 - rep
        here = pl.ds(place, block)
        held[here] = mine[here].astype(f32) + theirs[pl.ds(across, block)].astype(f32)
        row = pl.multiple_of(half * hidden + place % hidden, block)
        copies.append(pltpu.make_async_copy(held.at[here], grad_out.at[0, pl.ds(row, block)], sems.at[len(copies)]))
        copies[-1].start()
    for copy in copies:
        copy.wait()


def add_kernel(start, rows, keep, got, *chunks):
    total = keep[start : start + got.shape[0]] + got[...].astype(f32)
    width = total.shape[1] - LANES
    for c, chunk in enumerate(chunks):
        value = total[c * rows : (c + 1) * rows]
        if chunk.shape[0] > rows:
            blocks = [value[:, i : i + FOLD] for i in range(0, width, FOLD)]
            diagonal = iota((rows, FOLD), 0) == iota((rows, FOLD), 1)
            prob = jnp.sum(jnp.where(diagonal, value[:, width : width + 1], 0.0), axis=0, keepdims=True)
            value = jnp.concatenate([*blocks, jnp.broadcast_to(prob, (8, FOLD))])
        chunk[...] = value.astype(bf16)


def combine_kernel(chunk_count, rows, *refs):
    chunks, (slot, route_weight, tokens_out, probs_out) = refs[:chunk_count], refs[chunk_count:]
    tok_dev, width = tokens_out.shape
    top = slot.shape[0]
    total = 0.0
    probs = [0.0] * top
    for c, place in enumerate(reversed(range(chunk_count))):
        slot_of_row = iota((rows, tok_dev), 0) + place * rows
        hits = [(slot_of_row == slot[k : k + 1, :]).astype(f32) for k in range(top)]
        value = chunks[c][...].astype(f32)
        if value.shape[0] > rows:
            blocks = [value[i : i + rows] for i in range(0, width // FOLD * rows, rows)]
            diagonal = iota((rows, FOLD), 0) == iota((rows, FOLD), 1)
            prob = value[width // FOLD * rows :][:1]
            prob = jnp.sum(jnp.where(diagonal, prob, 0.0), axis=1, keepdims=True)
            value = jnp.concatenate(blocks, axis=1)
        else:
            prob = value[:, width : width + 1]
        total = total + dot(sum(hits).astype(bf16), value[:, :width].astype(bf16), (0, 0))
        for k in range(top):
            probs[k] = probs[k] + jnp.sum(hits[k] * prob, axis=0, keepdims=True)
    tokens_out[...] = total.astype(bf16)
    for k in range(top):
        probs_out[k : k + 1, :] = (probs[k] / route_weight[k : k + 1, :].astype(f32)).astype(bf16)


def local(tokens, upstream, expert_ids, route_weight, gate_weight, up_weight, down_weight):
    tok_dev, width = tokens.shape
    top = expert_ids.shape[1]
    experts, reps = lax.axis_size("ep"), lax.axis_size("rep")
    cap = 2 * ((5 * tok_dev * top + 8 * experts - 1) // (8 * experts))
    slots = experts * cap
    chunk_count = experts if experts <= 8 else 1
    rows = slots // chunk_count
    hidden = gate_weight.shape[1] // reps
    shape = jax.ShapeDtypeStruct
    in_hbm = pl.BlockSpec(memory_space=pltpu.HBM)

    given = [expert_ids.T, route_weight.T, tokens, upstream]
    *chunks, slot, first, second = kernel_call(
        functools.partial(dispatch_kernel, experts, cap, chunk_count),
        [pltpu.with_memory_space_constraint(a, pltpu.HBM) for a in [*given, gate_weight, up_weight, down_weight]],
        [shape((2 * rows, width), bf16)] * chunk_count
        + [shape((top, tok_dev), jnp.int32)]
        + [shape((3 * hidden, width), bf16)] * 2,
        in_specs=[in_hbm] * 7,
        scratch_shapes=[pltpu.VMEM(a.shape, a.dtype) for a in given] + [pltpu.SemaphoreType.DMA((2 + 2 * blocks(tok_dev) + 6 * blocks(hidden),))],
    )

    along, across = (1, 2), (2, 1)
    near = [swap_by_core(first, along), swap_by_core(second, along)]
    far = swap_by_core(near[0], across)

    if chunk_count > 1:
        chunks = exchange(chunks)
    else:
        moved = chunks[0].reshape(2, experts, cap, width)
        moved = lax.all_to_all(moved, "ep", split_axis=1, concat_axis=1, tiled=True)
        chunks = [moved.reshape(2 * rows, width)]
    own = kernel_call(gather_kernel, chunks[::-1], [shape((slots, width), bf16)] * 2, flops=2 * 10**9)
    other = [swap(part, "rep", 1) for part in own]

    wide = width + LANES
    dx, grad_own, grad_near = kernel_call(
        early_kernel,
        [*own, *other, first, near[0]],
        [shape((2 * slots, wide), f32), shape((hidden, width), f32), shape((hidden, width), bf16)],
        flops=10**9,
    )
    dx, grad_near = kernel_call(
        middle_kernel,
        [*own, *other, dx, grad_near, near[1]],
        [shape((2 * slots, wide), f32), shape((2 * hidden, width), bf16)],
        flops=0,
    )
    parts = 2 if chunk_count % 2 == 0 else 1
    keep, *gives, grad_far = kernel_call(
        late_kernel,
        [*own, *other, dx, far],
        [shape((slots, wide), f32)]
        + [shape((slots // parts, wide), bf16)] * parts
        + [shape((hidden, width), bf16)],
    )
    folds = chunk_count > 1 and rows <= FOLD and width % FOLD == 0 and rows * width // FOLD % 8 == 0
    returned = shape((rows * width // FOLD + 8, FOLD) if folds else (rows, wide), bf16)
    back = []
    for i, give in enumerate(gives):
        sums = kernel_call(
            functools.partial(add_kernel, (parts - 1 - i) * slots // parts, rows),
            [keep, swap(give, "rep", 1)],
            [returned] * (chunk_count // parts),
        )
        back = [*sums, *back]
    if chunk_count > 1:
        back = exchange(back)
    else:
        moved = back[0].reshape(experts, cap, wide)
        moved = lax.all_to_all(moved, "ep", split_axis=0, concat_axis=0, tiled=True)
        back = [moved.reshape(rows, wide)]
    d_tokens, d_probs = kernel_call(
        functools.partial(combine_kernel, chunk_count, rows),
        back[::-1] + [slot, route_weight.T],
        [shape((tok_dev, width), bf16), shape((top, tok_dev), bf16)],
        flops=8 * 10**9,
    )

    arrived = swap_by_core(grad_near, along), swap_by_core(grad_far, (3, 3))
    (mine,) = kernel_call(grad_kernel, [grad_own, *arrived], [shape((2 * hidden, width), bf16)])
    results = [
        shape((1, 2 * hidden, width), f32),
        shape((tok_dev, width), bf16),
        shape((top, tok_dev), bf16),
    ]
    grad_total, d_tokens, d_probs = kernel_call(
        finish_kernel,
        [mine, swap(mine, "rep", 1), d_tokens, d_probs],
        results,
        out_specs=[in_hbm] * 3,
        scratch_shapes=[pltpu.VMEM((2 * hidden, width), f32), pltpu.SemaphoreType.DMA((2 + 2 * blocks(hidden),))],
    )
    return d_tokens, d_probs.T, grad_total


def solution(mesh):
    rows = P(("rep", "ep", "dp"), None)
    weights = P("ep", "dp", None)
    return jax.shard_map(
        local,
        mesh=mesh,
        in_specs=(rows,) * 4 + (weights,) * 3,
        out_specs=(rows, rows, weights),
        check_vma=False,
    )
```

```python
import functools

import jax
import jax.numpy as jnp
from jax import lax
from jax.experimental import pallas as pl
from jax.experimental.pallas import tpu as pltpu
from jax.sharding import PartitionSpec as P

LANES = 128
FOLD = 256
VMEM_BYTES = 32 * 1024 * 1024
f32, bf16 = jnp.float32, jnp.bfloat16


def dot(left, right, contract):
    return lax.dot_general(left, right, ((contract[0:1], contract[1:2]), ((), ())), preferred_element_type=f32)


def swap(value, axis, mask):
    return lax.ppermute(value, axis, [(i, i ^ mask) for i in range(lax.axis_size(axis))])


def exchange(chunks):
    return chunks[:1] + [swap(chunks[c], "ep", c) for c in range(1, len(chunks))]


def swap_by_core(value, masks):
    count = lax.axis_size("dp")
    pairs = [(r * count + i, r * count + (i ^ mask)) for r, mask in enumerate(masks) for i in range(count)]
    return lax.ppermute(value, ("rep", "dp"), pairs)


def kernel_call(body, inputs, outputs, flops=0, **kwargs):
    whole = pl.BlockSpec(memory_space=pltpu.VMEM)
    moved = sum(a.size * a.dtype.itemsize for a in inputs + outputs)
    return pl.pallas_call(
        body,
        out_shape=outputs,
        in_specs=kwargs.pop("in_specs", [whole] * len(inputs)),
        out_specs=kwargs.pop("out_specs", [whole] * len(outputs)),
        cost_estimate=pl.CostEstimate(flops=flops, bytes_accessed=moved, transcendentals=0),
        compiler_params=pltpu.CompilerParams(vmem_limit_bytes=VMEM_BYTES),
        **kwargs,
    )(*inputs)


def iota(shape, dim):
    return lax.broadcasted_iota(jnp.int32, shape, dim)


def dispatch_kernel(experts, cap, chunk_count, *refs):
    given, weights, refs = refs[:4], refs[4:7], refs[7:]
    chunks, (slot_out, *packed), (*held, sems) = refs[:chunk_count], refs[chunk_count:-5], refs[-5:]
    hidden = packed[0].shape[0] // 3
    rep = lax.axis_index("rep")
    loads = [pltpu.make_async_copy(*pair, sems.at[i]) for i, pair in enumerate(zip(given, held))]
    packs = []
    for j, half in enumerate((rep, 1 - rep)):
        rows = pl.ds(pl.multiple_of(half * hidden, hidden), hidden)
        packs += [
            pltpu.make_async_copy(weight.at[0, rows], packed[j].at[pl.ds(i * hidden, hidden)], sems.at[4 + 3 * j + i])
            for i, weight in enumerate(weights)
        ]
    for copy in loads + packs:
        copy.start()
    for copy in loads[:2]:
        copy.wait()

    ids, route_weight, tokens, upstream = held
    top, tok_dev = ids.shape
    rows = experts * cap // chunk_count
    me = lax.axis_index("ep")
    expert_of_row = iota((experts, tok_dev), 0)
    named = [(expert_of_row == ids[k : k + 1, :]).astype(f32) for k in range(top)]
    earlier = (iota((tok_dev, tok_dev), 0) < iota((tok_dev, tok_dev), 1)).astype(bf16)
    before = dot(sum(named).astype(bf16), earlier, (1, 0))
    row = iota((2 * experts * cap, tok_dev), 0)
    take_x = jnp.zeros(row.shape, f32)
    take_dy = jnp.zeros(row.shape, f32)
    scale = jnp.zeros(row.shape, f32)
    for k in range(top):
        rank = jnp.sum(before * named[k], axis=0, keepdims=True).astype(jnp.int32)
        expert = ids[k : k + 1, :]
        if chunk_count > 1:
            chunk = expert ^ me
            slot = chunk * cap + rank
            x_row = slot + chunk * cap
        else:
            slot = expert * cap + rank
            x_row = slot
        slot_out[k : k + 1, :] = slot
        here_x = (row == x_row).astype(f32)
        here_dy = (row == x_row + rows).astype(f32)
        take_x += here_x
        take_dy += here_dy
        scale += here_x + here_dy * route_weight[k : k + 1, :].astype(f32)
    scale = jnp.sum(scale, axis=1, keepdims=True)
    take_x, take_dy = take_x.astype(bf16), take_dy.astype(bf16)
    for copy in loads[2:]:
        copy.wait()
    picked = dot(take_x, tokens[...], (1, 0)) + dot(take_dy, upstream[...], (1, 0))
    picked = picked * scale
    for c in range(chunk_count):
        chunks[c][...] = picked[2 * rows * c : 2 * rows * (c + 1)].astype(bf16)
    for copy in packs:
        copy.wait()


def expert_math(x_rows, d_rows, pieces):
    hidden = pieces[0].shape[0] // 3
    gate, up, down = [[piece[i * hidden : (i + 1) * hidden] for piece in pieces] for i in range(3)]
    mixers = jnp.concatenate(gate + up)
    pre = dot(x_rows, mixers, (1, 1))
    d_act = dot(d_rows, jnp.concatenate(down), (1, 1))
    gate_pre, up_pre = pre[:, : hidden * len(pieces)], pre[:, hidden * len(pieces) :]
    sig = jax.nn.sigmoid(gate_pre)
    silu = gate_pre * sig
    act = silu * up_pre
    prob = jnp.sum(act * d_act, axis=1, keepdims=True)
    d_gate = d_act * up_pre * sig * (1.0 + gate_pre * (1.0 - sig))
    d_pre = jnp.concatenate([d_gate, d_act * silu], axis=1).astype(bf16)
    return d_pre, mixers, prob, dot(act.astype(bf16), d_rows, (0, 0))


def gather_kernel(*refs):
    *chunks, x_out, d_out = refs
    rows = chunks[0].shape[0] // 2
    values = [c[...].astype(f32) for c in reversed(chunks)]
    x_out[...] = jnp.concatenate([v[:rows] for v in values]).astype(bf16)
    d_out[...] = jnp.concatenate([v[rows:] for v in values]).astype(bf16)


def both_cores(x_own, d_own, x_other, d_other):
    return [jnp.concatenate([a[...], b[...]]) for a, b in ((x_own, x_other), (d_own, d_other))]


def early_kernel(*refs):
    *pieces, dx_out, grad_own, grad_near = refs[4:]
    d_pre, mixers, prob, grad = expert_math(*both_cores(*refs[:4]), pieces)
    width, hidden = mixers.shape[1], grad_own.shape[0]
    dx_out[:, :width] = dot(d_pre, mixers, (1, 0))
    dx_out[:, width:] = jnp.broadcast_to(prob, (prob.shape[0], LANES))
    grad_own[...] = grad[:hidden]
    grad_near[...] = grad[hidden:].astype(bf16)


def middle_kernel(*refs):
    grad_ref, piece, pre_out, prob_out, grad_out = refs[4:]
    pre_out[...], _, prob, grad = expert_math(*both_cores(*refs[:4]), [piece])
    hidden = grad.shape[0]
    prob_out[...] = jnp.broadcast_to(prob, prob_out.shape)
    grad_out[:hidden] = grad_ref[...]
    grad_out[hidden:] = grad.astype(bf16)


def late_kernel(*refs):
    dx_ref, pre_ref, prob_ref, near, far, keep, *gives, grad_far = refs[4:]
    d_pre, mixers, prob, grad = expert_math(*both_cores(*refs[:4]), [far])
    mixers = jnp.concatenate([near[: mixers.shape[0]], mixers])
    dx = dot(jnp.concatenate([pre_ref[...], d_pre], axis=1), mixers, (1, 0))
    prob = prob_ref[...] + prob
    width, slots = dx.shape[1], keep.shape[0]
    for side, value in ((slice(0, width), dx), (slice(width, None), prob)):
        total = value + dx_ref[:, side]
        keep[:, side] = total[:slots]
        for i, give in enumerate(reversed(gives)):
            rows = give.shape[0]
            give[:, side] = total[slots + rows * i : slots + rows * (i + 1)].astype(bf16)
    grad_far[...] = grad.astype(bf16)


def grad_kernel(own, near, far, out):
    hidden = own.shape[0]
    out[:hidden] = (own[...] + near[:hidden].astype(f32) + far[...].astype(f32)).astype(bf16)
    out[hidden:] = near[hidden:]


def finish_kernel(mine, theirs, tokens, probs, grad_out, tokens_out, probs_out, held, sems):
    hidden = mine.shape[0] // 2
    rep = lax.axis_index("rep")
    copies = [pltpu.make_async_copy(tokens, tokens_out, sems.at[0]), pltpu.make_async_copy(probs, probs_out, sems.at[1])]
    for copy in copies:
        copy.start()
    for i, half in enumerate((rep, 1 - rep)):
        here, there = slice(i * hidden, (i + 1) * hidden), slice((1 - i) * hidden, (2 - i) * hidden)
        rows = pl.ds(pl.multiple_of(half * hidden, hidden), hidden)
        held[i] = mine[here].astype(f32) + theirs[there].astype(f32)
        copies.append(pltpu.make_async_copy(held.at[i], grad_out.at[0, rows], sems.at[2 + i]))
        copies[-1].start()
    for copy in copies:
        copy.wait()


def add_kernel(start, rows, keep, got, *chunks):
    total = keep[start : start + got.shape[0]] + got[...].astype(f32)
    width = total.shape[1] - LANES
    for c, chunk in enumerate(chunks):
        value = total[c * rows : (c + 1) * rows]
        if chunk.shape[0] > rows:
            blocks = [value[:, i : i + FOLD] for i in range(0, width, FOLD)]
            diagonal = iota((rows, FOLD), 0) == iota((rows, FOLD), 1)
            prob = jnp.sum(jnp.where(diagonal, value[:, width : width + 1], 0.0), axis=0, keepdims=True)
            value = jnp.concatenate([*blocks, jnp.broadcast_to(prob, (8, FOLD))])
        chunk[...] = value.astype(bf16)


def combine_kernel(chunk_count, rows, *refs):
    chunks, (slot, route_weight, tokens_out, probs_out) = refs[:chunk_count], refs[chunk_count:]
    tok_dev, width = tokens_out.shape
    top = slot.shape[0]
    total = 0.0
    probs = [0.0] * top
    for c, place in enumerate(reversed(range(chunk_count))):
        slot_of_row = iota((rows, tok_dev), 0) + place * rows
        hits = [(slot_of_row == slot[k : k + 1, :]).astype(f32) for k in range(top)]
        value = chunks[c][...].astype(f32)
        if value.shape[0] > rows:
            blocks = [value[i : i + rows] for i in range(0, width // FOLD * rows, rows)]
            diagonal = iota((rows, FOLD), 0) == iota((rows, FOLD), 1)
            prob = value[width // FOLD * rows :][:1]
            prob = jnp.sum(jnp.where(diagonal, prob, 0.0), axis=1, keepdims=True)
            value = jnp.concatenate(blocks, axis=1)
        else:
            prob = value[:, width : width + 1]
        total = total + dot(sum(hits).astype(bf16), value[:, :width].astype(bf16), (0, 0))
        for k in range(top):
            probs[k] = probs[k] + jnp.sum(hits[k] * prob, axis=0, keepdims=True)
    tokens_out[...] = total.astype(bf16)
    for k in range(top):
        probs_out[k : k + 1, :] = (probs[k] / route_weight[k : k + 1, :].astype(f32)).astype(bf16)


def local(tokens, upstream, expert_ids, route_weight, gate_weight, up_weight, down_weight):
    tok_dev, width = tokens.shape
    top = expert_ids.shape[1]
    experts, reps = lax.axis_size("ep"), lax.axis_size("rep")
    cap = 2 * ((5 * tok_dev * top + 8 * experts - 1) // (8 * experts))
    slots = experts * cap
    chunk_count = experts if experts <= 8 else 1
    rows = slots // chunk_count
    hidden = gate_weight.shape[1] // reps
    shape = jax.ShapeDtypeStruct
    in_hbm = pl.BlockSpec(memory_space=pltpu.HBM)

    given = [expert_ids.T, route_weight.T, tokens, upstream]
    *chunks, slot, first, second = kernel_call(
        functools.partial(dispatch_kernel, experts, cap, chunk_count),
        [pltpu.with_memory_space_constraint(a, pltpu.HBM) for a in [*given, gate_weight, up_weight, down_weight]],
        [shape((2 * rows, width), bf16)] * chunk_count
        + [shape((top, tok_dev), jnp.int32)]
        + [shape((3 * hidden, width), bf16)] * 2,
        in_specs=[in_hbm] * 7,
        scratch_shapes=[pltpu.VMEM(a.shape, a.dtype) for a in given] + [pltpu.SemaphoreType.DMA((10,))],
    )

    along, across = (1, 2), (2, 1)
    near = [swap_by_core(first, along), swap_by_core(second, along)]
    far = swap_by_core(near[0], across)

    if chunk_count > 1:
        chunks = exchange(chunks)
    else:
        moved = chunks[0].reshape(2, experts, cap, width)
        moved = lax.all_to_all(moved, "ep", split_axis=1, concat_axis=1, tiled=True)
        chunks = [moved.reshape(2 * rows, width)]
    own = kernel_call(gather_kernel, chunks[::-1], [shape((slots, width), bf16)] * 2, flops=2 * 10**9)
    other = [swap(part, "rep", 1) for part in own]

    wide = width + LANES
    dx, grad_own, grad_near = kernel_call(
        early_kernel,
        [*own, *other, first, near[0]],
        [shape((2 * slots, wide), f32), shape((hidden, width), f32), shape((hidden, width), bf16)],
        flops=10**9,
    )
    d_pre, prob, grad_near = kernel_call(
        middle_kernel,
        [*own, *other, grad_near, near[1]],
        [
            shape((2 * slots, 2 * hidden), bf16),
            shape((2 * slots, LANES), f32),
            shape((2 * hidden, width), bf16),
        ],
        flops=0,
    )
    parts = 2 if chunk_count % 2 == 0 else 1
    keep, *gives, grad_far = kernel_call(
        late_kernel,
        [*own, *other, dx, d_pre, prob, near[1], far],
        [shape((slots, wide), f32)]
        + [shape((slots // parts, wide), bf16)] * parts
        + [shape((hidden, width), bf16)],
    )
    folds = chunk_count > 1 and rows <= FOLD and width % FOLD == 0 and rows * width // FOLD % 8 == 0
    returned = shape((rows * width // FOLD + 8, FOLD) if folds else (rows, wide), bf16)
    back = []
    for i, give in enumerate(gives):
        sums = kernel_call(
            functools.partial(add_kernel, (parts - 1 - i) * slots // parts, rows),
            [keep, swap(give, "rep", 1)],
            [returned] * (chunk_count // parts),
        )
        back = [*sums, *back]
    if chunk_count > 1:
        back = exchange(back)
    else:
        moved = back[0].reshape(experts, cap, wide)
        moved = lax.all_to_all(moved, "ep", split_axis=0, concat_axis=0, tiled=True)
        back = [moved.reshape(rows, wide)]
    d_tokens, d_probs = kernel_call(
        functools.partial(combine_kernel, chunk_count, rows),
        back[::-1] + [slot, route_weight.T],
        [shape((tok_dev, width), bf16), shape((top, tok_dev), bf16)],
        flops=8 * 10**9,
    )

    arrived = swap_by_core(grad_near, along), swap_by_core(grad_far, (3, 3))
    (mine,) = kernel_call(grad_kernel, [grad_own, *arrived], [shape((2 * hidden, width), bf16)])
    results = [
        shape((1, 2 * hidden, width), f32),
        shape((tok_dev, width), bf16),
        shape((top, tok_dev), bf16),
    ]
    grad_total, d_tokens, d_probs = kernel_call(
        finish_kernel,
        [mine, swap(mine, "rep", 1), d_tokens, d_probs],
        results,
        out_specs=[in_hbm] * 3,
        scratch_shapes=[pltpu.VMEM((2, hidden, width), f32), pltpu.SemaphoreType.DMA((4,))],
    )
    return d_tokens, d_probs.T, grad_total


def solution(mesh):
    rows = P(("rep", "ep", "dp"), None)
    weights = P("ep", "dp", None)
    return jax.shard_map(
        local,
        mesh=mesh,
        in_specs=(rows,) * 4 + (weights,) * 3,
        out_specs=(rows, rows, weights),
        check_vma=False,
    )
```

```python
import functools

import jax
import jax.numpy as jnp
from jax import lax
from jax.experimental import pallas as pl
from jax.experimental.pallas import tpu as pltpu
from jax.sharding import PartitionSpec as P

LANES = 128
FOLD = 256
VMEM_BYTES = 32 * 1024 * 1024
f32, bf16 = jnp.float32, jnp.bfloat16


def dot(left, right, contract):
    return lax.dot_general(left, right, ((contract[0:1], contract[1:2]), ((), ())), preferred_element_type=f32)


def swap(value, axis, mask):
    return lax.ppermute(value, axis, [(i, i ^ mask) for i in range(lax.axis_size(axis))])


def exchange(chunks):
    return chunks[:1] + [swap(chunks[c], "ep", c) for c in range(1, len(chunks))]


def swap_by_core(value, masks):
    count = lax.axis_size("dp")
    pairs = [(r * count + i, r * count + (i ^ mask)) for r, mask in enumerate(masks) for i in range(count)]
    return lax.ppermute(value, ("rep", "dp"), pairs)


def kernel_call(body, inputs, outputs, flops=0, **kwargs):
    whole = pl.BlockSpec(memory_space=pltpu.VMEM)
    moved = sum(a.size * a.dtype.itemsize for a in inputs + outputs)
    return pl.pallas_call(
        body,
        out_shape=outputs,
        in_specs=kwargs.pop("in_specs", [whole] * len(inputs)),
        out_specs=kwargs.pop("out_specs", [whole] * len(outputs)),
        cost_estimate=pl.CostEstimate(flops=flops, bytes_accessed=moved, transcendentals=0),
        compiler_params=pltpu.CompilerParams(vmem_limit_bytes=VMEM_BYTES),
        **kwargs,
    )(*inputs)


def iota(shape, dim):
    return lax.broadcasted_iota(jnp.int32, shape, dim)


def dispatch_kernel(experts, cap, chunk_count, *refs):
    given, weights, refs = refs[:4], refs[4:7], refs[7:]
    chunks, (slot_out, weight_out, *packed), (*held, sems) = refs[:chunk_count], refs[chunk_count:-5], refs[-5:]
    hidden = packed[0].shape[0] // 3
    rep = lax.axis_index("rep")
    loads = [pltpu.make_async_copy(*pair, sems.at[i]) for i, pair in enumerate(zip(given, held))]
    packs = []
    for j, half in enumerate((rep, 1 - rep)):
        rows = pl.ds(pl.multiple_of(half * hidden, hidden), hidden)
        packs += [
            pltpu.make_async_copy(weight.at[0, rows], packed[j].at[pl.ds(i * hidden, hidden)], sems.at[4 + 3 * j + i])
            for i, weight in enumerate(weights)
        ]
    for copy in loads + packs:
        copy.start()
    for copy in loads[:2]:
        copy.wait()

    ids, route_weight, tokens, upstream = held
    top, tok_dev = ids.shape
    weight_out[...] = route_weight[...].astype(f32)
    rows = experts * cap // chunk_count
    me = lax.axis_index("ep")
    expert_of_row = iota((experts, tok_dev), 0)
    named = [(expert_of_row == ids[k : k + 1, :]).astype(f32) for k in range(top)]
    earlier = (iota((tok_dev, tok_dev), 0) < iota((tok_dev, tok_dev), 1)).astype(bf16)
    before = dot(sum(named).astype(bf16), earlier, (1, 0))
    row = iota((2 * experts * cap, tok_dev), 0)
    take_x = jnp.zeros(row.shape, f32)
    take_dy = jnp.zeros(row.shape, f32)
    scale = jnp.zeros(row.shape, f32)
    for k in range(top):
        rank = jnp.sum(before * named[k], axis=0, keepdims=True).astype(jnp.int32)
        expert = ids[k : k + 1, :]
        if chunk_count > 1:
            chunk = expert ^ me
            slot = chunk * cap + rank
            x_row = slot + chunk * cap
        else:
            slot = expert * cap + rank
            x_row = slot
        slot_out[k : k + 1, :] = slot
        here_x = (row == x_row).astype(f32)
        here_dy = (row == x_row + rows).astype(f32)
        take_x += here_x
        take_dy += here_dy
        scale += here_x + here_dy * route_weight[k : k + 1, :].astype(f32)
    scale = jnp.sum(scale, axis=1, keepdims=True)
    take_x, take_dy = take_x.astype(bf16), take_dy.astype(bf16)
    for copy in loads[2:]:
        copy.wait()
    picked = dot(take_x, tokens[...], (1, 0)) + dot(take_dy, upstream[...], (1, 0))
    picked = picked * scale
    for c in range(chunk_count):
        chunks[c][...] = picked[2 * rows * c : 2 * rows * (c + 1)].astype(bf16)
    for copy in packs:
        copy.wait()


def expert_math(x_rows, d_rows, pieces):
    hidden = pieces[0].shape[0] // 3
    gate, up, down = [[piece[i * hidden : (i + 1) * hidden] for piece in pieces] for i in range(3)]
    mixers = jnp.concatenate(gate + up)
    pre = dot(x_rows, mixers, (1, 1))
    d_act = dot(d_rows, jnp.concatenate(down), (1, 1))
    gate_pre, up_pre = pre[:, : hidden * len(pieces)], pre[:, hidden * len(pieces) :]
    sig = jax.nn.sigmoid(gate_pre)
    silu = gate_pre * sig
    act = silu * up_pre
    prob = jnp.sum(act * d_act, axis=1, keepdims=True)
    d_gate = d_act * up_pre * sig * (1.0 + gate_pre * (1.0 - sig))
    d_pre = jnp.concatenate([d_gate, d_act * silu], axis=1).astype(bf16)
    return d_pre, mixers, prob, dot(act.astype(bf16), d_rows, (0, 0))


def gather_kernel(*refs):
    *chunks, x_out, d_out = refs
    rows = chunks[0].shape[0] // 2
    values = [c[...].astype(f32) for c in reversed(chunks)]
    x_out[...] = jnp.concatenate([v[:rows] for v in values]).astype(bf16)
    d_out[...] = jnp.concatenate([v[rows:] for v in values]).astype(bf16)


def both_cores(x_own, d_own, x_other, d_other):
    return [jnp.concatenate([a[...], b[...]]) for a, b in ((x_own, x_other), (d_own, d_other))]


def early_kernel(*refs):
    *pieces, dx_out, grad_own, grad_near = refs[4:]
    d_pre, mixers, prob, grad = expert_math(*both_cores(*refs[:4]), pieces)
    width, hidden = mixers.shape[1], grad_own.shape[0]
    dx_out[:, :width] = dot(d_pre, mixers, (1, 0))
    dx_out[:, width:] = jnp.broadcast_to(prob, (prob.shape[0], LANES))
    grad_own[...] = grad[:hidden]
    grad_near[...] = grad[hidden:].astype(bf16)


def middle_kernel(*refs):
    grad_ref, piece, pre_out, prob_out, grad_out = refs[4:]
    pre_out[...], _, prob, grad = expert_math(*both_cores(*refs[:4]), [piece])
    hidden = grad.shape[0]
    prob_out[...] = jnp.broadcast_to(prob, prob_out.shape)
    grad_out[:hidden] = grad_ref[...]
    grad_out[hidden:] = grad.astype(bf16)


def late_kernel(*refs):
    dx_ref, pre_ref, prob_ref, near, far, keep, *gives, grad_far = refs[4:]
    d_pre, mixers, prob, grad = expert_math(*both_cores(*refs[:4]), [far])
    mixers = jnp.concatenate([near[: mixers.shape[0]], mixers])
    dx = dot(jnp.concatenate([pre_ref[...], d_pre], axis=1), mixers, (1, 0))
    prob = prob_ref[...] + prob
    width, slots = dx.shape[1], keep.shape[0]
    for side, value in ((slice(0, width), dx), (slice(width, None), prob)):
        total = value + dx_ref[:, side]
        keep[:, side] = total[:slots]
        for i, give in enumerate(reversed(gives)):
            rows = give.shape[0]
            give[:, side] = total[slots + rows * i : slots + rows * (i + 1)].astype(bf16)
    grad_far[...] = grad.astype(bf16)


def grad_kernel(own, near, far, out):
    hidden = own.shape[0]
    out[:hidden] = (own[...] + near[:hidden].astype(f32) + far[...].astype(f32)).astype(bf16)
    out[hidden:] = near[hidden:]


def add_kernel(start, rows, keep, got, *chunks):
    total = keep[start : start + got.shape[0]] + got[...].astype(f32)
    width = total.shape[1] - LANES
    for c, chunk in enumerate(chunks):
        value = total[c * rows : (c + 1) * rows]
        if chunk.shape[0] > rows:
            blocks = [value[:, i : i + FOLD] for i in range(0, width, FOLD)]
            diagonal = iota((rows, FOLD), 0) == iota((rows, FOLD), 1)
            prob = jnp.sum(jnp.where(diagonal, value[:, width : width + 1], 0.0), axis=0, keepdims=True)
            value = jnp.concatenate([*blocks, jnp.broadcast_to(prob, (8, FOLD))])
        chunk[...] = value.astype(bf16)


def combine(chunks, rows, slot, route_weight, tokens_out, probs_out):
    tok_dev, width = tokens_out.shape
    top = slot.shape[0]
    total = 0.0
    probs = [0.0] * top
    for c, place in enumerate(reversed(range(len(chunks)))):
        slot_of_row = iota((rows, tok_dev), 0) + place * rows
        hits = [(slot_of_row == slot[k : k + 1, :]).astype(f32) for k in range(top)]
        value = chunks[c][...].astype(f32)
        if value.shape[0] > rows:
            blocks = [value[i : i + rows] for i in range(0, width // FOLD * rows, rows)]
            diagonal = iota((rows, FOLD), 0) == iota((rows, FOLD), 1)
            prob = value[width // FOLD * rows :][:1]
            prob = jnp.sum(jnp.where(diagonal, prob, 0.0), axis=1, keepdims=True)
            value = jnp.concatenate(blocks, axis=1)
        else:
            prob = value[:, width : width + 1]
        total = total + dot(sum(hits).astype(bf16), value[:, :width].astype(bf16), (0, 0))
        for k in range(top):
            probs[k] = probs[k] + jnp.sum(hits[k] * prob, axis=0, keepdims=True)
    tokens_out[...] = total.astype(bf16)
    for k in range(top):
        probs_out[k : k + 1, :] = (probs[k] / route_weight[k : k + 1, :]).astype(bf16)


def pass_kernel(*refs):
    pass


def finish_kernel(chunk_count, rows_of_chunk, *refs):
    chunks, (slot, route_weight, mine, theirs, *refs) = refs[:chunk_count], refs[chunk_count:]
    grad_out, tokens_out, probs_out, held, tokens, probs, sems = refs
    hidden = mine.shape[0] // 2
    rep = lax.axis_index("rep")
    copies = []
    for i, half in enumerate((rep, 1 - rep)):
        here, there = slice(i * hidden, (i + 1) * hidden), slice((1 - i) * hidden, (2 - i) * hidden)
        rows = pl.ds(pl.multiple_of(half * hidden, hidden), hidden)
        held[i] = mine[here].astype(f32) + theirs[there].astype(f32)
        copies.append(pltpu.make_async_copy(held.at[i], grad_out.at[0, rows], sems.at[i]))
        copies[-1].start()
    combine(chunks, rows_of_chunk, slot, route_weight, tokens, probs)
    for i, pair in enumerate(((tokens, tokens_out), (probs, probs_out))):
        copies.append(pltpu.make_async_copy(*pair, sems.at[2 + i]))
        copies[-1].start()
    for copy in copies:
        copy.wait()


def local(tokens, upstream, expert_ids, route_weight, gate_weight, up_weight, down_weight):
    tok_dev, width = tokens.shape
    top = expert_ids.shape[1]
    experts, reps = lax.axis_size("ep"), lax.axis_size("rep")
    cap = 2 * ((5 * tok_dev * top + 8 * experts - 1) // (8 * experts))
    slots = experts * cap
    chunk_count = experts if experts <= 8 else 1
    rows = slots // chunk_count
    hidden = gate_weight.shape[1] // reps
    shape = jax.ShapeDtypeStruct
    in_hbm = pl.BlockSpec(memory_space=pltpu.HBM)

    given = [expert_ids.T, route_weight.T, tokens, upstream]
    *chunks, slot, weight, first, second = kernel_call(
        functools.partial(dispatch_kernel, experts, cap, chunk_count),
        [pltpu.with_memory_space_constraint(a, pltpu.HBM) for a in [*given, gate_weight, up_weight, down_weight]],
        [shape((2 * rows, width), bf16)] * chunk_count
        + [shape((top, tok_dev), jnp.int32), shape((top, tok_dev), f32)]
        + [shape((3 * hidden, width), bf16)] * 2,
        in_specs=[in_hbm] * 7,
        scratch_shapes=[pltpu.VMEM(a.shape, a.dtype) for a in given] + [pltpu.SemaphoreType.DMA((10,))],
    )

    along, across = (1, 2), (2, 1)
    near = [swap_by_core(first, along), swap_by_core(second, along)]
    far = swap_by_core(near[0], across)

    if chunk_count > 1:
        chunks = exchange(chunks)
    else:
        moved = chunks[0].reshape(2, experts, cap, width)
        moved = lax.all_to_all(moved, "ep", split_axis=1, concat_axis=1, tiled=True)
        chunks = [moved.reshape(2 * rows, width)]
    own = kernel_call(gather_kernel, chunks[::-1], [shape((slots, width), bf16)] * 2, flops=2 * 10**9)
    other = [swap(part, "rep", 1) for part in own]

    wide = width + LANES
    dx, grad_own, grad_near = kernel_call(
        early_kernel,
        [*own, *other, first, near[0]],
        [shape((2 * slots, wide), f32), shape((hidden, width), f32), shape((hidden, width), bf16)],
        flops=10**9,
    )
    d_pre, prob, grad_near = kernel_call(
        middle_kernel,
        [*own, *other, grad_near, near[1]],
        [
            shape((2 * slots, 2 * hidden), bf16),
            shape((2 * slots, LANES), f32),
            shape((2 * hidden, width), bf16),
        ],
        flops=0,
    )
    parts = 2 if chunk_count % 2 == 0 else 1
    keep, *gives, grad_far = kernel_call(
        late_kernel,
        [*own, *other, dx, d_pre, prob, near[1], far],
        [shape((slots, wide), f32)]
        + [shape((slots // parts, wide), bf16)] * parts
        + [shape((hidden, width), bf16)],
    )
    folds = chunk_count > 1 and rows <= FOLD and width % FOLD == 0 and rows * width // FOLD % 8 == 0
    returned = shape((rows * width // FOLD + 8, FOLD) if folds else (rows, wide), bf16)
    back = []
    for i, give in enumerate(gives):
        sums = kernel_call(
            functools.partial(add_kernel, (parts - 1 - i) * slots // parts, rows),
            [keep, swap(give, "rep", 1)],
            [returned] * (chunk_count // parts),
        )
        back = [*sums, *back]
    if chunk_count > 1:
        back = exchange(back)
    else:
        moved = back[0].reshape(experts, cap, wide)
        moved = lax.all_to_all(moved, "ep", split_axis=0, concat_axis=0, tiled=True)
        back = [moved.reshape(rows, wide)]
    back = kernel_call(
        pass_kernel,
        back[::-1],
        [shape(b.shape, b.dtype) for b in back],
        flops=8 * 10**9,
        input_output_aliases={i: i for i in range(len(back))},
    )
    arrived = swap_by_core(grad_near, along), swap_by_core(grad_far, (3, 3))
    (mine,) = kernel_call(grad_kernel, [grad_own, *arrived], [shape((2 * hidden, width), bf16)])
    results = [
        shape((1, 2 * hidden, width), f32),
        shape((tok_dev, width), bf16),
        shape((top, tok_dev), bf16),
    ]
    grad_total, d_tokens, d_probs = kernel_call(
        functools.partial(finish_kernel, chunk_count, rows),
        [*back, slot, weight, mine, swap(mine, "rep", 1)],
        results,
        out_specs=[in_hbm] * 3,
        scratch_shapes=[
            pltpu.VMEM((2, hidden, width), f32),
            *(pltpu.VMEM(result.shape, result.dtype) for result in results[1:]),
            pltpu.SemaphoreType.DMA((4,)),
        ],
    )
    return d_tokens, d_probs.T, grad_total


def solution(mesh):
    rows = P(("rep", "ep", "dp"), None)
    weights = P("ep", "dp", None)
    return jax.shard_map(
        local,
        mesh=mesh,
        in_specs=(rows,) * 4 + (weights,) * 3,
        out_specs=(rows, rows, weights),
        check_vma=False,
    )
```

```python
import functools

import jax
import jax.numpy as jnp
from jax import lax
from jax.experimental import pallas as pl
from jax.experimental.pallas import tpu as pltpu
from jax.sharding import PartitionSpec as P

LANES = 128
FOLD = 256
VMEM_BYTES = 32 * 1024 * 1024
f32, bf16 = jnp.float32, jnp.bfloat16


def dot(left, right, contract):
    return lax.dot_general(left, right, ((contract[0:1], contract[1:2]), ((), ())), preferred_element_type=f32)


def swap(value, axis, mask):
    return lax.ppermute(value, axis, [(i, i ^ mask) for i in range(lax.axis_size(axis))])


def exchange(chunks):
    return chunks[:1] + [swap(chunks[c], "ep", c) for c in range(1, len(chunks))]


def swap_by_core(value, masks):
    count = lax.axis_size("dp")
    pairs = [(r * count + i, r * count + (i ^ mask)) for r, mask in enumerate(masks) for i in range(count)]
    return lax.ppermute(value, ("rep", "dp"), pairs)


def kernel_call(body, inputs, outputs, flops=0, **kwargs):
    whole = pl.BlockSpec(memory_space=pltpu.VMEM)
    moved = sum(a.size * a.dtype.itemsize for a in inputs + outputs)
    return pl.pallas_call(
        body,
        out_shape=outputs,
        in_specs=kwargs.pop("in_specs", [whole] * len(inputs)),
        out_specs=kwargs.pop("out_specs", [whole] * len(outputs)),
        cost_estimate=pl.CostEstimate(flops=flops, bytes_accessed=moved, transcendentals=0),
        compiler_params=pltpu.CompilerParams(vmem_limit_bytes=VMEM_BYTES),
        **kwargs,
    )(*inputs)


def iota(shape, dim):
    return lax.broadcasted_iota(jnp.int32, shape, dim)


def dispatch_kernel(experts, cap, chunk_count, *refs):
    given, weights, refs = refs[:4], refs[4:7], refs[7:]
    chunks, (slot_out, weight_out, *packed), (ids, route_weight, both, sems) = refs[:chunk_count], refs[chunk_count:-4], refs[-4:]
    hidden = packed[0].shape[0] // 3
    rep = lax.axis_index("rep")
    top, tok_dev = ids.shape
    held = (ids, route_weight, both.at[pl.ds(0, tok_dev)], both.at[pl.ds(tok_dev, tok_dev)])
    loads = [pltpu.make_async_copy(*pair, sems.at[i]) for i, pair in enumerate(zip(given, held))]
    packs = []
    for j, half in enumerate((rep, 1 - rep)):
        rows = pl.ds(pl.multiple_of(half * hidden, hidden), hidden)
        packs += [
            pltpu.make_async_copy(weight.at[0, rows], packed[j].at[pl.ds(i * hidden, hidden)], sems.at[4 + 3 * j + i])
            for i, weight in enumerate(weights)
        ]
    for copy in loads + packs:
        copy.start()
    for copy in loads[:2]:
        copy.wait()

    weight_out[...] = route_weight[...].astype(f32)
    rows = experts * cap // chunk_count
    me = lax.axis_index("ep")
    expert_of_row = iota((experts, tok_dev), 0)
    named = [(expert_of_row == ids[k : k + 1, :]).astype(f32) for k in range(top)]
    earlier = (iota((tok_dev, tok_dev), 0) < iota((tok_dev, tok_dev), 1)).astype(bf16)
    before = dot(sum(named).astype(bf16), earlier, (1, 0))
    row = iota((2 * experts * cap, 2 * tok_dev), 0)
    take = jnp.zeros(row.shape, f32)
    scale = jnp.zeros(row.shape, f32)
    for k in range(top):
        rank = jnp.sum(before * named[k], axis=0, keepdims=True).astype(jnp.int32)
        expert = ids[k : k + 1, :]
        if chunk_count > 1:
            chunk = expert ^ me
            slot = chunk * cap + rank
            x_row = slot + chunk * cap
        else:
            slot = expert * cap + rank
            x_row = slot
        slot_out[k : k + 1, :] = slot
        weight = route_weight[k : k + 1, :].astype(f32)
        here = (row == jnp.concatenate([x_row, x_row + rows], axis=1)).astype(f32)
        take += here
        scale += here * jnp.concatenate([jnp.ones_like(weight), weight], axis=1)
    scale = jnp.sum(scale, axis=1, keepdims=True)
    take = take.astype(bf16)
    for copy in loads[2:]:
        copy.wait()
    picked = dot(take, both[...], (1, 0)) * scale
    for c in range(chunk_count):
        chunks[c][...] = picked[2 * rows * c : 2 * rows * (c + 1)].astype(bf16)
    for copy in packs:
        copy.wait()


def expert_math(x_rows, d_rows, pieces):
    hidden = pieces[0].shape[0] // 3
    gate, up, down = [[piece[i * hidden : (i + 1) * hidden] for piece in pieces] for i in range(3)]
    mixers = jnp.concatenate(gate + up)
    pre = dot(x_rows, mixers, (1, 1))
    d_act = dot(d_rows, jnp.concatenate(down), (1, 1))
    gate_pre, up_pre = pre[:, : hidden * len(pieces)], pre[:, hidden * len(pieces) :]
    sig = jax.nn.sigmoid(gate_pre)
    silu = gate_pre * sig
    act = silu * up_pre
    prob = jnp.sum(act * d_act, axis=1, keepdims=True)
    d_gate = d_act * up_pre * sig * (1.0 + gate_pre * (1.0 - sig))
    d_pre = jnp.concatenate([d_gate, d_act * silu], axis=1).astype(bf16)
    return d_pre, mixers, prob, dot(act.astype(bf16), d_rows, (0, 0))


def gather_kernel(*refs):
    *chunks, x_out, d_out = refs
    rows = chunks[0].shape[0] // 2
    values = [c[...].astype(f32) for c in reversed(chunks)]
    x_out[...] = jnp.concatenate([v[:rows] for v in values]).astype(bf16)
    d_out[...] = jnp.concatenate([v[rows:] for v in values]).astype(bf16)


def both_cores(x_own, d_own, x_other, d_other):
    return [jnp.concatenate([a[...], b[...]]) for a, b in ((x_own, x_other), (d_own, d_other))]


def early_kernel(*refs):
    *pieces, dx_out, grad_own, grad_near = refs[4:]
    d_pre, mixers, prob, grad = expert_math(*both_cores(*refs[:4]), pieces)
    width, hidden = mixers.shape[1], grad_own.shape[0]
    dx_out[:, :width] = dot(d_pre, mixers, (1, 0))
    dx_out[:, width:] = jnp.broadcast_to(prob, (prob.shape[0], LANES))
    grad_own[...] = grad[:hidden]
    grad_near[...] = grad[hidden:].astype(bf16)


def middle_kernel(*refs):
    grad_ref, piece, pre_out, prob_out, grad_out = refs[4:]
    pre_out[...], _, prob, grad = expert_math(*both_cores(*refs[:4]), [piece])
    hidden = grad.shape[0]
    prob_out[...] = jnp.broadcast_to(prob, prob_out.shape)
    grad_out[:hidden] = grad_ref[...]
    grad_out[hidden:] = grad.astype(bf16)


def late_kernel(*refs):
    dx_ref, pre_ref, prob_ref, near, far, keep, *gives, grad_far = refs[4:]
    d_pre, mixers, prob, grad = expert_math(*both_cores(*refs[:4]), [far])
    mixers = jnp.concatenate([near[: mixers.shape[0]], mixers])
    dx = dot(jnp.concatenate([pre_ref[...], d_pre], axis=1), mixers, (1, 0))
    prob = prob_ref[...] + prob
    width, slots = dx.shape[1], keep.shape[0]
    for side, value in ((slice(0, width), dx), (slice(width, None), prob)):
        total = value + dx_ref[:, side]
        keep[:, side] = total[:slots]
        for i, give in enumerate(reversed(gives)):
            rows = give.shape[0]
            give[:, side] = total[slots + rows * i : slots + rows * (i + 1)].astype(bf16)
    grad_far[...] = grad.astype(bf16)


def grad_kernel(own, near, far, out):
    hidden = own.shape[0]
    out[:hidden] = (own[...] + near[:hidden].astype(f32) + far[...].astype(f32)).astype(bf16)
    out[hidden:] = near[hidden:]


def add_kernel(start, rows, keep, got, *chunks):
    total = keep[start : start + got.shape[0]] + got[...].astype(f32)
    width = total.shape[1] - LANES
    for c, chunk in enumerate(chunks):
        value = total[c * rows : (c + 1) * rows]
        if chunk.shape[0] > rows:
            blocks = [value[:, i : i + FOLD] for i in range(0, width, FOLD)]
            diagonal = iota((rows, FOLD), 0) == iota((rows, FOLD), 1)
            prob = jnp.sum(jnp.where(diagonal, value[:, width : width + 1], 0.0), axis=0, keepdims=True)
            value = jnp.concatenate([*blocks, jnp.broadcast_to(prob, (8, FOLD))])
        chunk[...] = value.astype(bf16)


def combine(chunks, rows, slot, route_weight, tokens_out, probs_out):
    tok_dev, width = tokens_out.shape
    top = slot.shape[0]
    total = 0.0
    probs = [0.0] * top
    for c, place in enumerate(reversed(range(len(chunks)))):
        slot_of_row = iota((rows, tok_dev), 0) + place * rows
        hits = [(slot_of_row == slot[k : k + 1, :]).astype(f32) for k in range(top)]
        value = chunks[c][...].astype(f32)
        if value.shape[0] > rows:
            blocks = [value[i : i + rows] for i in range(0, width // FOLD * rows, rows)]
            diagonal = iota((rows, FOLD), 0) == iota((rows, FOLD), 1)
            prob = value[width // FOLD * rows :][:1]
            prob = jnp.sum(jnp.where(diagonal, prob, 0.0), axis=1, keepdims=True)
            value = jnp.concatenate(blocks, axis=1)
        else:
            prob = value[:, width : width + 1]
        total = total + dot(sum(hits).astype(bf16), value[:, :width].astype(bf16), (0, 0))
        for k in range(top):
            probs[k] = probs[k] + jnp.sum(hits[k] * prob, axis=0, keepdims=True)
    tokens_out[...] = total.astype(bf16)
    for k in range(top):
        probs_out[k : k + 1, :] = (probs[k] / route_weight[k : k + 1, :]).astype(bf16)


def pass_kernel(*refs):
    pass


def finish_kernel(chunk_count, rows_of_chunk, *refs):
    chunks, (slot, route_weight, mine, theirs, *refs) = refs[:chunk_count], refs[chunk_count:]
    grad_out, tokens_out, probs_out, held, tokens, probs, sems = refs
    hidden = mine.shape[0] // 2
    rep = lax.axis_index("rep")
    copies = []
    for i, half in enumerate((rep, 1 - rep)):
        here, there = slice(i * hidden, (i + 1) * hidden), slice((1 - i) * hidden, (2 - i) * hidden)
        rows = pl.ds(pl.multiple_of(half * hidden, hidden), hidden)
        held[i] = mine[here].astype(f32) + theirs[there].astype(f32)
        copies.append(pltpu.make_async_copy(held.at[i], grad_out.at[0, rows], sems.at[i]))
        copies[-1].start()
    combine(chunks, rows_of_chunk, slot, route_weight, tokens, probs)
    for i, pair in enumerate(((tokens, tokens_out), (probs, probs_out))):
        copies.append(pltpu.make_async_copy(*pair, sems.at[2 + i]))
        copies[-1].start()
    for copy in copies:
        copy.wait()


def local(tokens, upstream, expert_ids, route_weight, gate_weight, up_weight, down_weight):
    tok_dev, width = tokens.shape
    top = expert_ids.shape[1]
    experts, reps = lax.axis_size("ep"), lax.axis_size("rep")
    cap = 2 * ((5 * tok_dev * top + 8 * experts - 1) // (8 * experts))
    slots = experts * cap
    chunk_count = experts if experts <= 8 else 1
    rows = slots // chunk_count
    hidden = gate_weight.shape[1] // reps
    shape = jax.ShapeDtypeStruct
    in_hbm = pl.BlockSpec(memory_space=pltpu.HBM)

    given = [expert_ids.T, route_weight.T, tokens, upstream]
    *chunks, slot, weight, first, second = kernel_call(
        functools.partial(dispatch_kernel, experts, cap, chunk_count),
        [pltpu.with_memory_space_constraint(a, pltpu.HBM) for a in [*given, gate_weight, up_weight, down_weight]],
        [shape((2 * rows, width), bf16)] * chunk_count
        + [shape((top, tok_dev), jnp.int32), shape((top, tok_dev), f32)]
        + [shape((3 * hidden, width), bf16)] * 2,
        in_specs=[in_hbm] * 7,
        scratch_shapes=[
            *(pltpu.VMEM(a.shape, a.dtype) for a in given[:2]),
            pltpu.VMEM((2 * tok_dev, width), bf16),
            pltpu.SemaphoreType.DMA((10,)),
        ],
    )

    along, across = (1, 2), (2, 1)
    near = [swap_by_core(first, along), swap_by_core(second, along)]
    far = swap_by_core(near[0], across)

    if chunk_count > 1:
        chunks = exchange(chunks)
    else:
        moved = chunks[0].reshape(2, experts, cap, width)
        moved = lax.all_to_all(moved, "ep", split_axis=1, concat_axis=1, tiled=True)
        chunks = [moved.reshape(2 * rows, width)]
    own = kernel_call(gather_kernel, chunks[::-1], [shape((slots, width), bf16)] * 2, flops=2 * 10**9)
    other = [swap(part, "rep", 1) for part in own]

    wide = width + LANES
    dx, grad_own, grad_near = kernel_call(
        early_kernel,
        [*own, *other, first, near[0]],
        [shape((2 * slots, wide), f32), shape((hidden, width), f32), shape((hidden, width), bf16)],
        flops=10**9,
    )
    d_pre, prob, grad_near = kernel_call(
        middle_kernel,
        [*own, *other, grad_near, near[1]],
        [
            shape((2 * slots, 2 * hidden), bf16),
            shape((2 * slots, LANES), f32),
            shape((2 * hidden, width), bf16),
        ],
        flops=0,
    )
    parts = 2 if chunk_count % 2 == 0 else 1
    keep, *gives, grad_far = kernel_call(
        late_kernel,
        [*own, *other, dx, d_pre, prob, near[1], far],
        [shape((slots, wide), f32)]
        + [shape((slots // parts, wide), bf16)] * parts
        + [shape((hidden, width), bf16)],
    )
    folds = chunk_count > 1 and rows <= FOLD and width % FOLD == 0 and rows * width // FOLD % 8 == 0
    returned = shape((rows * width // FOLD + 8, FOLD) if folds else (rows, wide), bf16)
    back = []
    for i, give in enumerate(gives):
        sums = kernel_call(
            functools.partial(add_kernel, (parts - 1 - i) * slots // parts, rows),
            [keep, swap(give, "rep", 1)],
            [returned] * (chunk_count // parts),
        )
        back = [*sums, *back]
    if chunk_count > 1:
        back = exchange(back)
    else:
        moved = back[0].reshape(experts, cap, wide)
        moved = lax.all_to_all(moved, "ep", split_axis=0, concat_axis=0, tiled=True)
        back = [moved.reshape(rows, wide)]
    back = kernel_call(
        pass_kernel,
        back[::-1],
        [shape(b.shape, b.dtype) for b in back],
        flops=8 * 10**9,
        input_output_aliases={i: i for i in range(len(back))},
    )
    arrived = swap_by_core(grad_near, along), swap_by_core(grad_far, (3, 3))
    (mine,) = kernel_call(grad_kernel, [grad_own, *arrived], [shape((2 * hidden, width), bf16)])
    results = [
        shape((1, 2 * hidden, width), f32),
        shape((tok_dev, width), bf16),
        shape((top, tok_dev), bf16),
    ]
    grad_total, d_tokens, d_probs = kernel_call(
        functools.partial(finish_kernel, chunk_count, rows),
        [*back, slot, weight, mine, swap(mine, "rep", 1)],
        results,
        out_specs=[in_hbm] * 3,
        scratch_shapes=[
            pltpu.VMEM((2, hidden, width), f32),
            *(pltpu.VMEM(result.shape, result.dtype) for result in results[1:]),
            pltpu.SemaphoreType.DMA((4,)),
        ],
    )
    return d_tokens, d_probs.T, grad_total


def solution(mesh):
    rows = P(("rep", "ep", "dp"), None)
    weights = P("ep", "dp", None)
    return jax.shard_map(
        local,
        mesh=mesh,
        in_specs=(rows,) * 4 + (weights,) * 3,
        out_specs=(rows, rows, weights),
        check_vma=False,
    )
```

```python
import functools

import jax
import jax.numpy as jnp
from jax import lax
from jax.experimental import pallas as pl
from jax.experimental.pallas import tpu as pltpu
from jax.sharding import PartitionSpec as P

LANES = 128
FOLD = 256
VMEM_BYTES = 32 * 1024 * 1024
f32, bf16 = jnp.float32, jnp.bfloat16


def dot(left, right, contract):
    return lax.dot_general(left, right, ((contract[0:1], contract[1:2]), ((), ())), preferred_element_type=f32)


def swap(value, axis, mask):
    return lax.ppermute(value, axis, [(i, i ^ mask) for i in range(lax.axis_size(axis))])


def exchange(chunks):
    return chunks[:1] + [swap(chunks[c], "ep", c) for c in range(1, len(chunks))]


def swap_by_core(value, masks):
    count = lax.axis_size("dp")
    pairs = [(r * count + i, r * count + (i ^ mask)) for r, mask in enumerate(masks) for i in range(count)]
    return lax.ppermute(value, ("rep", "dp"), pairs)


def kernel_call(body, inputs, outputs, flops=0, **kwargs):
    whole = pl.BlockSpec(memory_space=pltpu.VMEM)
    moved = sum(a.size * a.dtype.itemsize for a in inputs + outputs)
    return pl.pallas_call(
        body,
        out_shape=outputs,
        in_specs=kwargs.pop("in_specs", [whole] * len(inputs)),
        out_specs=kwargs.pop("out_specs", [whole] * len(outputs)),
        cost_estimate=pl.CostEstimate(flops=flops, bytes_accessed=moved, transcendentals=0),
        compiler_params=pltpu.CompilerParams(vmem_limit_bytes=VMEM_BYTES),
        **kwargs,
    )(*inputs)


def iota(shape, dim):
    return lax.broadcasted_iota(jnp.int32, shape, dim)


def dispatch_kernel(experts, cap, chunk_count, *refs):
    given, weights, refs = refs[:4], refs[4:7], refs[7:]
    chunks, (slot_out, *packed), (ids, route_weight, both, sems) = refs[:chunk_count], refs[chunk_count:-4], refs[-4:]
    hidden = packed[0].shape[0] // 3
    rep = lax.axis_index("rep")
    top, tok_dev = ids.shape
    held = (ids, route_weight, both.at[pl.ds(0, tok_dev)], both.at[pl.ds(tok_dev, tok_dev)])
    loads = [pltpu.make_async_copy(*pair, sems.at[i]) for i, pair in enumerate(zip(given, held))]
    packs = []
    for j, half in enumerate((rep, 1 - rep)):
        rows = pl.ds(pl.multiple_of(half * hidden, hidden), hidden)
        packs += [
            pltpu.make_async_copy(weight.at[0, rows], packed[j].at[pl.ds(i * hidden, hidden)], sems.at[4 + 3 * j + i])
            for i, weight in enumerate(weights)
        ]
    for copy in loads + packs:
        copy.start()
    for copy in loads[:2]:
        copy.wait()

    rows = experts * cap // chunk_count
    me = lax.axis_index("ep")
    expert_of_row = iota((experts, tok_dev), 0)
    named = [(expert_of_row == ids[k : k + 1, :]).astype(f32) for k in range(top)]
    earlier = (iota((tok_dev, tok_dev), 0) < iota((tok_dev, tok_dev), 1)).astype(bf16)
    before = dot(sum(named).astype(bf16), earlier, (1, 0))
    row = iota((2 * experts * cap, 2 * tok_dev), 0)
    take = jnp.zeros(row.shape, f32)
    scale = jnp.zeros(row.shape, f32)
    for k in range(top):
        rank = jnp.sum(before * named[k], axis=0, keepdims=True).astype(jnp.int32)
        expert = ids[k : k + 1, :]
        if chunk_count > 1:
            chunk = expert ^ me
            slot = chunk * cap + rank
            x_row = slot + chunk * cap
        else:
            slot = expert * cap + rank
            x_row = slot
        slot_out[k : k + 1, :] = slot
        weight = route_weight[k : k + 1, :].astype(f32)
        here = (row == jnp.concatenate([x_row, x_row + rows], axis=1)).astype(f32)
        take += here
        scale += here * jnp.concatenate([jnp.ones_like(weight), weight], axis=1)
    scale = jnp.sum(scale, axis=1, keepdims=True)
    take = take.astype(bf16)
    for copy in loads[2:]:
        copy.wait()
    picked = dot(take, both[...], (1, 0)) * scale
    for c in range(chunk_count):
        chunks[c][...] = picked[2 * rows * c : 2 * rows * (c + 1)].astype(bf16)
    for copy in packs:
        copy.wait()


def expert_math(x_rows, d_rows, pieces):
    hidden = pieces[0].shape[0] // 3
    gate, up, down = [[piece[i * hidden : (i + 1) * hidden] for piece in pieces] for i in range(3)]
    mixers = jnp.concatenate(gate + up)
    pre = dot(x_rows, mixers, (1, 1))
    d_act = dot(d_rows, jnp.concatenate(down), (1, 1))
    gate_pre, up_pre = pre[:, : hidden * len(pieces)], pre[:, hidden * len(pieces) :]
    sig = jax.nn.sigmoid(gate_pre)
    silu = gate_pre * sig
    act = silu * up_pre
    prob = jnp.sum(act * d_act, axis=1, keepdims=True)
    d_gate = d_act * up_pre * sig * (1.0 + gate_pre * (1.0 - sig))
    d_pre = jnp.concatenate([d_gate, d_act * silu], axis=1).astype(bf16)
    return d_pre, mixers, prob, dot(act.astype(bf16), d_rows, (0, 0))


def gather_kernel(*refs):
    *chunks, x_out, d_out = refs
    rows = chunks[0].shape[0] // 2
    values = [c[...].astype(f32) for c in reversed(chunks)]
    x_out[...] = jnp.concatenate([v[:rows] for v in values]).astype(bf16)
    d_out[...] = jnp.concatenate([v[rows:] for v in values]).astype(bf16)


def both_cores(x_own, d_own, x_other, d_other):
    return [jnp.concatenate([a[...], b[...]]) for a, b in ((x_own, x_other), (d_own, d_other))]


def early_kernel(*refs):
    *pieces, dx_out, grad_own, grad_near = refs[4:]
    d_pre, mixers, prob, grad = expert_math(*both_cores(*refs[:4]), pieces)
    width, hidden = mixers.shape[1], grad_own.shape[0]
    dx_out[:, :width] = dot(d_pre, mixers, (1, 0))
    dx_out[:, width:] = jnp.broadcast_to(prob, (prob.shape[0], LANES))
    grad_own[...] = grad[:hidden]
    grad_near[...] = grad[hidden:].astype(bf16)


def middle_kernel(*refs):
    grad_ref, piece, pre_out, prob_out, grad_out = refs[4:]
    pre_out[...], _, prob, grad = expert_math(*both_cores(*refs[:4]), [piece])
    hidden = grad.shape[0]
    prob_out[...] = jnp.broadcast_to(prob, prob_out.shape)
    grad_out[:hidden] = grad_ref[...]
    grad_out[hidden:] = grad.astype(bf16)


def late_kernel(*refs):
    dx_ref, pre_ref, prob_ref, near, far, keep, *gives, grad_far = refs[4:]
    d_pre, mixers, prob, grad = expert_math(*both_cores(*refs[:4]), [far])
    mixers = jnp.concatenate([near[: mixers.shape[0]], mixers])
    dx = dot(jnp.concatenate([pre_ref[...], d_pre], axis=1), mixers, (1, 0))
    prob = prob_ref[...] + prob
    width, slots = dx.shape[1], keep.shape[0]
    for side, value in ((slice(0, width), dx), (slice(width, None), prob)):
        total = value + dx_ref[:, side]
        keep[:, side] = total[:slots]
        for i, give in enumerate(reversed(gives)):
            rows = give.shape[0]
            give[:, side] = total[slots + rows * i : slots + rows * (i + 1)].astype(bf16)
    grad_far[...] = grad.astype(bf16)


def grad_kernel(own, near, far, out):
    hidden = own.shape[0]
    out[:hidden] = (own[...] + near[:hidden].astype(f32) + far[...].astype(f32)).astype(bf16)
    out[hidden:] = near[hidden:]


def finish_kernel(mine, theirs, tokens, probs, grad_out, tokens_out, probs_out, held, sems):
    hidden = mine.shape[0] // 2
    rep = lax.axis_index("rep")
    copies = [pltpu.make_async_copy(tokens, tokens_out, sems.at[0]), pltpu.make_async_copy(probs, probs_out, sems.at[1])]
    for copy in copies:
        copy.start()
    for i, half in enumerate((rep, 1 - rep)):
        here, there = slice(i * hidden, (i + 1) * hidden), slice((1 - i) * hidden, (2 - i) * hidden)
        rows = pl.ds(pl.multiple_of(half * hidden, hidden), hidden)
        held[i] = mine[here].astype(f32) + theirs[there].astype(f32)
        copies.append(pltpu.make_async_copy(held.at[i], grad_out.at[0, rows], sems.at[2 + i]))
        copies[-1].start()
    for copy in copies:
        copy.wait()


def add_kernel(start, rows, keep, got, *chunks):
    total = keep[start : start + got.shape[0]] + got[...].astype(f32)
    width = total.shape[1] - LANES
    for c, chunk in enumerate(chunks):
        value = total[c * rows : (c + 1) * rows]
        if chunk.shape[0] > rows:
            blocks = [value[:, i : i + FOLD] for i in range(0, width, FOLD)]
            diagonal = iota((rows, FOLD), 0) == iota((rows, FOLD), 1)
            prob = jnp.sum(jnp.where(diagonal, value[:, width : width + 1], 0.0), axis=0, keepdims=True)
            value = jnp.concatenate([*blocks, jnp.broadcast_to(prob, (8, FOLD))])
        chunk[...] = value.astype(bf16)


def combine_kernel(chunk_count, rows, *refs):
    chunks, (slot, route_weight, tokens_out, probs_out) = refs[:chunk_count], refs[chunk_count:]
    tok_dev, width = tokens_out.shape
    top = slot.shape[0]
    total = 0.0
    probs = [0.0] * top
    for c, place in enumerate(reversed(range(chunk_count))):
        slot_of_row = iota((rows, tok_dev), 0) + place * rows
        hits = [(slot_of_row == slot[k : k + 1, :]).astype(f32) for k in range(top)]
        value = chunks[c][...].astype(f32)
        if value.shape[0] > rows:
            blocks = [value[i : i + rows] for i in range(0, width // FOLD * rows, rows)]
            diagonal = iota((rows, FOLD), 0) == iota((rows, FOLD), 1)
            prob = value[width // FOLD * rows :][:1]
            prob = jnp.sum(jnp.where(diagonal, prob, 0.0), axis=1, keepdims=True)
            value = jnp.concatenate(blocks, axis=1)
        else:
            prob = value[:, width : width + 1]
        total = total + dot(sum(hits).astype(bf16), value[:, :width].astype(bf16), (0, 0))
        for k in range(top):
            probs[k] = probs[k] + jnp.sum(hits[k] * prob, axis=0, keepdims=True)
    tokens_out[...] = total.astype(bf16)
    for k in range(top):
        probs_out[k : k + 1, :] = (probs[k] / route_weight[k : k + 1, :].astype(f32)).astype(bf16)


def local(tokens, upstream, expert_ids, route_weight, gate_weight, up_weight, down_weight):
    tok_dev, width = tokens.shape
    top = expert_ids.shape[1]
    experts, reps = lax.axis_size("ep"), lax.axis_size("rep")
    cap = 2 * ((5 * tok_dev * top + 8 * experts - 1) // (8 * experts))
    slots = experts * cap
    chunk_count = experts if experts <= 8 else 1
    rows = slots // chunk_count
    hidden = gate_weight.shape[1] // reps
    shape = jax.ShapeDtypeStruct
    in_hbm = pl.BlockSpec(memory_space=pltpu.HBM)

    given = [expert_ids.T, route_weight.T, tokens, upstream]
    *chunks, slot, first, second = kernel_call(
        functools.partial(dispatch_kernel, experts, cap, chunk_count),
        [pltpu.with_memory_space_constraint(a, pltpu.HBM) for a in [*given, gate_weight, up_weight, down_weight]],
        [shape((2 * rows, width), bf16)] * chunk_count
        + [shape((top, tok_dev), jnp.int32)]
        + [shape((3 * hidden, width), bf16)] * 2,
        in_specs=[in_hbm] * 7,
        scratch_shapes=[
            *(pltpu.VMEM(a.shape, a.dtype) for a in given[:2]),
            pltpu.VMEM((2 * tok_dev, width), bf16),
            pltpu.SemaphoreType.DMA((10,)),
        ],
    )

    along, across = (1, 2), (2, 1)
    near = [swap_by_core(first, along), swap_by_core(second, along)]
    far = swap_by_core(near[0], across)

    if chunk_count > 1:
        chunks = exchange(chunks)
    else:
        moved = chunks[0].reshape(2, experts, cap, width)
        moved = lax.all_to_all(moved, "ep", split_axis=1, concat_axis=1, tiled=True)
        chunks = [moved.reshape(2 * rows, width)]
    own = kernel_call(gather_kernel, chunks[::-1], [shape((slots, width), bf16)] * 2, flops=2 * 10**9)
    other = [swap(part, "rep", 1) for part in own]

    wide = width + LANES
    dx, grad_own, grad_near = kernel_call(
        early_kernel,
        [*own, *other, first, near[0]],
        [shape((2 * slots, wide), f32), shape((hidden, width), f32), shape((hidden, width), bf16)],
        flops=10**9,
    )
    d_pre, prob, grad_near = kernel_call(
        middle_kernel,
        [*own, *other, grad_near, near[1]],
        [
            shape((2 * slots, 2 * hidden), bf16),
            shape((2 * slots, LANES), f32),
            shape((2 * hidden, width), bf16),
        ],
        flops=0,
    )
    parts = 2 if chunk_count % 2 == 0 else 1
    keep, *gives, grad_far = kernel_call(
        late_kernel,
        [*own, *other, dx, d_pre, prob, near[1], far],
        [shape((slots, wide), f32)]
        + [shape((slots // parts, wide), bf16)] * parts
        + [shape((hidden, width), bf16)],
    )
    folds = chunk_count > 1 and rows <= FOLD and width % FOLD == 0 and rows * width // FOLD % 8 == 0
    returned = shape((rows * width // FOLD + 8, FOLD) if folds else (rows, wide), bf16)
    back = []
    for i, give in enumerate(gives):
        sums = kernel_call(
            functools.partial(add_kernel, (parts - 1 - i) * slots // parts, rows),
            [keep, swap(give, "rep", 1)],
            [returned] * (chunk_count // parts),
        )
        back = [*sums, *back]
    if chunk_count > 1:
        back = exchange(back)
    else:
        moved = back[0].reshape(experts, cap, wide)
        moved = lax.all_to_all(moved, "ep", split_axis=0, concat_axis=0, tiled=True)
        back = [moved.reshape(rows, wide)]
    d_tokens, d_probs = kernel_call(
        functools.partial(combine_kernel, chunk_count, rows),
        back[::-1] + [slot, route_weight.T],
        [shape((tok_dev, width), bf16), shape((top, tok_dev), bf16)],
        flops=8 * 10**9,
    )

    arrived = swap_by_core(grad_near, along), swap_by_core(grad_far, (3, 3))
    (mine,) = kernel_call(grad_kernel, [grad_own, *arrived], [shape((2 * hidden, width), bf16)])
    results = [
        shape((1, 2 * hidden, width), f32),
        shape((tok_dev, width), bf16),
        shape((top, tok_dev), bf16),
    ]
    grad_total, d_tokens, d_probs = kernel_call(
        finish_kernel,
        [mine, swap(mine, "rep", 1), d_tokens, d_probs],
        results,
        out_specs=[in_hbm] * 3,
        scratch_shapes=[pltpu.VMEM((2, hidden, width), f32), pltpu.SemaphoreType.DMA((4,))],
    )
    return d_tokens, d_probs.T, grad_total


def solution(mesh):
    rows = P(("rep", "ep", "dp"), None)
    weights = P("ep", "dp", None)
    return jax.shard_map(
        local,
        mesh=mesh,
        in_specs=(rows,) * 4 + (weights,) * 3,
        out_specs=(rows, rows, weights),
        check_vma=False,
    )
```

```python
import functools

import jax
import jax.numpy as jnp
from jax import lax
from jax.experimental import pallas as pl
from jax.experimental.pallas import tpu as pltpu
from jax.sharding import PartitionSpec as P

LANES = 128
FOLD = 128
VMEM_BYTES = 32 * 1024 * 1024
f32, bf16 = jnp.float32, jnp.bfloat16


def dot(left, right, contract):
    return lax.dot_general(left, right, ((contract[0:1], contract[1:2]), ((), ())), preferred_element_type=f32)


def swap(value, axis, mask):
    return lax.ppermute(value, axis, [(i, i ^ mask) for i in range(lax.axis_size(axis))])


def exchange(chunks):
    return chunks[:1] + [swap(chunks[c], "ep", c) for c in range(1, len(chunks))]


def swap_by_core(value, masks):
    count = lax.axis_size("dp")
    pairs = [(r * count + i, r * count + (i ^ mask)) for r, mask in enumerate(masks) for i in range(count)]
    return lax.ppermute(value, ("rep", "dp"), pairs)


def kernel_call(body, inputs, outputs, flops=0, **kwargs):
    whole = pl.BlockSpec(memory_space=pltpu.VMEM)
    moved = sum(a.size * a.dtype.itemsize for a in inputs + outputs)
    return pl.pallas_call(
        body,
        out_shape=outputs,
        in_specs=kwargs.pop("in_specs", [whole] * len(inputs)),
        out_specs=kwargs.pop("out_specs", [whole] * len(outputs)),
        cost_estimate=pl.CostEstimate(flops=flops, bytes_accessed=moved, transcendentals=0),
        compiler_params=pltpu.CompilerParams(vmem_limit_bytes=VMEM_BYTES),
        **kwargs,
    )(*inputs)


def iota(shape, dim):
    return lax.broadcasted_iota(jnp.int32, shape, dim)


def dispatch_kernel(experts, cap, chunk_count, *refs):
    given, weights, refs = refs[:4], refs[4:7], refs[7:]
    chunks, (slot_out, *packed), (ids, route_weight, both, sems) = refs[:chunk_count], refs[chunk_count:-4], refs[-4:]
    hidden = packed[0].shape[0] // 3
    rep = lax.axis_index("rep")
    top, tok_dev = ids.shape
    held = (ids, route_weight, both.at[pl.ds(0, tok_dev)], both.at[pl.ds(tok_dev, tok_dev)])
    loads = [pltpu.make_async_copy(*pair, sems.at[i]) for i, pair in enumerate(zip(given, held))]
    packs = []
    for j, half in enumerate((rep, 1 - rep)):
        rows = pl.ds(pl.multiple_of(half * hidden, hidden), hidden)
        packs += [
            pltpu.make_async_copy(weight.at[0, rows], packed[j].at[pl.ds(i * hidden, hidden)], sems.at[4 + 3 * j + i])
            for i, weight in enumerate(weights)
        ]
    for copy in loads + packs:
        copy.start()
    for copy in loads[:2]:
        copy.wait()

    rows = experts * cap // chunk_count
    me = lax.axis_index("ep")
    expert_of_row = iota((experts, tok_dev), 0)
    named = [(expert_of_row == ids[k : k + 1, :]).astype(f32) for k in range(top)]
    earlier = (iota((tok_dev, tok_dev), 0) < iota((tok_dev, tok_dev), 1)).astype(bf16)
    before = dot(sum(named).astype(bf16), earlier, (1, 0))
    row = iota((2 * experts * cap, 2 * tok_dev), 0)
    take = jnp.zeros(row.shape, f32)
    scale = jnp.zeros(row.shape, f32)
    for k in range(top):
        rank = jnp.sum(before * named[k], axis=0, keepdims=True).astype(jnp.int32)
        expert = ids[k : k + 1, :]
        if chunk_count > 1:
            chunk = expert ^ me
            slot = chunk * cap + rank
            x_row = slot + chunk * cap
        else:
            slot = expert * cap + rank
            x_row = slot
        slot_out[k : k + 1, :] = slot
        weight = route_weight[k : k + 1, :].astype(f32)
        here = (row == jnp.concatenate([x_row, x_row + rows], axis=1)).astype(f32)
        take += here
        scale += here * jnp.concatenate([jnp.ones_like(weight), weight], axis=1)
    scale = jnp.sum(scale, axis=1, keepdims=True)
    take = take.astype(bf16)
    for copy in loads[2:]:
        copy.wait()
    picked = dot(take, both[...], (1, 0)) * scale
    for c in range(chunk_count):
        chunks[c][...] = picked[2 * rows * c : 2 * rows * (c + 1)].astype(bf16)
    for copy in packs:
        copy.wait()


def expert_math(x_rows, d_rows, pieces):
    hidden = pieces[0].shape[0] // 3
    gate, up, down = [[piece[i * hidden : (i + 1) * hidden] for piece in pieces] for i in range(3)]
    mixers = jnp.concatenate(gate + up)
    pre = dot(x_rows, mixers, (1, 1))
    d_act = dot(d_rows, jnp.concatenate(down), (1, 1))
    gate_pre, up_pre = pre[:, : hidden * len(pieces)], pre[:, hidden * len(pieces) :]
    sig = jax.nn.sigmoid(gate_pre)
    silu = gate_pre * sig
    act = silu * up_pre
    prob = jnp.sum(act * d_act, axis=1, keepdims=True)
    d_gate = d_act * up_pre * sig * (1.0 + gate_pre * (1.0 - sig))
    d_pre = jnp.concatenate([d_gate, d_act * silu], axis=1).astype(bf16)
    return d_pre, mixers, prob, dot(act.astype(bf16), d_rows, (0, 0))


def gather_kernel(*refs):
    *chunks, x_out, d_out = refs
    rows = chunks[0].shape[0] // 2
    values = [c[...].astype(f32) for c in reversed(chunks)]
    x_out[...] = jnp.concatenate([v[:rows] for v in values]).astype(bf16)
    d_out[...] = jnp.concatenate([v[rows:] for v in values]).astype(bf16)


def both_cores(x_own, d_own, x_other, d_other):
    return [jnp.concatenate([a[...], b[...]]) for a, b in ((x_own, x_other), (d_own, d_other))]


def early_kernel(*refs):
    *pieces, dx_out, grad_own, grad_near = refs[4:]
    d_pre, mixers, prob, grad = expert_math(*both_cores(*refs[:4]), pieces)
    width, hidden = mixers.shape[1], grad_own.shape[0]
    dx_out[:, :width] = dot(d_pre, mixers, (1, 0))
    dx_out[:, width:] = jnp.broadcast_to(prob, (prob.shape[0], LANES))
    grad_own[...] = grad[:hidden]
    grad_near[...] = grad[hidden:].astype(bf16)


def middle_kernel(*refs):
    grad_ref, piece, pre_out, prob_out, grad_out = refs[4:]
    pre_out[...], _, prob, grad = expert_math(*both_cores(*refs[:4]), [piece])
    hidden = grad.shape[0]
    prob_out[...] = jnp.broadcast_to(prob, prob_out.shape)
    grad_out[:hidden] = grad_ref[...]
    grad_out[hidden:] = grad.astype(bf16)


def late_kernel(*refs):
    dx_ref, pre_ref, prob_ref, near, far, keep, *gives, grad_far = refs[4:]
    d_pre, mixers, prob, grad = expert_math(*both_cores(*refs[:4]), [far])
    mixers = jnp.concatenate([near[: mixers.shape[0]], mixers])
    dx = dot(jnp.concatenate([pre_ref[...], d_pre], axis=1), mixers, (1, 0))
    prob = prob_ref[...] + prob
    width, slots = dx.shape[1], keep.shape[0]
    for side, value in ((slice(0, width), dx), (slice(width, None), prob)):
        total = value + dx_ref[:, side]
        keep[:, side] = total[:slots]
        for i, give in enumerate(reversed(gives)):
            rows = give.shape[0]
            give[:, side] = total[slots + rows * i : slots + rows * (i + 1)].astype(bf16)
    grad_far[...] = grad.astype(bf16)


def grad_kernel(own, near, far, out):
    hidden = own.shape[0]
    out[:hidden] = (own[...] + near[:hidden].astype(f32) + far[...].astype(f32)).astype(bf16)
    out[hidden:] = near[hidden:]


def finish_kernel(mine, theirs, tokens, probs, grad_out, tokens_out, probs_out, held, sems):
    hidden = mine.shape[0] // 2
    rep = lax.axis_index("rep")
    copies = [pltpu.make_async_copy(tokens, tokens_out, sems.at[0]), pltpu.make_async_copy(probs, probs_out, sems.at[1])]
    for copy in copies:
        copy.start()
    for i, half in enumerate((rep, 1 - rep)):
        here, there = slice(i * hidden, (i + 1) * hidden), slice((1 - i) * hidden, (2 - i) * hidden)
        rows = pl.ds(pl.multiple_of(half * hidden, hidden), hidden)
        held[i] = mine[here].astype(f32) + theirs[there].astype(f32)
        copies.append(pltpu.make_async_copy(held.at[i], grad_out.at[0, rows], sems.at[2 + i]))
        copies[-1].start()
    for copy in copies:
        copy.wait()


def add_kernel(start, rows, keep, got, *chunks):
    total = keep[start : start + got.shape[0]] + got[...].astype(f32)
    width = total.shape[1] - LANES
    for c, chunk in enumerate(chunks):
        value = total[c * rows : (c + 1) * rows]
        if chunk.shape[0] > rows:
            blocks = [value[:, i : i + FOLD] for i in range(0, width, FOLD)]
            diagonal = iota((rows, FOLD), 0) == iota((rows, FOLD), 1)
            prob = jnp.sum(jnp.where(diagonal, value[:, width : width + 1], 0.0), axis=0, keepdims=True)
            value = jnp.concatenate([*blocks, jnp.broadcast_to(prob, (8, FOLD))])
        chunk[...] = value.astype(bf16)


def combine_kernel(chunk_count, rows, *refs):
    chunks, (slot, route_weight, tokens_out, probs_out) = refs[:chunk_count], refs[chunk_count:]
    tok_dev, width = tokens_out.shape
    top = slot.shape[0]
    total = 0.0
    probs = [0.0] * top
    for c, place in enumerate(reversed(range(chunk_count))):
        slot_of_row = iota((rows, tok_dev), 0) + place * rows
        hits = [(slot_of_row == slot[k : k + 1, :]).astype(f32) for k in range(top)]
        value = chunks[c][...].astype(f32)
        if value.shape[0] > rows:
            blocks = [value[i : i + rows] for i in range(0, width // FOLD * rows, rows)]
            diagonal = iota((rows, FOLD), 0) == iota((rows, FOLD), 1)
            prob = value[width // FOLD * rows :][:1]
            prob = jnp.sum(jnp.where(diagonal, prob, 0.0), axis=1, keepdims=True)
            value = jnp.concatenate(blocks, axis=1)
        else:
            prob = value[:, width : width + 1]
        total = total + dot(sum(hits).astype(bf16), value[:, :width].astype(bf16), (0, 0))
        for k in range(top):
            probs[k] = probs[k] + jnp.sum(hits[k] * prob, axis=0, keepdims=True)
    tokens_out[...] = total.astype(bf16)
    for k in range(top):
        probs_out[k : k + 1, :] = (probs[k] / route_weight[k : k + 1, :].astype(f32)).astype(bf16)


def local(tokens, upstream, expert_ids, route_weight, gate_weight, up_weight, down_weight):
    tok_dev, width = tokens.shape
    top = expert_ids.shape[1]
    experts, reps = lax.axis_size("ep"), lax.axis_size("rep")
    cap = 2 * ((5 * tok_dev * top + 8 * experts - 1) // (8 * experts))
    slots = experts * cap
    chunk_count = experts if experts <= 8 else 1
    rows = slots // chunk_count
    hidden = gate_weight.shape[1] // reps
    shape = jax.ShapeDtypeStruct
    in_hbm = pl.BlockSpec(memory_space=pltpu.HBM)

    given = [expert_ids.T, route_weight.T, tokens, upstream]
    *chunks, slot, first, second = kernel_call(
        functools.partial(dispatch_kernel, experts, cap, chunk_count),
        [pltpu.with_memory_space_constraint(a, pltpu.HBM) for a in [*given, gate_weight, up_weight, down_weight]],
        [shape((2 * rows, width), bf16)] * chunk_count
        + [shape((top, tok_dev), jnp.int32)]
        + [shape((3 * hidden, width), bf16)] * 2,
        in_specs=[in_hbm] * 7,
        scratch_shapes=[
            *(pltpu.VMEM(a.shape, a.dtype) for a in given[:2]),
            pltpu.VMEM((2 * tok_dev, width), bf16),
            pltpu.SemaphoreType.DMA((10,)),
        ],
    )

    along, across = (1, 2), (2, 1)
    near = [swap_by_core(first, along), swap_by_core(second, along)]
    far = swap_by_core(near[0], across)

    if chunk_count > 1:
        chunks = exchange(chunks)
    else:
        moved = chunks[0].reshape(2, experts, cap, width)
        moved = lax.all_to_all(moved, "ep", split_axis=1, concat_axis=1, tiled=True)
        chunks = [moved.reshape(2 * rows, width)]
    own = kernel_call(gather_kernel, chunks[::-1], [shape((slots, width), bf16)] * 2, flops=2 * 10**9)
    other = [swap(part, "rep", 1) for part in own]

    wide = width + LANES
    dx, grad_own, grad_near = kernel_call(
        early_kernel,
        [*own, *other, first, near[0]],
        [shape((2 * slots, wide), f32), shape((hidden, width), f32), shape((hidden, width), bf16)],
        flops=10**9,
    )
    d_pre, prob, grad_near = kernel_call(
        middle_kernel,
        [*own, *other, grad_near, near[1]],
        [
            shape((2 * slots, 2 * hidden), bf16),
            shape((2 * slots, LANES), f32),
            shape((2 * hidden, width), bf16),
        ],
        flops=0,
    )
    parts = 2 if chunk_count % 2 == 0 else 1
    keep, *gives, grad_far = kernel_call(
        late_kernel,
        [*own, *other, dx, d_pre, prob, near[1], far],
        [shape((slots, wide), f32)]
        + [shape((slots // parts, wide), bf16)] * parts
        + [shape((hidden, width), bf16)],
    )
    folds = chunk_count > 1 and rows <= FOLD and width % FOLD == 0 and rows * width // FOLD % 8 == 0
    returned = shape((rows * width // FOLD + 8, FOLD) if folds else (rows, wide), bf16)
    back = []
    for i, give in enumerate(gives):
        sums = kernel_call(
            functools.partial(add_kernel, (parts - 1 - i) * slots // parts, rows),
            [keep, swap(give, "rep", 1)],
            [returned] * (chunk_count // parts),
        )
        back = [*sums, *back]
    if chunk_count > 1:
        back = exchange(back)
    else:
        moved = back[0].reshape(experts, cap, wide)
        moved = lax.all_to_all(moved, "ep", split_axis=0, concat_axis=0, tiled=True)
        back = [moved.reshape(rows, wide)]
    d_tokens, d_probs = kernel_call(
        functools.partial(combine_kernel, chunk_count, rows),
        back[::-1] + [slot, route_weight.T],
        [shape((tok_dev, width), bf16), shape((top, tok_dev), bf16)],
        flops=8 * 10**9,
    )

    arrived = swap_by_core(grad_near, along), swap_by_core(grad_far, (3, 3))
    (mine,) = kernel_call(grad_kernel, [grad_own, *arrived], [shape((2 * hidden, width), bf16)])
    results = [
        shape((1, 2 * hidden, width), f32),
        shape((tok_dev, width), bf16),
        shape((top, tok_dev), bf16),
    ]
    grad_total, d_tokens, d_probs = kernel_call(
        finish_kernel,
        [mine, swap(mine, "rep", 1), d_tokens, d_probs],
        results,
        out_specs=[in_hbm] * 3,
        scratch_shapes=[pltpu.VMEM((2, hidden, width), f32), pltpu.SemaphoreType.DMA((4,))],
    )
    return d_tokens, d_probs.T, grad_total


def solution(mesh):
    rows = P(("rep", "ep", "dp"), None)
    weights = P("ep", "dp", None)
    return jax.shard_map(
        local,
        mesh=mesh,
        in_specs=(rows,) * 4 + (weights,) * 3,
        out_specs=(rows, rows, weights),
        check_vma=False,
    )
```

```python
import functools

import jax
import jax.numpy as jnp
from jax import lax
from jax.experimental import pallas as pl
from jax.experimental.pallas import tpu as pltpu
from jax.sharding import PartitionSpec as P

LANES = 128
FOLD = 128
VMEM_BYTES = 32 * 1024 * 1024
f32, bf16 = jnp.float32, jnp.bfloat16


def dot(left, right, contract):
    return lax.dot_general(left, right, ((contract[0:1], contract[1:2]), ((), ())), preferred_element_type=f32)


def swap(value, axis, mask):
    return lax.ppermute(value, axis, [(i, i ^ mask) for i in range(lax.axis_size(axis))])


def exchange(chunks):
    return chunks[:1] + [swap(chunks[c], "ep", c) for c in range(1, len(chunks))]


def swap_by_core(value, masks):
    count = lax.axis_size("dp")
    pairs = [(r * count + i, r * count + (i ^ mask)) for r, mask in enumerate(masks) for i in range(count)]
    return lax.ppermute(value, ("rep", "dp"), pairs)


def kernel_call(body, inputs, outputs, flops=0, **kwargs):
    whole = pl.BlockSpec(memory_space=pltpu.VMEM)
    moved = sum(a.size * a.dtype.itemsize for a in inputs + outputs)
    return pl.pallas_call(
        body,
        out_shape=outputs,
        in_specs=kwargs.pop("in_specs", [whole] * len(inputs)),
        out_specs=kwargs.pop("out_specs", [whole] * len(outputs)),
        cost_estimate=pl.CostEstimate(flops=flops, bytes_accessed=moved, transcendentals=0),
        compiler_params=pltpu.CompilerParams(vmem_limit_bytes=VMEM_BYTES),
        **kwargs,
    )(*inputs)


def iota(shape, dim):
    return lax.broadcasted_iota(jnp.int32, shape, dim)


def pack_copies(weights, packed, half, sems, start):
    hidden = packed.shape[0] // 3
    rows = pl.ds(pl.multiple_of(half * hidden, hidden), hidden)
    return [
        pltpu.make_async_copy(weight.at[0, rows], packed.at[pl.ds(i * hidden, hidden)], sems.at[start + i])
        for i, weight in enumerate(weights)
    ]


def pack_kernel(gate, up, down, packed, sems):
    copies = pack_copies((gate, up, down), packed, 1 - lax.axis_index("rep"), sems, 0)
    for copy in copies:
        copy.start()
    for copy in copies:
        copy.wait()


def dispatch_kernel(experts, cap, chunk_count, *refs):
    given, weights, refs = refs[:4], refs[4:7], refs[7:]
    chunks, (slot_out, packed), (ids, route_weight, both, sems) = refs[:chunk_count], refs[chunk_count:-4], refs[-4:]
    rep = lax.axis_index("rep")
    top, tok_dev = ids.shape
    held = (ids, route_weight, both.at[pl.ds(0, tok_dev)], both.at[pl.ds(tok_dev, tok_dev)])
    loads = [pltpu.make_async_copy(*pair, sems.at[i]) for i, pair in enumerate(zip(given, held))]
    packs = pack_copies(weights, packed, rep, sems, 4)
    for copy in loads + packs:
        copy.start()
    for copy in loads[:2]:
        copy.wait()

    rows = experts * cap // chunk_count
    me = lax.axis_index("ep")
    expert_of_row = iota((experts, tok_dev), 0)
    named = [(expert_of_row == ids[k : k + 1, :]).astype(f32) for k in range(top)]
    earlier = (iota((tok_dev, tok_dev), 0) < iota((tok_dev, tok_dev), 1)).astype(bf16)
    before = dot(sum(named).astype(bf16), earlier, (1, 0))
    row = iota((2 * experts * cap, 2 * tok_dev), 0)
    take = jnp.zeros(row.shape, f32)
    scale = jnp.zeros(row.shape, f32)
    for k in range(top):
        rank = jnp.sum(before * named[k], axis=0, keepdims=True).astype(jnp.int32)
        expert = ids[k : k + 1, :]
        if chunk_count > 1:
            chunk = expert ^ me
            slot = chunk * cap + rank
            x_row = slot + chunk * cap
        else:
            slot = expert * cap + rank
            x_row = slot
        slot_out[k : k + 1, :] = slot
        weight = route_weight[k : k + 1, :].astype(f32)
        here = (row == jnp.concatenate([x_row, x_row + rows], axis=1)).astype(f32)
        take += here
        scale += here * jnp.concatenate([jnp.ones_like(weight), weight], axis=1)
    scale = jnp.sum(scale, axis=1, keepdims=True)
    take = take.astype(bf16)
    for copy in loads[2:]:
        copy.wait()
    picked = dot(take, both[...], (1, 0)) * scale
    for c in range(chunk_count):
        chunks[c][...] = picked[2 * rows * c : 2 * rows * (c + 1)].astype(bf16)
    for copy in packs:
        copy.wait()


def expert_math(x_rows, d_rows, pieces):
    hidden = pieces[0].shape[0] // 3
    gate, up, down = [[piece[i * hidden : (i + 1) * hidden] for piece in pieces] for i in range(3)]
    mixers = jnp.concatenate(gate + up)
    pre = dot(x_rows, mixers, (1, 1))
    d_act = dot(d_rows, jnp.concatenate(down), (1, 1))
    gate_pre, up_pre = pre[:, : hidden * len(pieces)], pre[:, hidden * len(pieces) :]
    sig = jax.nn.sigmoid(gate_pre)
    silu = gate_pre * sig
    act = silu * up_pre
    prob = jnp.sum(act * d_act, axis=1, keepdims=True)
    d_gate = d_act * up_pre * sig * (1.0 + gate_pre * (1.0 - sig))
    d_pre = jnp.concatenate([d_gate, d_act * silu], axis=1).astype(bf16)
    return d_pre, mixers, prob, dot(act.astype(bf16), d_rows, (0, 0))


def gather_kernel(*refs):
    *chunks, x_out, d_out = refs
    rows = chunks[0].shape[0] // 2
    values = [c[...].astype(f32) for c in reversed(chunks)]
    x_out[...] = jnp.concatenate([v[:rows] for v in values]).astype(bf16)
    d_out[...] = jnp.concatenate([v[rows:] for v in values]).astype(bf16)


def both_cores(x_own, d_own, x_other, d_other):
    return [jnp.concatenate([a[...], b[...]]) for a, b in ((x_own, x_other), (d_own, d_other))]


def early_kernel(*refs):
    *pieces, dx_out, grad_own, grad_near = refs[4:]
    d_pre, mixers, prob, grad = expert_math(*both_cores(*refs[:4]), pieces)
    width, hidden = mixers.shape[1], grad_own.shape[0]
    dx_out[:, :width] = dot(d_pre, mixers, (1, 0))
    dx_out[:, width:] = jnp.broadcast_to(prob, (prob.shape[0], LANES))
    grad_own[...] = grad[:hidden]
    grad_near[...] = grad[hidden:].astype(bf16)


def middle_kernel(*refs):
    grad_ref, piece, pre_out, prob_out, grad_out = refs[4:]
    pre_out[...], _, prob, grad = expert_math(*both_cores(*refs[:4]), [piece])
    hidden = grad.shape[0]
    prob_out[...] = jnp.broadcast_to(prob, prob_out.shape)
    grad_out[:hidden] = grad_ref[...]
    grad_out[hidden:] = grad.astype(bf16)


def late_kernel(*refs):
    dx_ref, pre_ref, prob_ref, near, far, keep, *gives, grad_far = refs[4:]
    d_pre, mixers, prob, grad = expert_math(*both_cores(*refs[:4]), [far])
    mixers = jnp.concatenate([near[: mixers.shape[0]], mixers])
    dx = dot(jnp.concatenate([pre_ref[...], d_pre], axis=1), mixers, (1, 0))
    prob = prob_ref[...] + prob
    width, slots = dx.shape[1], keep.shape[0]
    for side, value in ((slice(0, width), dx), (slice(width, None), prob)):
        total = value + dx_ref[:, side]
        keep[:, side] = total[:slots]
        for i, give in enumerate(reversed(gives)):
            rows = give.shape[0]
            give[:, side] = total[slots + rows * i : slots + rows * (i + 1)].astype(bf16)
    grad_far[...] = grad.astype(bf16)


def grad_kernel(own, near, far, out):
    hidden = own.shape[0]
    out[:hidden] = (own[...] + near[:hidden].astype(f32) + far[...].astype(f32)).astype(bf16)
    out[hidden:] = near[hidden:]


def finish_kernel(mine, theirs, tokens, probs, grad_out, tokens_out, probs_out, held, sems):
    hidden = mine.shape[0] // 2
    rep = lax.axis_index("rep")
    copies = [pltpu.make_async_copy(tokens, tokens_out, sems.at[0]), pltpu.make_async_copy(probs, probs_out, sems.at[1])]
    for copy in copies:
        copy.start()
    for i, half in enumerate((rep, 1 - rep)):
        here, there = slice(i * hidden, (i + 1) * hidden), slice((1 - i) * hidden, (2 - i) * hidden)
        rows = pl.ds(pl.multiple_of(half * hidden, hidden), hidden)
        held[i] = mine[here].astype(f32) + theirs[there].astype(f32)
        copies.append(pltpu.make_async_copy(held.at[i], grad_out.at[0, rows], sems.at[2 + i]))
        copies[-1].start()
    for copy in copies:
        copy.wait()


def add_kernel(start, rows, keep, got, *chunks):
    total = keep[start : start + got.shape[0]] + got[...].astype(f32)
    width = total.shape[1] - LANES
    for c, chunk in enumerate(chunks):
        value = total[c * rows : (c + 1) * rows]
        if chunk.shape[0] > rows:
            blocks = [value[:, i : i + FOLD] for i in range(0, width, FOLD)]
            diagonal = iota((rows, FOLD), 0) == iota((rows, FOLD), 1)
            prob = jnp.sum(jnp.where(diagonal, value[:, width : width + 1], 0.0), axis=0, keepdims=True)
            value = jnp.concatenate([*blocks, jnp.broadcast_to(prob, (8, FOLD))])
        chunk[...] = value.astype(bf16)


def combine_kernel(chunk_count, rows, *refs):
    chunks, (slot, route_weight, tokens_out, probs_out) = refs[:chunk_count], refs[chunk_count:]
    tok_dev, width = tokens_out.shape
    top = slot.shape[0]
    total = 0.0
    probs = [0.0] * top
    for c, place in enumerate(reversed(range(chunk_count))):
        slot_of_row = iota((rows, tok_dev), 0) + place * rows
        hits = [(slot_of_row == slot[k : k + 1, :]).astype(f32) for k in range(top)]
        value = chunks[c][...].astype(f32)
        if value.shape[0] > rows:
            blocks = [value[i : i + rows] for i in range(0, width // FOLD * rows, rows)]
            diagonal = iota((rows, FOLD), 0) == iota((rows, FOLD), 1)
            prob = value[width // FOLD * rows :][:1]
            prob = jnp.sum(jnp.where(diagonal, prob, 0.0), axis=1, keepdims=True)
            value = jnp.concatenate(blocks, axis=1)
        else:
            prob = value[:, width : width + 1]
        total = total + dot(sum(hits).astype(bf16), value[:, :width].astype(bf16), (0, 0))
        for k in range(top):
            probs[k] = probs[k] + jnp.sum(hits[k] * prob, axis=0, keepdims=True)
    tokens_out[...] = total.astype(bf16)
    for k in range(top):
        probs_out[k : k + 1, :] = (probs[k] / route_weight[k : k + 1, :].astype(f32)).astype(bf16)


def local(tokens, upstream, expert_ids, route_weight, gate_weight, up_weight, down_weight):
    tok_dev, width = tokens.shape
    top = expert_ids.shape[1]
    experts, reps = lax.axis_size("ep"), lax.axis_size("rep")
    cap = 2 * ((5 * tok_dev * top + 8 * experts - 1) // (8 * experts))
    slots = experts * cap
    chunk_count = experts if experts <= 8 else 1
    rows = slots // chunk_count
    hidden = gate_weight.shape[1] // reps
    shape = jax.ShapeDtypeStruct
    in_hbm = pl.BlockSpec(memory_space=pltpu.HBM)

    given = [expert_ids.T, route_weight.T, tokens, upstream]
    *chunks, slot, first = kernel_call(
        functools.partial(dispatch_kernel, experts, cap, chunk_count),
        [pltpu.with_memory_space_constraint(a, pltpu.HBM) for a in [*given, gate_weight, up_weight, down_weight]],
        [shape((2 * rows, width), bf16)] * chunk_count
        + [shape((top, tok_dev), jnp.int32)]
        + [shape((3 * hidden, width), bf16)],
        in_specs=[in_hbm] * 7,
        scratch_shapes=[
            *(pltpu.VMEM(a.shape, a.dtype) for a in given[:2]),
            pltpu.VMEM((2 * tok_dev, width), bf16),
            pltpu.SemaphoreType.DMA((7,)),
        ],
    )

    weights, _ = lax.optimization_barrier(((gate_weight, up_weight, down_weight), slot))
    (second,) = kernel_call(
        pack_kernel,
        [pltpu.with_memory_space_constraint(a, pltpu.HBM) for a in weights],
        [shape((3 * hidden, width), bf16)],
        in_specs=[in_hbm] * 3,
        scratch_shapes=[pltpu.SemaphoreType.DMA((3,))],
    )

    along, across = (1, 2), (2, 1)
    near = [swap_by_core(first, along), swap_by_core(second, along)]
    far = swap_by_core(near[0], across)

    if chunk_count > 1:
        chunks = exchange(chunks)
    else:
        moved = chunks[0].reshape(2, experts, cap, width)
        moved = lax.all_to_all(moved, "ep", split_axis=1, concat_axis=1, tiled=True)
        chunks = [moved.reshape(2 * rows, width)]
    own = kernel_call(gather_kernel, chunks[::-1], [shape((slots, width), bf16)] * 2, flops=2 * 10**9)
    other = [swap(part, "rep", 1) for part in own]

    wide = width + LANES
    dx, grad_own, grad_near = kernel_call(
        early_kernel,
        [*own, *other, first, near[0]],
        [shape((2 * slots, wide), f32), shape((hidden, width), f32), shape((hidden, width), bf16)],
        flops=10**9,
    )
    d_pre, prob, grad_near = kernel_call(
        middle_kernel,
        [*own, *other, grad_near, near[1]],
        [
            shape((2 * slots, 2 * hidden), bf16),
            shape((2 * slots, LANES), f32),
            shape((2 * hidden, width), bf16),
        ],
        flops=0,
    )
    parts = 2 if chunk_count % 2 == 0 else 1
    keep, *gives, grad_far = kernel_call(
        late_kernel,
        [*own, *other, dx, d_pre, prob, near[1], far],
        [shape((slots, wide), f32)]
        + [shape((slots // parts, wide), bf16)] * parts
        + [shape((hidden, width), bf16)],
    )
    folds = chunk_count > 1 and rows <= FOLD and width % FOLD == 0 and rows * width // FOLD % 8 == 0
    returned = shape((rows * width // FOLD + 8, FOLD) if folds else (rows, wide), bf16)
    back = []
    for i, give in enumerate(gives):
        sums = kernel_call(
            functools.partial(add_kernel, (parts - 1 - i) * slots // parts, rows),
            [keep, swap(give, "rep", 1)],
            [returned] * (chunk_count // parts),
        )
        back = [*sums, *back]
    if chunk_count > 1:
        back = exchange(back)
    else:
        moved = back[0].reshape(experts, cap, wide)
        moved = lax.all_to_all(moved, "ep", split_axis=0, concat_axis=0, tiled=True)
        back = [moved.reshape(rows, wide)]
    d_tokens, d_probs = kernel_call(
        functools.partial(combine_kernel, chunk_count, rows),
        back[::-1] + [slot, route_weight.T],
        [shape((tok_dev, width), bf16), shape((top, tok_dev), bf16)],
        flops=8 * 10**9,
    )

    arrived = swap_by_core(grad_near, along), swap_by_core(grad_far, (3, 3))
    (mine,) = kernel_call(grad_kernel, [grad_own, *arrived], [shape((2 * hidden, width), bf16)])
    results = [
        shape((1, 2 * hidden, width), f32),
        shape((tok_dev, width), bf16),
        shape((top, tok_dev), bf16),
    ]
    grad_total, d_tokens, d_probs = kernel_call(
        finish_kernel,
        [mine, swap(mine, "rep", 1), d_tokens, d_probs],
        results,
        out_specs=[in_hbm] * 3,
        scratch_shapes=[pltpu.VMEM((2, hidden, width), f32), pltpu.SemaphoreType.DMA((4,))],
    )
    return d_tokens, d_probs.T, grad_total


def solution(mesh):
    rows = P(("rep", "ep", "dp"), None)
    weights = P("ep", "dp", None)
    return jax.shard_map(
        local,
        mesh=mesh,
        in_specs=(rows,) * 4 + (weights,) * 3,
        out_specs=(rows, rows, weights),
        check_vma=False,
    )
```

```python
import functools

import jax
import jax.numpy as jnp
from jax import lax
from jax.experimental import pallas as pl
from jax.experimental.pallas import tpu as pltpu
from jax.sharding import PartitionSpec as P

LANES = 128
FOLD = 128
VMEM_BYTES = 32 * 1024 * 1024
f32, bf16 = jnp.float32, jnp.bfloat16


def dot(left, right, contract):
    return lax.dot_general(left, right, ((contract[0:1], contract[1:2]), ((), ())), preferred_element_type=f32)


def swap(value, axis, mask):
    return lax.ppermute(value, axis, [(i, i ^ mask) for i in range(lax.axis_size(axis))])


def exchange(chunks):
    return chunks[:1] + [swap(chunks[c], "ep", c) for c in range(1, len(chunks))]


def swap_by_core(value, masks):
    count = lax.axis_size("dp")
    pairs = [(r * count + i, r * count + (i ^ mask)) for r, mask in enumerate(masks) for i in range(count)]
    return lax.ppermute(value, ("rep", "dp"), pairs)


def kernel_call(body, inputs, outputs, flops=0, **kwargs):
    whole = pl.BlockSpec(memory_space=pltpu.VMEM)
    moved = sum(a.size * a.dtype.itemsize for a in inputs + outputs)
    return pl.pallas_call(
        body,
        out_shape=outputs,
        in_specs=kwargs.pop("in_specs", [whole] * len(inputs)),
        out_specs=kwargs.pop("out_specs", [whole] * len(outputs)),
        cost_estimate=pl.CostEstimate(flops=flops, bytes_accessed=moved, transcendentals=0),
        compiler_params=pltpu.CompilerParams(vmem_limit_bytes=VMEM_BYTES),
        **kwargs,
    )(*inputs)


def iota(shape, dim):
    return lax.broadcasted_iota(jnp.int32, shape, dim)


def dispatch_kernel(experts, cap, chunk_count, *refs):
    given, weights, refs = refs[:4], refs[4:7], refs[7:]
    chunks, (slot_out, *packed), (ids, route_weight, both, sems) = refs[:chunk_count], refs[chunk_count:-4], refs[-4:]
    hidden = packed[0].shape[0] // 3
    rep = lax.axis_index("rep")
    top, tok_dev = ids.shape
    held = (ids, route_weight, both.at[pl.ds(0, tok_dev)], both.at[pl.ds(tok_dev, tok_dev)])
    loads = [pltpu.make_async_copy(*pair, sems.at[i]) for i, pair in enumerate(zip(given, held))]
    packs = []
    for j, half in enumerate((rep, 1 - rep)):
        rows = pl.ds(pl.multiple_of(half * hidden, hidden), hidden)
        packs += [
            pltpu.make_async_copy(weight.at[0, rows], packed[j].at[pl.ds(i * hidden, hidden)], sems.at[4 + 3 * j + i])
            for i, weight in enumerate(weights)
        ]
    for copy in loads + packs:
        copy.start()
    for copy in loads[:2]:
        copy.wait()

    rows = experts * cap // chunk_count
    me = lax.axis_index("ep")
    expert_of_row = iota((experts, tok_dev), 0)
    named = [(expert_of_row == ids[k : k + 1, :]).astype(f32) for k in range(top)]
    earlier = (iota((tok_dev, tok_dev), 0) < iota((tok_dev, tok_dev), 1)).astype(bf16)
    before = dot(sum(named).astype(bf16), earlier, (1, 0))
    row = iota((2 * experts * cap, 2 * tok_dev), 0)
    take = jnp.zeros(row.shape, f32)
    scale = jnp.zeros(row.shape, f32)
    for k in range(top):
        rank = jnp.sum(before * named[k], axis=0, keepdims=True).astype(jnp.int32)
        expert = ids[k : k + 1, :]
        if chunk_count > 1:
            chunk = expert ^ me
            slot = chunk * cap + rank
            x_row = slot + chunk * cap
        else:
            slot = expert * cap + rank
            x_row = slot
        slot_out[k : k + 1, :] = slot
        weight = route_weight[k : k + 1, :].astype(f32)
        here = (row == jnp.concatenate([x_row, x_row + rows], axis=1)).astype(f32)
        take += here
        scale += here * jnp.concatenate([jnp.ones_like(weight), weight], axis=1)
    scale = jnp.sum(scale, axis=1, keepdims=True)
    take = take.astype(bf16)
    for copy in loads[2:]:
        copy.wait()
    picked = dot(take, both[...], (1, 0)) * scale
    for c in range(chunk_count):
        chunks[c][...] = picked[2 * rows * c : 2 * rows * (c + 1)].astype(bf16)
    for copy in packs:
        copy.wait()


def expert_math(x_rows, d_rows, pieces):
    hidden = pieces[0].shape[0] // 3
    gate, up, down = [[piece[i * hidden : (i + 1) * hidden] for piece in pieces] for i in range(3)]
    mixers = jnp.concatenate(gate + up)
    pre = dot(x_rows, mixers, (1, 1))
    d_act = dot(d_rows, jnp.concatenate(down), (1, 1))
    gate_pre, up_pre = pre[:, : hidden * len(pieces)], pre[:, hidden * len(pieces) :]
    sig = jax.nn.sigmoid(gate_pre)
    silu = gate_pre * sig
    act = silu * up_pre
    prob = jnp.sum(act * d_act, axis=1, keepdims=True)
    d_gate = d_act * up_pre * sig * (1.0 + gate_pre * (1.0 - sig))
    d_pre = jnp.concatenate([d_gate, d_act * silu], axis=1).astype(bf16)
    return d_pre, mixers, prob, dot(act.astype(bf16), d_rows, (0, 0))


def gather_kernel(order, *refs):
    *chunks, x_out, d_out = refs
    rows = chunks[0].shape[0] // 2
    values = [chunks[order.index(c)][...].astype(f32) for c in range(len(order))]
    x_out[...] = jnp.concatenate([v[:rows] for v in values]).astype(bf16)
    d_out[...] = jnp.concatenate([v[rows:] for v in values]).astype(bf16)


def both_cores(x_own, d_own, x_other, d_other):
    return [jnp.concatenate([a[...], b[...]]) for a, b in ((x_own, x_other), (d_own, d_other))]


def early_kernel(*refs):
    *pieces, dx_out, grad_own, grad_near = refs[4:]
    d_pre, mixers, prob, grad = expert_math(*both_cores(*refs[:4]), pieces)
    width, hidden = mixers.shape[1], grad_own.shape[0]
    dx_out[:, :width] = dot(d_pre, mixers, (1, 0))
    dx_out[:, width:] = jnp.broadcast_to(prob, (prob.shape[0], LANES))
    grad_own[...] = grad[:hidden]
    grad_near[...] = grad[hidden:].astype(bf16)


def middle_kernel(*refs):
    grad_ref, piece, pre_out, prob_out, grad_out = refs[4:]
    pre_out[...], _, prob, grad = expert_math(*both_cores(*refs[:4]), [piece])
    hidden = grad.shape[0]
    prob_out[...] = jnp.broadcast_to(prob, prob_out.shape)
    grad_out[:hidden] = grad_ref[...]
    grad_out[hidden:] = grad.astype(bf16)


def late_kernel(*refs):
    dx_ref, pre_ref, prob_ref, near, far, keep, *gives, grad_far = refs[4:]
    d_pre, mixers, prob, grad = expert_math(*both_cores(*refs[:4]), [far])
    mixers = jnp.concatenate([near[: mixers.shape[0]], mixers])
    dx = dot(jnp.concatenate([pre_ref[...], d_pre], axis=1), mixers, (1, 0))
    prob = prob_ref[...] + prob
    width, slots = dx.shape[1], keep.shape[0]
    for side, value in ((slice(0, width), dx), (slice(width, None), prob)):
        total = value + dx_ref[:, side]
        keep[:, side] = total[:slots]
        for i, give in enumerate(reversed(gives)):
            rows = give.shape[0]
            give[:, side] = total[slots + rows * i : slots + rows * (i + 1)].astype(bf16)
    grad_far[...] = grad.astype(bf16)


def grad_kernel(own, near, far, out):
    hidden = own.shape[0]
    out[:hidden] = (own[...] + near[:hidden].astype(f32) + far[...].astype(f32)).astype(bf16)
    out[hidden:] = near[hidden:]


def finish_kernel(mine, theirs, tokens, probs, grad_out, tokens_out, probs_out, held, sems):
    hidden = mine.shape[0] // 2
    rep = lax.axis_index("rep")
    copies = [pltpu.make_async_copy(tokens, tokens_out, sems.at[0]), pltpu.make_async_copy(probs, probs_out, sems.at[1])]
    for copy in copies:
        copy.start()
    for i, half in enumerate((rep, 1 - rep)):
        here, there = slice(i * hidden, (i + 1) * hidden), slice((1 - i) * hidden, (2 - i) * hidden)
        rows = pl.ds(pl.multiple_of(half * hidden, hidden), hidden)
        held[i] = mine[here].astype(f32) + theirs[there].astype(f32)
        copies.append(pltpu.make_async_copy(held.at[i], grad_out.at[0, rows], sems.at[2 + i]))
        copies[-1].start()
    for copy in copies:
        copy.wait()


def add_kernel(start, rows, keep, got, *chunks):
    total = keep[start : start + got.shape[0]] + got[...].astype(f32)
    width = total.shape[1] - LANES
    for c, chunk in enumerate(chunks):
        value = total[c * rows : (c + 1) * rows]
        if chunk.shape[0] > rows:
            blocks = [value[:, i : i + FOLD] for i in range(0, width, FOLD)]
            diagonal = iota((rows, FOLD), 0) == iota((rows, FOLD), 1)
            prob = jnp.sum(jnp.where(diagonal, value[:, width : width + 1], 0.0), axis=0, keepdims=True)
            value = jnp.concatenate([*blocks, jnp.broadcast_to(prob, (8, FOLD))])
        chunk[...] = value.astype(bf16)


def combine_kernel(chunk_count, rows, *refs):
    chunks, (slot, route_weight, tokens_out, probs_out) = refs[:chunk_count], refs[chunk_count:]
    tok_dev, width = tokens_out.shape
    top = slot.shape[0]
    total = 0.0
    probs = [0.0] * top
    for c, place in enumerate(reversed(range(chunk_count))):
        slot_of_row = iota((rows, tok_dev), 0) + place * rows
        hits = [(slot_of_row == slot[k : k + 1, :]).astype(f32) for k in range(top)]
        value = chunks[c][...].astype(f32)
        if value.shape[0] > rows:
            blocks = [value[i : i + rows] for i in range(0, width // FOLD * rows, rows)]
            diagonal = iota((rows, FOLD), 0) == iota((rows, FOLD), 1)
            prob = value[width // FOLD * rows :][:1]
            prob = jnp.sum(jnp.where(diagonal, prob, 0.0), axis=1, keepdims=True)
            value = jnp.concatenate(blocks, axis=1)
        else:
            prob = value[:, width : width + 1]
        total = total + dot(sum(hits).astype(bf16), value[:, :width].astype(bf16), (0, 0))
        for k in range(top):
            probs[k] = probs[k] + jnp.sum(hits[k] * prob, axis=0, keepdims=True)
    tokens_out[...] = total.astype(bf16)
    for k in range(top):
        probs_out[k : k + 1, :] = (probs[k] / route_weight[k : k + 1, :].astype(f32)).astype(bf16)


def local(tokens, upstream, expert_ids, route_weight, gate_weight, up_weight, down_weight):
    tok_dev, width = tokens.shape
    top = expert_ids.shape[1]
    experts, reps = lax.axis_size("ep"), lax.axis_size("rep")
    cap = 2 * ((5 * tok_dev * top + 8 * experts - 1) // (8 * experts))
    slots = experts * cap
    chunk_count = experts if experts <= 8 else 1
    rows = slots // chunk_count
    hidden = gate_weight.shape[1] // reps
    shape = jax.ShapeDtypeStruct
    in_hbm = pl.BlockSpec(memory_space=pltpu.HBM)

    given = [expert_ids.T, route_weight.T, tokens, upstream]
    *chunks, slot, first, second = kernel_call(
        functools.partial(dispatch_kernel, experts, cap, chunk_count),
        [pltpu.with_memory_space_constraint(a, pltpu.HBM) for a in [*given, gate_weight, up_weight, down_weight]],
        [shape((2 * rows, width), bf16)] * chunk_count
        + [shape((top, tok_dev), jnp.int32)]
        + [shape((3 * hidden, width), bf16)] * 2,
        in_specs=[in_hbm] * 7,
        scratch_shapes=[
            *(pltpu.VMEM(a.shape, a.dtype) for a in given[:2]),
            pltpu.VMEM((2 * tok_dev, width), bf16),
            pltpu.SemaphoreType.DMA((10,)),
        ],
    )

    along, across = (1, 2), (2, 1)
    near = [swap_by_core(first, along), swap_by_core(second, along)]
    far = swap_by_core(near[0], across)

    if chunk_count > 1:
        chunks = exchange(chunks)
    else:
        moved = chunks[0].reshape(2, experts, cap, width)
        moved = lax.all_to_all(moved, "ep", split_axis=1, concat_axis=1, tiled=True)
        chunks = [moved.reshape(2 * rows, width)]
    order = [*range(chunk_count)][::-1]
    order = [*order[1:2], *order[:1], *order[2:]]
    own = kernel_call(functools.partial(gather_kernel, order), [chunks[c] for c in order], [shape((slots, width), bf16)] * 2, flops=2 * 10**9)
    other = [swap(part, "rep", 1) for part in own]

    wide = width + LANES
    dx, grad_own, grad_near = kernel_call(
        early_kernel,
        [*own, *other, first, near[0]],
        [shape((2 * slots, wide), f32), shape((hidden, width), f32), shape((hidden, width), bf16)],
        flops=10**9,
    )
    d_pre, prob, grad_near = kernel_call(
        middle_kernel,
        [*own, *other, grad_near, near[1]],
        [
            shape((2 * slots, 2 * hidden), bf16),
            shape((2 * slots, LANES), f32),
            shape((2 * hidden, width), bf16),
        ],
        flops=0,
    )
    parts = 2 if chunk_count % 2 == 0 else 1
    keep, *gives, grad_far = kernel_call(
        late_kernel,
        [*own, *other, dx, d_pre, prob, near[1], far],
        [shape((slots, wide), f32)]
        + [shape((slots // parts, wide), bf16)] * parts
        + [shape((hidden, width), bf16)],
    )
    folds = chunk_count > 1 and rows <= FOLD and width % FOLD == 0 and rows * width // FOLD % 8 == 0
    returned = shape((rows * width // FOLD + 8, FOLD) if folds else (rows, wide), bf16)
    back = []
    for i, give in enumerate(gives):
        sums = kernel_call(
            functools.partial(add_kernel, (parts - 1 - i) * slots // parts, rows),
            [keep, swap(give, "rep", 1)],
            [returned] * (chunk_count // parts),
        )
        back = [*sums, *back]
    if chunk_count > 1:
        back = exchange(back)
    else:
        moved = back[0].reshape(experts, cap, wide)
        moved = lax.all_to_all(moved, "ep", split_axis=0, concat_axis=0, tiled=True)
        back = [moved.reshape(rows, wide)]
    d_tokens, d_probs = kernel_call(
        functools.partial(combine_kernel, chunk_count, rows),
        back[::-1] + [slot, route_weight.T],
        [shape((tok_dev, width), bf16), shape((top, tok_dev), bf16)],
        flops=8 * 10**9,
    )

    arrived = swap_by_core(grad_near, along), swap_by_core(grad_far, (3, 3))
    (mine,) = kernel_call(grad_kernel, [grad_own, *arrived], [shape((2 * hidden, width), bf16)])
    results = [
        shape((1, 2 * hidden, width), f32),
        shape((tok_dev, width), bf16),
        shape((top, tok_dev), bf16),
    ]
    grad_total, d_tokens, d_probs = kernel_call(
        finish_kernel,
        [mine, swap(mine, "rep", 1), d_tokens, d_probs],
        results,
        out_specs=[in_hbm] * 3,
        scratch_shapes=[pltpu.VMEM((2, hidden, width), f32), pltpu.SemaphoreType.DMA((4,))],
    )
    return d_tokens, d_probs.T, grad_total


def solution(mesh):
    rows = P(("rep", "ep", "dp"), None)
    weights = P("ep", "dp", None)
    return jax.shard_map(
        local,
        mesh=mesh,
        in_specs=(rows,) * 4 + (weights,) * 3,
        out_specs=(rows, rows, weights),
        check_vma=False,
    )
```
